32 devices in a mesh: ctx: 16 (over z, y, core), wsh: 2 (over x).
Axes of the slice: x: 2, y: 2, z: 4, core: 2. Of those that a mesh axis runs over, the one named last changes fastest.
Arguments:
- tokens: bfloat16 [2, 2048, 768], P('wsh', 'ctx'), may hold values from -6 to 6
- doc_ids: int32 [2, 2048], P('wsh', 'ctx'), may hold values from 0 to 7, never falling along the last dimension, each value on 1 to 512 neighbouring positions
- w_qkv: bfloat16 [768, 2304], P('wsh'), may hold values from -0.21875 to 0.21875
- b_query: bfloat16 [768], P('wsh'), may hold values from -3 to 3
- b_value: bfloat16 [768], P('wsh'), may hold values from -3 to 3
- w_out: bfloat16 [768, 768], P('wsh'), may hold values from -0.875 to 0.875
- b_out: bfloat16 [768], P('wsh'), may hold values from -2 to 2
- ln1_gain: bfloat16 [768], P('wsh'), may hold values from 0.5 to 1.5
- ln1_bias: bfloat16 [768], P('wsh'), may hold values from -2 to 2
- w_in: bfloat16 [768, 3072], P('wsh'), may hold values from -0.21875 to 0.21875
- b_in: bfloat16 [3072], P('wsh'), may hold values from -3 to 3
- w_back: bfloat16 [3072, 768], P('wsh'), may hold values from -0.109375 to 0.109375
- b_back: bfloat16 [768], P('wsh'), may hold values from -2 to 2
- ln2_gain: bfloat16 [768], P('wsh'), may hold values from 0.5 to 1.5
- ln2_bias: bfloat16 [768], P('wsh'), may hold values from -2 to 2
- d_out: bfloat16 [2, 2048, 768], P('wsh', 'ctx'), may hold values from -6 to 6
Outputs:
- output: bfloat16 [2, 2048, 768], P('wsh', 'ctx')
- d_tokens: float32 [2, 2048, 768], P('wsh', 'ctx')
- d_w_qkv: float32 [768, 2304], P('wsh')
- d_b_query: float32 [768], P('wsh')
- d_b_value: float32 [768], P('wsh')
- d_w_out: float32 [768, 768], P('wsh')
- d_b_out: float32 [768], P('wsh')
- d_ln1_gain: float32 [768], P('wsh')
- d_ln1_bias: float32 [768], P('wsh')
- d_w_in: float32 [768, 3072], P('wsh')
- d_b_in: float32 [3072], P('wsh')
- d_w_back: float32 [3072, 768], P('wsh')
- d_b_back: float32 [768], P('wsh')
- d_ln2_gain: float32 [768], P('wsh')
- d_ln2_bias: float32 [768], P('wsh')
The draws below stay inside these ranges and needn't reach their ends.
Inputs may be any that keep to these rules, and one draw needn't show every extreme that they name: `doc_ids`: along each sequence the ids never fall; each document has 1 to 512 tokens and one has exactly 512.
All inputs are finite; a program needn't handle non-finite values.
Results may differ from the reference program's by a relative error of at most 0.019.
Values may be sent and summed in bfloat16 or wider, within the bound.
A program may use at most 192 MiB of HBM per device.

```python
import math
import jax
import jax.numpy as jnp
import numpy as np
from jax import lax

D = 768
HEADS = 12
HEAD_DIM = 64
FF = 3072
DOC_MAX = 512
SEQ = 2048
SEQS = 2
DOCS = 8


def block_scale(own_key, extent, cuts, least, largest):
    def one(position, parts):
        steps = jax.random.uniform(jax.random.fold_in(jax.random.fold_in(own_key, 6), position), (parts,), jnp.float32, least / len(cuts), largest / len(cuts))
        return jnp.repeat(jnp.exp(steps), extent[position] // parts).reshape((-1,) + (1,) * (len(extent) - position - 1))

    loudness = one(*cuts[0])
    for cut in cuts[1:]:
        loudness = loudness * one(*cut)
    return loudness


def profile(amount, total, limit, skew):
    portions = [(1 << 20) // math.isqrt(rank ** skew) + 1 for rank in range(2, amount + 1)]
    rest, counts = total - limit - (amount - 1), [1] * (amount - 1)
    while rest > 0:
        free = [i for i in range(amount - 1) if counts[i] < limit]
        pool, left = sum([portions[i] for i in free]), rest
        for i in free:
            more = min(limit - counts[i], max(1, left * portions[i] // pool), rest)
            counts[i] = counts[i] + more
            rest = rest - more
    return np.array([limit] + counts)


def ragged_sizes(key, count, total, bound, lean):
    if count == 2:
        one = jax.random.randint(key, (), max(1, total - bound), min(bound, total - 1) + 1)
        return jnp.stack([one, total - one])
    lengths = jnp.asarray(profile(count, total, bound, lean), jnp.int32)
    pairs = (count - 1) // 2
    donor, sink = lengths[1:1 + 2 * pairs:2], lengths[2:2 + 2 * pairs:2]
    slack = jnp.minimum(donor - 1, bound - sink)
    passed = jax.random.randint(jax.random.fold_in(key, 1), (pairs,), 0, 1 << 20) % (slack + 1)
    lengths = lengths.at[1:1 + 2 * pairs:2].set(donor - passed).at[2:2 + 2 * pairs:2].set(sink + passed)
    return lengths[jax.random.permutation(jax.random.fold_in(key, 2), count)]


def bell_draw(stream_key, shape, scale, most, shards=(), kind=jnp.bfloat16):
    values = scale * jax.random.normal(stream_key, shape, jnp.float32)
    if shards:
        values = values * block_scale(stream_key, shape, shards, -0.22, 0.18)
    return jnp.clip(values, -most, most).astype(kind)


def setup_inputs(seed: int = 0) -> dict:
    splits = jax.random.split(jax.random.key(seed), 17)
    return {
        "tokens": bell_draw(splits[0], (SEQS, SEQ, D), 1.0, 6.0, ((0, 2), (1, 16))),
        "doc_ids": jax.vmap(lambda own: jnp.searchsorted(jnp.cumsum(ragged_sizes(own, DOCS, SEQ, DOC_MAX, 2)), jnp.arange(SEQ), side="right"))(jax.random.split(splits[1], SEQS)).reshape((SEQS, SEQ)).astype(jnp.int32),
        "w_qkv": bell_draw(splits[2], (D, 3 * D), D ** -0.5, 0.21875, ((0, 2),)),
        "b_query": bell_draw(splits[3], (D,), 0.5, 3.0, ((0, 2),)),
        "b_value": bell_draw(splits[4], (D,), 0.5, 3.0, ((0, 2),)),
        "w_out": bell_draw(splits[5], (D, D), (D // 16) ** -0.5, 0.875, ((0, 2),)),
        "b_out": bell_draw(splits[6], (D,), 0.3, 2.0, ((0, 2),)),
        "ln1_gain": jnp.clip(1.0 + 0.1 * jax.random.normal(splits[7], (D,), jnp.float32), 0.5, 1.5).astype(jnp.bfloat16),
        "ln1_bias": bell_draw(splits[8], (D,), 0.3, 2.0, ((0, 2),)),
        "w_in": bell_draw(splits[9], (D, FF), D ** -0.5, 0.21875, ((0, 2),)),
        "b_in": bell_draw(splits[10], (FF,), 0.5, 3.0, ((0, 2),)),
        "w_back": bell_draw(splits[11], (FF, D), FF ** -0.5, 0.109375, ((0, 2),)),
        "b_back": bell_draw(splits[12], (D,), 0.3, 2.0, ((0, 2),)),
        "ln2_gain": jnp.clip(1.0 + 0.1 * jax.random.normal(splits[13], (D,), jnp.float32), 0.5, 1.5).astype(jnp.bfloat16),
        "ln2_bias": bell_draw(splits[14], (D,), 0.3, 2.0, ((0, 2),)),
        "d_out": bell_draw(splits[15], (SEQS, SEQ, D), 1.0, 6.0, ((0, 2), (1, 16))),
    }


EPSILON = 1e-05
NEGATIVE = -1e+30
HIGHEST = lax.Precision.HIGHEST

@jax.custom_vjp
def low(v):
    return lax.optimization_barrier(v.astype(jnp.bfloat16)).astype(jnp.float32)

@jax.custom_vjp
def low_back(v):
    return v

def low_keep(v):
    return (low(v), None)

def low_pass(kept, grad):
    return (grad,)

def back_keep(v):
    return (v, None)

def back_low(kept, grad):
    return (low(grad),)
low.defvjp(low_keep, low_pass)
low_back.defvjp(back_keep, back_low)

def layer_norm(hidden, gain, offset):
    center = hidden - lax.optimization_barrier(jnp.mean(hidden, -1, keepdims=True))
    normed = center * lax.rsqrt(lax.optimization_barrier(jnp.mean(center * center, -1, keepdims=True)) + EPSILON)
    return normed * gain + offset

def gelu_exact(values):
    return 0.5 * values * (1.0 + lax.erf(values * 0.7071067811865476))

def attend_sequence(queries, keys, values, doc_row):
    length = queries.shape[0]
    q_block = min(512, length)
    window = min(length, q_block + 2 * DOC_MAX)
    att_scale = HEAD_DIM ** (-0.5)

    def one_block(index):
        start = (index * q_block).astype(jnp.int32)
        k_start = jnp.clip(start - DOC_MAX, 0, length - window).astype(jnp.int32)
        q_part = lax.dynamic_slice_in_dim(queries, start, q_block, 0)
        k_part = lax.dynamic_slice_in_dim(keys, k_start, window, 0)
        v_part = lax.dynamic_slice_in_dim(values, k_start, window, 0)
        q_docs = lax.dynamic_slice_in_dim(doc_row, start, q_block, 0)
        k_docs = lax.dynamic_slice_in_dim(doc_row, k_start, window, 0)
        raw_dots = jnp.einsum('qhd,khd->hqk', q_part, k_part, precision=HIGHEST)
        score = low_back(raw_dots) * att_scale
        same_doc = (q_docs[:, None] == k_docs[None, :])[None]
        masked = jnp.where(same_doc, score, NEGATIVE)
        peak = lax.optimization_barrier(jnp.max(masked, -1, keepdims=True))
        summed = lax.optimization_barrier(jnp.sum(jnp.where(same_doc, jnp.exp(masked - peak), 0.0), -1, keepdims=True))
        log_total = peak + jnp.log(summed)
        probs = low(jnp.where(same_doc, jnp.exp(masked - log_total), 0.0))
        return jnp.einsum('hqk,khd->qhd', probs, v_part, precision=HIGHEST)
    blocks = lax.map(jax.checkpoint(one_block), jnp.arange(length // q_block, dtype=jnp.int32))
    return blocks.reshape(length, HEADS * HEAD_DIM)

def forward(tokens, w_qkv, b_query, b_value, w_out, b_out, ln1_gain, ln1_bias, w_in, b_in, w_back, b_back, ln2_gain, ln2_bias, doc_ids):
    bias_qkv = jnp.concatenate([b_query, jnp.zeros_like(b_query), b_value])
    head_shape = (-1, HEADS, HEAD_DIM)

    def one_sequence(pair):
        hidden, doc_row = pair
        packed = low(low_back(jnp.dot(hidden, w_qkv, precision=HIGHEST) + bias_qkv))
        queries, keys, values = jnp.split(packed, 3, axis=1)
        attended = low(low_back(attend_sequence(queries.reshape(head_shape), keys.reshape(head_shape), values.reshape(head_shape), doc_row)))
        first = hidden + low_back(jnp.dot(attended, w_out, precision=HIGHEST)) + b_out
        normed_one = layer_norm(first, ln1_gain, ln1_bias)
        inner = low_back(jnp.dot(low(normed_one), w_in, precision=HIGHEST)) + b_in
        second = normed_one + low_back(jnp.dot(low(gelu_exact(inner)), w_back, precision=HIGHEST)) + b_back
        return layer_norm(second, ln2_gain, ln2_bias)
    return lax.map(one_sequence, (tokens, doc_ids))

def reference(tokens, doc_ids, w_qkv, b_query, b_value, w_out, b_out, ln1_gain, ln1_bias, w_in, b_in, w_back, b_back, ln2_gain, ln2_bias, d_out):
    floats = [item.astype(jnp.float32) for item in (tokens, w_qkv, b_query, b_value, w_out, b_out, ln1_gain, ln1_bias, w_in, b_in, w_back, b_back, ln2_gain, ln2_bias)]

    def closed(*params):
        return forward(*params, doc_ids)
    result, pullback = jax.vjp(closed, *floats)
    grads = pullback(d_out.astype(jnp.float32))
    return (result.astype(jnp.bfloat16), grads[0], grads[1], grads[2], grads[3], grads[4], grads[5], grads[6], grads[7], grads[8], grads[9], grads[10], grads[11], grads[12], grads[13])
```

```python
import functools
import types

import jax
import jax.numpy as jnp
from jax import lax
from jax.experimental import pallas as pl
from jax.experimental.pallas import tpu as pltpu
from jax.sharding import PartitionSpec as P

HEAD_DIM = 64
GROUP = 4
GROUP_HEADS = 3
BLOCK = 128
PLANE = GROUP * BLOCK
MODEL = 768
FF = 3072
HALF = MODEL // 2
LANES = GROUP_HEADS * HEAD_DIM
TILES = 4
OWN_ROWS = (4 * 2 * BLOCK, 0)
BOTH = 2 * BLOCK
EPSILON = 1e-05
NEGATIVE = -1e30
ROOT_HALF = 0.7071067811865476
INV_ROOT_TAU = 0.3989422804014327
SCALE = HEAD_DIM**-0.5
MESH = pl.DeviceIdType.MESH
F32 = jnp.float32
BF16 = jnp.bfloat16
NT = (((1,), (1,)), ((), ()))
TN = (((0,), (0,)), ((), ()))


class Place:
    def __init__(self, planes):
        self.n = planes
        self.c = lax.axis_index("ctx")
        self.x = lax.axis_index("wsh")
        self.p = self.c // GROUP
        self.r = self.c % GROUP
        self.y = self.r // 2
        self.k = self.r % 2
        self.parity = self.p % 2
        self.sister = (self.c + 1 - 2 * self.k, self.x)
        self.beside = (self.c + 2 - 4 * self.y, self.x)
        self.across = (self.c, 1 - self.x)
        self.pair = (self.c + GROUP * (1 - 2 * self.parity), self.x)
        self.up = (self.c + GROUP, self.x)
        self.down = (self.c - GROUP, self.x)
        self.has_up = self.p < planes - 1
        self.has_down = self.p > 0

    def peer(self, d):
        if d == 1:
            return self.y * 2 + (1 - self.k)
        if d == 2:
            return (1 - self.y) * 2 + self.k
        return (1 - self.y) * 2 + (1 - self.k)

    def in_plane(self, position):
        return (self.p * GROUP + position, self.x)

    def plane(self, p):
        return (p * GROUP + self.r, self.x)


def signal(sem, device):
    pl.semaphore_signal(sem, inc=1, device_id=device, device_id_type=MESH)


def greet(at):
    barrier = pltpu.get_barrier_semaphore()
    for d in (1, 2, 3):
        signal(barrier, at.in_plane(at.peer(d)))
    signal(barrier, at.across)

    def other_plane(d, carry):
        signal(barrier, at.plane((at.p + d) % at.n))
        return carry

    lax.fori_loop(1, at.n, other_plane, 0)
    pl.semaphore_wait(barrier, 4 + at.n - 1)


def remote(src, dst, sems, index, device, recv_index=None):
    send, recv = sems
    return pltpu.make_async_remote_copy(
        src_ref=src,
        dst_ref=dst,
        send_sem=send.at[index],
        recv_sem=recv.at[index if recv_index is None else recv_index],
        device_id=device,
        device_id_type=MESH,
    )


def lane_head(shape, first):
    return lax.broadcasted_iota(jnp.int32, shape, 1) // HEAD_DIM - first


def column_of(row):
    return jnp.broadcast_to(row, (BLOCK, BLOCK)).T


def chunk_of(rows, planes):
    chunk = -(-(-(-rows // planes)) // 16) * 16
    while rows % chunk:
        chunk += 16
    return chunk


SET_ROWS = (HALF, 512, HALF)
SET_WIDTH = (MODEL, MODEL, 640)
QUARTER = HALF // GROUP


def scratch_plan(planes):
    steps = planes.bit_length() - 1
    buffers = dict(
        wq=((MODEL, 3 * MODEL), BF16),
        wo=((MODEL, MODEL), BF16),
        wi=((MODEL, FF), BF16),
        wb=((FF, MODEL), BF16),
        bias_own=((16, HALF), BF16),
        bias2=((2, 16, HALF), BF16),
        dout_far=((BLOCK, MODEL), BF16),
        ids=((3, GROUP, 8, BLOCK), F32),
        acc=((BLOCK, 3 * MODEL), F32),
        qsend=((GROUP, BLOCK, 256), BF16),
        kvsend=((GROUP, BLOCK, 2 * LANES), BF16),
        qp=((PLANE, 256), BF16),
        kv=((3 * PLANE, 2 * LANES), BF16),
        og=((PLANE, 256), F32),
        lse=((PLANE, BLOCK), F32),
        asend=((GROUP, BLOCK, 256), BF16),
        arecv=((GROUP, BLOCK, 256), BF16),
        tok_plane=((PLANE, MODEL), BF16),
        tok2=((BOTH, MODEL), BF16),
        att2=((BOTH, MODEL), BF16),
        unit_one=((BOTH, MODEL), F32),
        norm_low=((BOTH, MODEL), BF16),
        act=((BOTH, FF), BF16),
        d_inner=((BOTH, FF), BF16),
        d_second=((BOTH, MODEL), BF16),
        d_first=((BOTH, MODEL), BF16),
        second=((BOTH, MODEL), F32),
        slope=((4 * BOTH + HALF, MODEL), F32),
        out_tile=((HALF, MODEL), F32),
        dsend=((GROUP, BLOCK, 256), BF16),
        do=((PLANE, 256), BF16),
        grads=((3 * PLANE, 2 * LANES), F32),
        dq=((PLANE, 256), F32),
        k_ids=((3 * PLANE, BLOCK), F32),
        stats=((2 * GROUP_HEADS, 8, PLANE), F32),
        halo_send=((2, PLANE, 2 * LANES), BF16),
        halo=((2, PLANE, 2 * LANES), BF16),
        d_group=((PLANE, 640), BF16),
        d_recv=((GROUP, BLOCK, 640), BF16),
        d_packed=((BLOCK, 3 * MODEL), BF16),
        q_sum=((HALF, 640), F32),
        x_send=((HALF, 640), BF16),
        x_recv=((HALF, 640), BF16),
        small_recv=((2 + steps, 24, MODEL), F32),
        line_send=((8, 640), F32),
        line_recv=((8, 640), F32),
    )
    for g, (rows, width) in enumerate(zip(SET_ROWS, SET_WIDTH)):
        chunk = chunk_of(rows, planes)
        if g < 2:
            buffers[f"core_send{g}"] = ((2, rows, width), BF16)
            buffers[f"core_recv{g}"] = ((2, rows, width), BF16)
            buffers[f"y_send{g}"] = ((rows, width), BF16)
            buffers[f"y_recv{g}"] = ((rows, width), BF16)
        buffers[f"z_send{g}"] = ((rows, width), BF16)
        buffers[f"z_recv{g}"] = ((planes, chunk, width), BF16)
        buffers[f"final{g}"] = ((chunk, width), BF16)
    semaphores = dict(
        local=(4 + 3,),
        wx=(4, 2),
        wy=(4, 2),
        wz=(4, 2),
        wc=(4, 5),
        ex=(5,),
        tp=(4,),
        a2a=(6, 4),
        halo_f=(2, 5),
        halo_b=(2,),
        core=(4,),
        xs=(planes,),
        ys=(2, planes),
        zs=(3, planes),
        gu=(3, planes),
        gd=(3, planes),
        gy=(3, planes),
        gc=(3, planes),
        gf=(3, planes),
        sm=(2 + steps,),
    )
    return buffers, semaphores


ARGS = ["tokens", "doc_ids", "w_qkv", "b_query", "b_value", "w_out", "b_out", "ln1_gain"]
ARGS += ["ln1_bias", "w_in", "b_in", "w_back", "b_back", "ln2_gain", "ln2_bias", "d_out"]
RESULTS = ["result", "d_tokens", "sums0", "sums1", "sums2", "small"]


def layer_kernel(planes, names, sem_names, *refs):
    split = len(ARGS) + len(RESULTS) + len(names)
    b = types.SimpleNamespace(**dict(zip(ARGS + RESULTS + names, refs[:split])))
    pairs = refs[split:]
    s = types.SimpleNamespace(
        **{n: (pairs[2 * i], pairs[2 * i + 1]) for i, n in enumerate(sem_names)}
    )
    at = Place(planes)
    sent = []

    def start(copy):
        copy.start()
        sent.append(copy)

    def block_rows(first, i):
        return pl.ds(pl.multiple_of(first + i * BLOCK, BLOCK), BLOCK)

    b.ids[1, at.r] = jnp.broadcast_to(b.doc_ids[...].astype(F32), (8, BLOCK))

    @pl.when(jnp.logical_not(at.has_down))
    def _():
        b.kv[pl.ds(0, PLANE), :] = jnp.zeros((PLANE, 2 * LANES), BF16)
        b.ids[0] = jnp.full((GROUP, 8, BLOCK), -1.0, F32)

    @pl.when(jnp.logical_not(at.has_up))
    def _():
        b.kv[pl.ds(2 * PLANE, PLANE), :] = jnp.zeros((PLANE, 2 * LANES), BF16)
        b.ids[2] = jnp.full((GROUP, 8, BLOCK), -1.0, F32)

    vectors = [b.b_query, b.b_value, b.b_out, b.ln1_gain, b.ln1_bias]
    lines = [v[...].astype(F32).reshape(1, HALF) for v in vectors]
    lines += [
        b.b_in[pl.ds(i * HALF, HALF)].astype(F32).reshape(1, HALF) for i in range(4)
    ]
    lines += [
        v[...].astype(F32).reshape(1, HALF) for v in (b.b_back, b.ln2_gain, b.ln2_bias)
    ]
    lines.append(jnp.zeros((4, HALF), F32))
    packed_bias = jnp.concatenate(lines, axis=0).astype(BF16)
    b.bias_own[...] = packed_bias
    b.bias2[at.x] = packed_bias
    greet(at)

    shards = (b.w_qkv, b.w_out, b.w_in, b.w_back)
    wholes = (b.wq, b.wo, b.wi, b.wb)
    direct = (True, True, False, False)
    own_q = at.y * 2 + at.parity
    diag_q = (1 - at.y) * 2 + (1 - at.parity)
    beside_q = (1 - at.y) * 2 + at.parity
    pair_q = at.y * 2 + (1 - at.parity)

    def rows(w, quarter, core):
        eighth = shards[w].shape[0] // 8
        return pl.multiple_of((quarter * 2 + core) * eighth, 16), eighth

    def far(w, quarter, core, part=None):
        first, size = rows(w, quarter, core)
        base = (1 - at.x) * shards[w].shape[0]
        lines = pl.ds(pl.multiple_of(base + first, 16), size)
        if part is None:
            return wholes[w].at[lines]
        width = shards[w].shape[1] // 2
        return wholes[w].at[lines, pl.ds(part * width, width)]

    def across_copy(w, i):
        first, size = rows(w, (own_q, diag_q)[i], at.k)
        base = at.x * shards[w].shape[0]
        return remote(
            shards[w].at[pl.ds(first, size)],
            wholes[w].at[pl.ds(pl.multiple_of(base + first, 16), size)],
            s.wx,
            (w, i),
            at.across,
        )

    def piece_copy(w, quarter, sems, index, device, part=None, core=None):
        piece = far(w, quarter, at.k if core is None else core, part)
        return remote(piece, piece, sems, (w, index), device)

    def relay_own(w):
        piece_copy(w, own_q, s.wx, 0, at.across).wait_recv()
        start(piece_copy(w, own_q, s.wy, 0, at.beside))
        start(piece_copy(w, own_q, s.wz, 0, at.pair))
        start(piece_copy(w, own_q, s.wc, 0, at.sister))

    def relay_rest(w):
        if direct[w]:
            piece_copy(w, diag_q, s.wx, 1, at.across).wait_recv()
            start(piece_copy(w, diag_q, s.wc, 1, at.sister))
        piece_copy(w, beside_q, s.wy, 0, at.beside).wait_recv()
        if not direct[w]:
            start(piece_copy(w, beside_q, s.wz, 1, at.pair, part=1))
        start(piece_copy(w, beside_q, s.wc, 2, at.sister))
        piece_copy(w, pair_q, s.wz, 0, at.pair).wait_recv()
        if not direct[w]:
            start(piece_copy(w, pair_q, s.wy, 1, at.beside, part=0))
        start(piece_copy(w, pair_q, s.wc, 3, at.sister))

    def relay_diagonal(w):
        piece_copy(w, diag_q, s.wy, 1, at.beside, part=0).wait_recv()
        start(piece_copy(w, diag_q, s.wc, 1, at.sister, part=0))
        piece_copy(w, diag_q, s.wz, 1, at.pair, part=1).wait_recv()
        start(piece_copy(w, diag_q, s.wc, 4, at.sister, part=1))

    def sister_arrivals(w):
        other = 1 - at.k
        piece_copy(w, own_q, s.wc, 0, at.sister, core=other).wait_recv()
        piece_copy(w, beside_q, s.wc, 2, at.sister, core=other).wait_recv()
        piece_copy(w, pair_q, s.wc, 3, at.sister, core=other).wait_recv()
        if direct[w]:
            piece_copy(w, diag_q, s.wc, 1, at.sister, core=other).wait_recv()
        else:
            piece_copy(w, diag_q, s.wc, 1, at.sister, part=0, core=other).wait_recv()
            piece_copy(w, diag_q, s.wc, 4, at.sister, part=1, core=other).wait_recv()

    near_tokens = pl.ds(0, BLOCK)
    far_tokens = pl.ds(BLOCK, BLOCK)
    bias_copy = remote(b.bias_own, b.bias2.at[at.x], s.ex, 0, at.across)
    tok_copy = remote(b.tokens.at[0], b.tok2.at[far_tokens], s.ex, 1, at.across)
    dout_copy = remote(b.d_out.at[0], b.dout_far, s.ex, 2, at.across)
    for i in range(2):
        start(across_copy(0, i))
    start(bias_copy)
    for d in (1, 2, 3):
        mine = b.ids.at[1, at.r]
        start(remote(mine, mine, s.a2a, (0, d), at.in_plane(at.peer(d))))
    own_copies = []
    for w in range(4):
        size = shards[w].shape[0]
        own_copies.append(
            pltpu.make_async_copy(
                shards[w],
                wholes[w].at[pl.ds(pl.multiple_of(at.x * size, 16), size)],
                s.local[0].at[w],
            )
        )
    own_copies[0].start()

    near_rows = pl.multiple_of(at.x * HALF, HALF)
    far_rows = pl.multiple_of((1 - at.x) * HALF, HALF)
    b.tok2[near_tokens, :] = b.tokens[0]
    b.tok_plane[block_rows(0, at.r), :] = b.tokens[0]
    own_copies[0].wait()
    near = b.tokens[0, :, pl.ds(near_rows, HALF)]
    for j in range(3):
        cols = slice(j * MODEL, (j + 1) * MODEL)
        b.acc[:, cols] = jnp.dot(
            near, b.wq[pl.ds(near_rows, HALF), cols], preferred_element_type=F32
        )
    for w in (1, 2, 3):
        own_copies[w].start()
    relay_own(0)
    relay_rest(0)
    for i in range(2):
        start(across_copy(1, i))
    start(across_copy(2, 0))
    remote(b.bias_own, b.bias2.at[1 - at.x], s.ex, 0, at.across).wait_recv()
    halves = (b.bias2[0].astype(F32), b.bias2[1].astype(F32))
    bias = jnp.concatenate(halves, axis=1)
    sister_arrivals(0)
    apart = b.tokens[0, :, pl.ds(far_rows, HALF)]
    for j in range(3):
        cols = slice(j * MODEL, (j + 1) * MODEL)
        part = b.acc[:, cols] + jnp.dot(
            apart, b.wq[pl.ds(far_rows, HALF), cols], preferred_element_type=F32
        )
        if j == 0:
            part = part + bias[0:1]
        if j == 2:
            part = part + bias[1:2]
        b.acc[:, cols] = part

    zero_lanes = jnp.zeros((BLOCK, HEAD_DIM), F32)
    for g in range(GROUP):
        cols = [
            b.acc[:, j * MODEL + g * LANES : j * MODEL + (g + 1) * LANES] for j in range(3)
        ]
        b.qsend[g] = jnp.concatenate([cols[0], zero_lanes], axis=1).astype(BF16)
        b.kvsend[g] = jnp.concatenate([cols[1], cols[2]], axis=1).astype(BF16)

    for d in (1, 2, 3):
        g = at.peer(d)
        start(
            remote(
                b.kvsend.at[g],
                b.kv.at[block_rows(PLANE, at.r)],
                s.a2a,
                (1, d),
                at.in_plane(g),
            )
        )
    for d in (1, 2, 3):
        g = at.peer(d)
        start(
            remote(
                b.qsend.at[g], b.qp.at[block_rows(0, at.r)], s.a2a, (2, d), at.in_plane(g)
            )
        )
    b.kv[block_rows(PLANE, at.r), :] = b.kvsend[at.r]
    b.qp[block_rows(0, at.r), :] = b.qsend[at.r]

    def both_ways(up, down, act):
        @pl.when(at.has_up)
        def _():
            act(up)

        @pl.when(at.has_down)
        def _():
            act(down)

    def go(copy):
        copy.start()

    def block_of(d):
        return at.r if d == 0 else at.peer(d)

    def up_kv(d):
        i = block_of(d)
        return remote(
            b.kv.at[block_rows(PLANE, i)], b.kv.at[block_rows(0, i)], s.halo_f, (0, d), at.up
        )

    def down_kv(d):
        i = block_of(d)
        return remote(
            b.kv.at[block_rows(PLANE, i)],
            b.kv.at[block_rows(2 * PLANE, i)],
            s.halo_f,
            (1, d),
            at.down,
        )

    up_ids = remote(b.ids.at[1], b.ids.at[0], s.halo_f, (0, 4), at.up)
    down_ids = remote(b.ids.at[1], b.ids.at[2], s.halo_f, (1, 4), at.down)

    def from_peer(piece, kind, d):
        remote(piece, piece, s.a2a, (kind, d), at.in_plane(at.peer(d))).wait_recv()

    both_ways(up_kv(0), down_kv(0), go)
    for d in (1, 2, 3):
        from_peer(b.ids.at[1, at.peer(d)], 0, d)
    both_ways(up_ids, down_ids, go)
    relay_own(1)
    for d in (1, 2, 3):
        from_peer(b.kv.at[block_rows(PLANE, at.peer(d))], 1, d)
        both_ways(up_kv(d), down_kv(d), go)
    relay_rest(1)
    relay_own(2)
    start(across_copy(3, 0))
    start(tok_copy)
    for d in (1, 2, 3):
        from_peer(b.qp.at[block_rows(0, at.peer(d))], 2, d)
    relay_rest(2)

    @pl.when(at.has_down)
    def _():
        for d in range(4):
            piece = b.kv.at[block_rows(0, block_of(d))]
            remote(piece, piece, s.halo_f, (0, d), at.down).wait_recv()
        remote(b.ids.at[0], b.ids.at[0], s.halo_f, (0, 4), at.down).wait_recv()

    @pl.when(at.has_up)
    def _():
        for d in range(4):
            piece = b.kv.at[block_rows(2 * PLANE, block_of(d))]
            remote(piece, piece, s.halo_f, (1, d), at.up).wait_recv()
        remote(b.ids.at[2], b.ids.at[2], s.halo_f, (1, 4), at.up).wait_recv()

    def attend(t, carry):
        q_rows = block_rows(0, t)
        q_ids = column_of(b.ids[1, t][0:1, :])[:, 0:1]
        k_ids = jnp.concatenate(
            [b.ids[i, j][0:1, :] for i in range(3) for j in range(GROUP)], axis=1
        )
        same = q_ids == k_ids
        total = jnp.zeros((BLOCK, 256), F32)
        logs = jnp.zeros((BLOCK, BLOCK), F32)
        for h in range(GROUP_HEADS):
            q = b.qp[q_rows, :] * SCALE
            q = jnp.where(lane_head((BLOCK, 256), 0) == h, q, jnp.zeros_like(q))
            score = lax.dot_general(q, b.kv[:, 0:256], NT, preferred_element_type=F32)
            score = jnp.where(same, score, NEGATIVE)
            peak = jnp.max(score, axis=1, keepdims=True)
            weight = jnp.exp(score - peak)
            summed = jnp.sum(weight, axis=1, keepdims=True)
            out = jnp.dot(weight.astype(BF16), b.kv[:, 128:384], preferred_element_type=F32)
            out = out / summed
            total = jnp.where(lane_head((BLOCK, 256), 1) == h, out, total)
            lane = lax.broadcasted_iota(jnp.int32, (BLOCK, BLOCK), 1)
            logs = jnp.where(lane == h, peak + jnp.log(summed), logs)
        b.og[q_rows, :] = total
        b.lse[q_rows, :] = logs
        b.asend[t] = total.astype(BF16)
        return carry

    lax.fori_loop(0, GROUP, attend, 0)

    for d in (1, 2, 3):
        i = at.peer(d)
        start(remote(b.asend.at[i], b.arecv.at[at.r], s.a2a, (3, d), at.in_plane(i)))
    b.arecv[at.r] = b.asend[at.r]
    relay_own(3)
    for d in (1, 2, 3):
        from_peer(b.arecv.at[at.peer(d)], 3, d)
    b.att2[near_tokens, :] = jnp.concatenate(
        [b.arecv[g].astype(F32)[:, HEAD_DIM : HEAD_DIM + LANES] for g in range(GROUP)], axis=1
    ).astype(BF16)
    att_copy = remote(b.att2.at[near_tokens], b.att2.at[far_tokens], s.ex, 3, at.across)
    start(att_copy)
    start(dout_copy)
    relay_rest(3)
    relay_diagonal(2)
    own_copies[1].wait()
    sister_arrivals(1)
    tok_copy.wait_recv()
    att_copy.wait_recv()

    def normalise(hidden):
        center = hidden - jnp.mean(hidden, -1, keepdims=True)
        inverse = lax.rsqrt(jnp.mean(center * center, -1, keepdims=True) + EPSILON)
        return center * inverse, inverse

    def norm_back(upstream, unit, inverse, gain):
        scaled = upstream * gain
        return inverse * (
            scaled
            - jnp.mean(scaled, -1, keepdims=True)
            - unit * jnp.mean(scaled * unit, -1, keepdims=True)
        )

    def column_sum(value):
        return jnp.sum(value, axis=0, keepdims=True)

    def tok_block(i, sem, device):
        piece = b.tok_plane.at[block_rows(0, i)]
        return remote(piece, piece, s.tp, sem, device)

    start(tok_block(at.r, 0, at.beside))
    start(tok_block(at.r, 1, at.sister))
    first = (
        b.tok2[...].astype(F32)
        + jnp.dot(b.att2[...], b.wo[...], preferred_element_type=F32)
        + bias[2:3]
    )
    unit_one, inverse_one = normalise(first)
    b.unit_one[...] = unit_one
    normed = unit_one * bias[3:4] + bias[4:5]
    b.norm_low[...] = normed.astype(BF16)
    b.second[...] = normed + bias[9:10]
    relay_diagonal(3)
    for w in (2, 3):
        own_copies[w].wait()
        sister_arrivals(w)
    for c in range(4):
        cols = slice(c * MODEL, (c + 1) * MODEL)
        part = halves[c // 2]
        i = 5 + 2 * (c % 2)
        line = jnp.concatenate([part[i : i + 1], part[i + 1 : i + 2]], axis=1)
        inner = jnp.dot(b.norm_low[...], b.wi[:, cols], preferred_element_type=F32) + line
        gate = 0.5 * (1.0 + lax.erf(inner * ROOT_HALF))
        activation = (inner * gate).astype(BF16)
        b.act[:, cols] = activation
        b.slope[c * BOTH : (c + 1) * BOTH, :] = (
            gate + inner * jnp.exp(-0.5 * inner * inner) * INV_ROOT_TAU
        )
        b.second[...] += jnp.dot(activation, b.wb[cols, :], preferred_element_type=F32)
    unit_two, inverse_two = normalise(b.second[...])
    b.result[...] = (unit_two[:BLOCK] * bias[10:11] + bias[11:12]).astype(BF16)
    dout_copy.wait_recv()
    upstream = jnp.concatenate([b.d_out[0], b.dout_far[...]], axis=0).astype(F32)
    b.small[...] = jnp.zeros_like(b.small)
    b.small[10:11, :] = column_sum(upstream * unit_two)
    b.small[11:12, :] = column_sum(upstream)
    d_second = norm_back(upstream, unit_two, inverse_two, bias[10:11])
    b.small[9:10, :] = column_sum(d_second)
    b.d_second[...] = d_second.astype(BF16)
    b.second[...] = d_second

    chunks = [chunk_of(rows, planes) for rows in SET_ROWS]
    owners = [rows // chunk for rows, chunk in zip(SET_ROWS, chunks)]

    def of(name, group):
        return getattr(b, f"{name}{group}")

    def tile(group, t):
        if group == 0:
            lanes = pl.multiple_of(at.x * (TILES * HALF) + t * HALF, 128)
            left, right = b.act[:, pl.ds(lanes, HALF)], b.d_second[...]
        else:
            left = b.norm_low[:, pl.ds(near_rows, HALF)]
            right = b.d_inner[:, pl.ds(pl.multiple_of(t * MODEL, 128), MODEL)]
        return lax.dot_general(left, right, TN, preferred_element_type=F32)

    def out_quarter(t):
        return b.out_tile[pl.ds(pl.multiple_of(t * QUARTER, 16), QUARTER), :]

    def chunk_rows(group, j):
        return pl.ds(pl.multiple_of(j * chunks[group], 16), chunks[group])

    def own_chunk(group, j):
        if group == 2:
            return b.q_sum.at[chunk_rows(2, j)]
        first_row = OWN_ROWS[group] + j * chunks[group]
        return b.slope.at[pl.ds(pl.multiple_of(first_row, 16), chunks[group])]

    def core_copy(group, i):
        return remote(
            of("core_send", group).at[i],
            of("core_recv", group).at[i],
            s.core,
            group * 2 + i,
            at.sister,
        )

    def y_copy(group, j):
        lines = chunk_rows(group, j)
        return remote(
            of("y_send", group).at[lines],
            of("y_recv", group).at[lines],
            s.ys,
            (group, j),
            at.beside,
        )

    def z_copy(group, j):
        return remote(
            of("z_send", group).at[chunk_rows(group, j)],
            of("z_recv", group).at[at.p],
            s.zs,
            (group, j),
            at.plane(j),
            (group, at.p),
        )

    def each_owner(group, act, first=1):
        def one(d, carry):
            j = (at.p + d) % planes

            @pl.when(j < owners[group])
            def _():
                act(j)

            return carry

        lax.fori_loop(first, first + planes, one, 0)

    def produce(group):
        base = OWN_ROWS[group]
        for i, t in enumerate((at.peer(3), at.peer(1))):
            of("core_send", group)[i, 0:HALF, :] = tile(group, t).astype(BF16)
            if group == 1:
                of("core_send", group)[i, HALF : HALF + QUARTER, :] = out_quarter(t).astype(BF16)
            start(core_copy(group, i))
        passing = tile(group, at.peer(2))
        b.slope[base : base + HALF, :] = tile(group, at.r)
        if group == 1:
            b.slope[base + HALF : base + HALF + QUARTER, :] = out_quarter(at.r)
        core_copy(group, 0).wait_recv()
        come = of("core_recv", group)
        of("y_send", group)[0:HALF, :] = (passing + come[0, 0:HALF, :].astype(F32)).astype(BF16)
        if group == 1:
            lines = slice(HALF, HALF + QUARTER)
            b.y_send1[HALF + QUARTER :, :] = jnp.zeros((BLOCK - QUARTER, MODEL), BF16)
            of("y_send", group)[lines, :] = (
                out_quarter(at.peer(2)) + come[0, lines, :].astype(F32)
            ).astype(BF16)
        each_owner(group, lambda j: y_copy(group, j).start())
        core_copy(group, 1).wait_recv()
        used = SET_ROWS[0] if group == 0 else HALF + QUARTER
        b.slope[base : base + used, :] += come[1, 0:used, :].astype(F32)

    def scatter(group):
        def act(j):
            mine = own_chunk(group, j)
            if group == 2:
                x_copy(j).wait_recv()
                came = b.x_recv[chunk_rows(2, j), :]
            else:
                y_copy(group, j).wait_recv()
                came = of("y_recv", group)[chunk_rows(group, j), :]
            total = mine[...] + came.astype(F32)
            mine[...] = total

            @pl.when(j != at.p)
            def _():
                of("z_send", group)[chunk_rows(group, j), :] = total.astype(BF16)
                z_copy(group, j).start()

        each_owner(group, act)

    def x_copy(j):
        lines = chunk_rows(2, j)
        return remote(b.x_send.at[lines], b.x_recv.at[lines], s.xs, j, at.across)

    def place(group, t, j):
        first_row = t * SET_ROWS[group] + j * chunks[group]
        return of("sums", group).at[pl.ds(pl.multiple_of(first_row, 16), chunks[group])]

    def gather_copy(group, t, j, sems, device, source=None):
        piece = place(group, t, j)
        return remote(piece if source is None else source, piece, sems, (group, j), device)

    def spread(group, j, source=None):
        @pl.when(jnp.logical_and(j <= at.p, at.has_up))
        def _():
            gather_copy(group, at.r, j, s.gu, at.up, source).start()

        @pl.when(jnp.logical_and(j >= at.p, at.has_down))
        def _():
            gather_copy(group, at.r, j, s.gd, at.down, source).start()

        gather_copy(group, at.r, j, s.gy, at.beside, source).start()
        gather_copy(group, at.r, j, s.gc, at.sister, source).start()

    def settle_copy(group):
        return pltpu.make_async_copy(
            of("final", group), place(group, at.r, at.p), s.local[0].at[4 + group]
        )

    def settle(group):
        @pl.when(at.p < owners[group])
        def _():
            came = of("z_recv", group)

            def add(d, total):
                q = (at.p + d) % planes
                remote(came.at[q], came.at[q], s.zs, (group, q), at.plane(q)).wait_recv()
                return total + came[q].astype(F32)

            total = lax.fori_loop(1, planes, add, own_chunk(group, at.p)[...])
            of("final", group)[...] = total.astype(BF16)
            spread(group, at.p, of("final", group))
            settle_copy(group).start()

    def come_in(group):
        def one(d, carry):
            @pl.when(jnp.logical_and(at.p - d >= 0, at.p - d < owners[group]))
            def _():
                gather_copy(group, at.r, at.p - d, s.gu, at.down).wait_recv()
                spread(group, at.p - d)

            @pl.when(at.p + d < owners[group])
            def _():
                gather_copy(group, at.r, at.p + d, s.gd, at.up).wait_recv()
                spread(group, at.p + d)

            return carry

        lax.fori_loop(1, planes, one, 0)

    def hand_over(group):
        def act(j):
            gather_copy(group, at.peer(2), j, s.gy, at.beside).wait_recv()
            gather_copy(group, at.peer(2), j, s.gf, at.sister).start()

        each_owner(group, act, 0)

    for c in range(4):
        cols = slice(c * MODEL, (c + 1) * MODEL)
        d_inner = (
            lax.dot_general(b.d_second[...], b.wb[cols, :], NT, preferred_element_type=F32)
            * b.slope[c * BOTH : (c + 1) * BOTH, :]
        )
        b.small[5 + c : 6 + c, :] = column_sum(d_inner)
        low = d_inner.astype(BF16)
        b.d_inner[:, cols] = low
        b.second[...] += lax.dot_general(low, b.wi[:, cols], NT, preferred_element_type=F32)
    d_normed = b.second[...]
    unit_one = b.unit_one[...]
    b.small[3:4, :] = column_sum(d_normed * unit_one)
    b.small[4:5, :] = column_sum(d_normed)
    d_first = norm_back(d_normed, unit_one, inverse_one, bias[3:4])
    b.small[2:3, :] = column_sum(d_first)
    d_first_low = d_first.astype(BF16)
    b.d_first[...] = d_first_low
    b.d_tokens[...] = d_first[:BLOCK]
    d_attn = lax.dot_general(d_first_low[:BLOCK], b.wo[...], NT, preferred_element_type=F32)
    for g in range(GROUP):
        b.dsend[g] = jnp.concatenate(
            [zero_lanes, d_attn[:, g * LANES : (g + 1) * LANES]], axis=1
        ).astype(BF16)
    for d in (1, 2, 3):
        g = at.peer(d)
        start(
            remote(
                b.dsend.at[g], b.do.at[block_rows(0, at.r)], s.a2a, (4, d), at.in_plane(g)
            )
        )
    b.do[block_rows(0, at.r), :] = b.dsend[at.r]

    tok_block(at.peer(2), 0, at.beside).wait_recv()
    start(tok_block(at.peer(2), 2, at.sister))
    produce(0)

    b.grads[...] = jnp.zeros_like(b.grads)
    b.dq[...] = jnp.zeros_like(b.dq)
    for i in range(3):
        for j in range(GROUP):
            b.k_ids[(i * GROUP + j) * BLOCK : (i * GROUP + j + 1) * BLOCK, :] = column_of(
                b.ids[i, j][0:1, :]
            )
    q_ids = jnp.concatenate([b.ids[1, j][0:1, :] for j in range(GROUP)], axis=1)
    lse_rows = b.lse[...].T
    for d in (1, 2, 3):
        from_peer(b.do.at[block_rows(0, at.peer(d))], 4, d)
    prod = (b.do[...].astype(F32) * b.og[...]).T
    for h in range(GROUP_HEADS):
        b.stats[h] = jnp.broadcast_to(lse_rows[h : h + 1, :], (8, PLANE))
        b.stats[GROUP_HEADS + h] = jnp.broadcast_to(
            column_sum(prod[HEAD_DIM * (h + 1) : HEAD_DIM * (h + 2), :]), (8, PLANE)
        )

    def visit(h, i):
        span = pl.ds(i * PLANE, PLANE)
        pick_q = lane_head((PLANE, 256), 0) == h
        q = b.qp[...]
        q = jnp.where(pick_q, q, jnp.zeros_like(q))
        dout = b.do[...]
        dout = jnp.where(lane_head((PLANE, 256), 1) == h, dout, jnp.zeros_like(dout))
        keys = b.kv[span, 0:256]
        score = lax.dot_general(keys, q * SCALE, NT, preferred_element_type=F32)
        same = b.k_ids[span, 0:1] == q_ids
        prob = jnp.where(same, jnp.exp(score - b.stats[h][0:1, :]), 0.0)
        d_prob = lax.dot_general(b.kv[span, 128:384], dout, NT, preferred_element_type=F32)
        d_score = (prob * (d_prob - b.stats[GROUP_HEADS + h][0:1, :]) * SCALE).astype(BF16)
        b.grads[span, 0:256] += jnp.dot(d_score, q, preferred_element_type=F32)
        b.grads[span, 128:384] += jnp.dot(
            prob.astype(BF16), dout, preferred_element_type=F32
        )
        b.dq[...] += jnp.where(
            pick_q, lax.dot_general(d_score, keys, TN, preferred_element_type=F32), 0.0
        )

    def visit_plane(i):
        def one(h, carry):
            visit(h, i)
            return carry

        lax.fori_loop(0, GROUP_HEADS, one, 0)

    down_grads = remote(b.halo_send.at[0], b.halo.at[1], s.halo_b, 0, at.down)
    up_grads = remote(b.halo_send.at[1], b.halo.at[0], s.halo_b, 1, at.up)
    visit_plane(0)
    b.halo_send[0] = b.grads[pl.ds(0, PLANE), :].astype(BF16)

    @pl.when(at.has_down)
    def _():
        down_grads.start()

    visit_plane(2)
    b.halo_send[1] = b.grads[pl.ds(2 * PLANE, PLANE), :].astype(BF16)

    @pl.when(at.has_up)
    def _():
        up_grads.start()

    visit_plane(1)
    b.d_group[:, 0:256] = b.dq[...].astype(BF16)
    b.out_tile[...] = lax.dot_general(
        b.att2[:, pl.ds(near_rows, HALF)], b.d_first[...], TN, preferred_element_type=F32
    )
    produce(1)

    @pl.when(at.has_up)
    def _():
        remote(b.halo.at[1], b.halo.at[1], s.halo_b, 0, at.up).wait_recv()
        b.grads[pl.ds(PLANE, PLANE), :] += b.halo[1].astype(F32)

    @pl.when(at.has_down)
    def _():
        remote(b.halo.at[0], b.halo.at[0], s.halo_b, 1, at.down).wait_recv()
        b.grads[pl.ds(PLANE, PLANE), :] += b.halo[0].astype(F32)

    b.d_group[:, 256:640] = b.grads[pl.ds(PLANE, PLANE), :].astype(BF16)

    tok_block(at.peer(1), 1, at.sister).wait_recv()
    tok_block(at.peer(3), 2, at.sister).wait_recv()
    b.x_send[...] = lax.dot_general(
        b.tok_plane[:, pl.ds(far_rows, HALF)], b.d_group[...], TN, preferred_element_type=F32
    ).astype(BF16)
    each_owner(2, lambda j: x_copy(j).start())
    b.line_send[...] = jnp.broadcast_to(column_sum(b.d_group[...].astype(F32)), (8, 640))
    line_copy = remote(b.line_send, b.line_recv, s.ex, 4, at.across)
    start(line_copy)
    for d in (1, 2, 3):
        i = at.peer(d)
        start(
            remote(
                b.d_group.at[block_rows(0, i)],
                b.d_recv.at[at.r],
                s.a2a,
                (5, d),
                at.in_plane(i),
            )
        )
    b.d_recv[at.r] = b.d_group[block_rows(0, at.r), :]
    b.q_sum[...] = lax.dot_general(
        b.tok_plane[:, pl.ds(near_rows, HALF)], b.d_group[...], TN, preferred_element_type=F32
    )
    scatter(0)
    scatter(2)

    partners = [at.sister, at.beside]
    span = 1
    while span < planes:
        partners.append((at.c + GROUP * span * (1 - 2 * ((at.p // span) % 2)), at.x))
        span *= 2

    def small_copy(i):
        return remote(b.small, b.small_recv.at[i], s.sm, i, partners[i])

    def small_finish(i):
        small_copy(i).wait()
        b.small[...] += b.small_recv[i]

    line_copy.wait_recv()
    line = b.line_send[...] + b.line_recv[...]
    mine = lax.broadcasted_iota(jnp.int32, (8, 640), 0) == at.r
    b.small[16:24, 0:640] = jnp.where(mine, line, 0.0)
    small_copy(0).start()
    settle(0)
    small_finish(0)
    small_copy(1).start()
    scatter(1)
    small_finish(1)
    small_copy(2).start()
    settle(2)
    come_in(0)
    small_finish(2)
    small_copy(3).start()

    for d in (1, 2, 3):
        from_peer(b.d_recv.at[at.peer(d)], 5, d)
    for j, first_lane in enumerate((0, 256, 448)):
        b.d_packed[:, j * MODEL : (j + 1) * MODEL] = jnp.concatenate(
            [
                b.d_recv[g].astype(F32)[:, first_lane : first_lane + LANES]
                for g in range(GROUP)
            ],
            axis=1,
        ).astype(BF16)
    b.d_tokens[...] += lax.dot_general(
        b.d_packed[...], b.wq[...], NT, preferred_element_type=F32
    )

    hand_over(0)
    small_finish(3)
    for i in range(4, len(partners)):
        small_copy(i).start()
        small_finish(i)
    settle(1)
    come_in(2)
    hand_over(2)
    come_in(1)
    hand_over(1)

    for group in range(3):

        def last(j, carry, group=group):
            gather_copy(group, at.peer(1), j, s.gc, at.sister).wait_recv()
            gather_copy(group, at.peer(3), j, s.gf, at.sister).wait_recv()
            gather_copy(group, at.r, j, s.gy, at.beside).wait_send()
            gather_copy(group, at.r, j, s.gc, at.sister).wait_send()
            gather_copy(group, at.peer(2), j, s.gf, at.sister).wait_send()
            if group == 2:
                x_copy(j).wait_send()
            else:
                y_copy(group, j).wait_send()

            @pl.when(jnp.logical_and(j <= at.p, at.has_up))
            def _():
                gather_copy(group, at.r, j, s.gu, at.up).wait_send()

            @pl.when(jnp.logical_and(j >= at.p, at.has_down))
            def _():
                gather_copy(group, at.r, j, s.gd, at.down).wait_send()

            @pl.when(j != at.p)
            def _():
                z_copy(group, j).wait_send()

            return carry

        lax.fori_loop(0, owners[group], last, 0)

        @pl.when(at.p < owners[group])
        def _(group=group):
            settle_copy(group).wait()

    for copy in sent:
        copy.wait_send()

    def finish(copy):
        copy.wait_send()

    for d in range(4):
        both_ways(up_kv(d), down_kv(d), finish)
    both_ways(up_ids, down_ids, finish)
    both_ways(up_grads, down_grads, finish)


def layer_call(planes, args):
    buffers, semaphores = scratch_plan(planes)
    hbm = pl.BlockSpec(memory_space=pltpu.HBM)
    vmem = pl.BlockSpec(memory_space=pltpu.VMEM)
    weights = ("w_qkv", "w_out", "w_in", "w_back")
    scratch = [pltpu.VMEM(shape, kind) for shape, kind in buffers.values()]
    for shape in semaphores.values():
        scratch += [pltpu.SemaphoreType.DMA(shape)] * 2
    return pl.pallas_call(
        functools.partial(layer_kernel, planes, list(buffers), list(semaphores)),
        out_shape=[
            jax.ShapeDtypeStruct((BLOCK, MODEL), BF16),
            jax.ShapeDtypeStruct((BLOCK, MODEL), F32),
        ]
        + [
            jax.ShapeDtypeStruct((TILES * rows, width), BF16)
            for rows, width in zip(SET_ROWS, SET_WIDTH)
        ]
        + [jax.ShapeDtypeStruct((24, MODEL), F32)],
        in_specs=[hbm if name in weights else vmem for name in ARGS],
        out_specs=[vmem, vmem, hbm, hbm, hbm, vmem],
        scratch_shapes=scratch,
        compiler_params=pltpu.CompilerParams(
            collective_id=0, has_side_effects=True, vmem_limit_bytes=60 * 2**20
        ),
        name="layer",
    )(*args)


def unpack_kernel(result_in, tokens_in, sums0, sums1, sums2, small, *refs):
    result, d_tokens, w_qkv, bq, bv, w_out, bo, g1, o1, w_in, bi, w_back, bb, g2, o2 = refs[:15]
    in0, in1, in2, out_q, out_o, out_i, out_b, come, go = refs[15:]
    loads = []
    for g, (sums, held) in enumerate(((sums0, in0), (sums1, in1), (sums2, in2))):
        for t in range(TILES):
            lines = pl.ds(t * SET_ROWS[g], SET_ROWS[g])
            loads.append(
                pltpu.make_async_copy(sums.at[lines], held.at[t], come.at[g * TILES + t])
            )
    for load in loads:
        load.start()
    stores = [
        pltpu.make_async_copy(result_in, result, go.at[14]),
        pltpu.make_async_copy(tokens_in, d_tokens, go.at[15]),
    ]
    for store in stores:
        store.start()

    def put(source, target, i):
        store = pltpu.make_async_copy(source, target, go.at[i])
        store.start()
        stores.append(store)

    x = lax.axis_index("wsh")
    half = small[0:16, pl.ds(pl.multiple_of(x * HALF, 128), HALF)]
    for ref, row in zip((bo, g1, o1, bb, g2, o2), (2, 3, 4, 9, 10, 11)):
        ref[...] = half[row, :]
    whole = jnp.where(x == 0, small[5:7, :], small[7:9, :])
    bi[pl.ds(0, MODEL)] = whole[0, :]
    bi[pl.ds(MODEL, MODEL)] = whole[1, :]
    for ref, first in ((bq, 0), (bv, 448)):
        row = jnp.concatenate(
            [small[16 + g : 17 + g, first : first + LANES] for g in range(GROUP)], axis=1
        )
        ref[...] = jnp.where(x == 0, row[:, :HALF], row[:, HALF:])[0, :]

    for t in range(TILES):
        loads[t].wait()
        lines = pl.ds(t * HALF, HALF)
        out_b[lines, :] = in0[t].astype(F32)
        put(out_b.at[lines], w_back.at[lines], t)
    for t in range(TILES):
        loads[TILES + t].wait()
        out_i[t] = in1[t, 0:HALF, :].astype(F32)
        put(out_i.at[t], w_in.at[:, pl.ds(t * MODEL, MODEL)], 4 + t)
        lines = pl.ds(t * QUARTER, QUARTER)
        out_o[lines, :] = in1[t, HALF : HALF + QUARTER, :].astype(F32)
        put(out_o.at[lines], w_out.at[lines], 8 + t)
    for pair in range(2):
        loads[2 * TILES + 2 * pair].wait()
        loads[2 * TILES + 2 * pair + 1].wait()
        for j, first in enumerate((0, 256, 448)):
            out_q[:, j * MODEL + pair * HALF : j * MODEL + (pair + 1) * HALF] = (
                jnp.concatenate(
                    [
                        in2[2 * pair + i].astype(F32)[:, first : first + LANES]
                        for i in range(2)
                    ],
                    axis=1,
                )
            )
    put(out_q, w_qkv, 12)
    for store in stores:
        store.wait()


def unpack_call(*arrays):
    shape = jax.ShapeDtypeStruct
    vmem = pl.BlockSpec(memory_space=pltpu.VMEM)
    hbm = pl.BlockSpec(memory_space=pltpu.HBM)
    vector = (shape((HALF,), F32), vmem)
    outs = [
        (shape((BLOCK, MODEL), BF16), hbm),
        (shape((BLOCK, MODEL), F32), hbm),
        (shape((HALF, 3 * MODEL), F32), hbm),
        vector,
        vector,
        (shape((HALF, MODEL), F32), hbm),
        vector,
        vector,
        vector,
        (shape((HALF, FF), F32), hbm),
        (shape((FF // 2,), F32), vmem),
        (shape((FF // 2, MODEL), F32), hbm),
        vector,
        vector,
        vector,
    ]
    return pl.pallas_call(
        unpack_kernel,
        out_shape=[o[0] for o in outs],
        in_specs=[vmem, vmem, hbm, hbm, hbm, vmem],
        out_specs=[o[1] for o in outs],
        scratch_shapes=[
            pltpu.VMEM((TILES, rows, width), BF16)
            for rows, width in zip(SET_ROWS, SET_WIDTH)
        ]
        + [
            pltpu.VMEM((HALF, 3 * MODEL), F32),
            pltpu.VMEM((HALF, MODEL), F32),
            pltpu.VMEM((TILES, HALF, MODEL), F32),
            pltpu.VMEM((FF // 2, MODEL), F32),
            pltpu.SemaphoreType.DMA((3 * TILES,)),
            pltpu.SemaphoreType.DMA((16,)),
        ],
        compiler_params=pltpu.CompilerParams(vmem_limit_bytes=60 * 2**20),
        name="unpack",
    )(*arrays)


def body(*args):
    planes = lax.axis_size("ctx") // GROUP
    result, d_tokens, *rest = unpack_call(*layer_call(planes, args))
    return (result[None], d_tokens[None], *rest)


def solution(mesh):
    token_spec = P("wsh", "ctx", None)
    matrix, vector = P("wsh", None), P("wsh")
    in_specs = (
        token_spec,
        P("wsh", "ctx"),
        matrix,
        vector,
        vector,
        matrix,
        vector,
        vector,
        vector,
        matrix,
        vector,
        matrix,
        vector,
        vector,
        vector,
        token_spec,
    )
    out_specs = (
        token_spec,
        token_spec,
        matrix,
        vector,
        vector,
        matrix,
        vector,
        vector,
        vector,
        matrix,
        vector,
        matrix,
        vector,
        vector,
        vector,
    )
    return jax.shard_map(body, mesh=mesh, in_specs=in_specs, out_specs=out_specs, check_vma=False)
```

```python
import functools
import types

import jax
import jax.numpy as jnp
from jax import lax
from jax.experimental import pallas as pl
from jax.experimental.pallas import tpu as pltpu
from jax.sharding import PartitionSpec as P

HEAD_DIM = 64
GROUP = 4
GROUP_HEADS = 3
BLOCK = 128
PLANE = GROUP * BLOCK
MODEL = 768
FF = 3072
HALF = MODEL // 2
LANES = GROUP_HEADS * HEAD_DIM
TILES = 4
OWN_ROWS = (4 * 2 * BLOCK, 0)
BOTH = 2 * BLOCK
EPSILON = 1e-05
NEGATIVE = -1e30
ROOT_HALF = 0.7071067811865476
INV_ROOT_TAU = 0.3989422804014327
SCALE = HEAD_DIM**-0.5
MESH = pl.DeviceIdType.MESH
F32 = jnp.float32
BF16 = jnp.bfloat16
NT = (((1,), (1,)), ((), ()))
TN = (((0,), (0,)), ((), ()))


class Place:
    def __init__(self, planes):
        self.n = planes
        self.c = lax.axis_index("ctx")
        self.x = lax.axis_index("wsh")
        self.p = self.c // GROUP
        self.r = self.c % GROUP
        self.y = self.r // 2
        self.k = self.r % 2
        self.parity = self.p % 2
        self.sister = (self.c + 1 - 2 * self.k, self.x)
        self.beside = (self.c + 2 - 4 * self.y, self.x)
        self.across = (self.c, 1 - self.x)
        self.pair = (self.c + GROUP * (1 - 2 * self.parity), self.x)
        self.up = (self.c + GROUP, self.x)
        self.down = (self.c - GROUP, self.x)
        self.has_up = self.p < planes - 1
        self.has_down = self.p > 0

    def peer(self, d):
        if d == 1:
            return self.y * 2 + (1 - self.k)
        if d == 2:
            return (1 - self.y) * 2 + self.k
        return (1 - self.y) * 2 + (1 - self.k)

    def in_plane(self, position):
        return (self.p * GROUP + position, self.x)

    def plane(self, p):
        return (p * GROUP + self.r, self.x)


def signal(sem, device):
    pl.semaphore_signal(sem, inc=1, device_id=device, device_id_type=MESH)


def greet(at):
    barrier = pltpu.get_barrier_semaphore()
    for d in (1, 2, 3):
        signal(barrier, at.in_plane(at.peer(d)))
    signal(barrier, at.across)

    def other_plane(d, carry):
        signal(barrier, at.plane((at.p + d) % at.n))
        return carry

    lax.fori_loop(1, at.n, other_plane, 0)
    pl.semaphore_wait(barrier, 4 + at.n - 1)


def remote(src, dst, sems, index, device, recv_index=None):
    send, recv = sems
    return pltpu.make_async_remote_copy(
        src_ref=src,
        dst_ref=dst,
        send_sem=send.at[index],
        recv_sem=recv.at[index if recv_index is None else recv_index],
        device_id=device,
        device_id_type=MESH,
    )


def lane_head(shape, first):
    return lax.broadcasted_iota(jnp.int32, shape, 1) // HEAD_DIM - first


def column_of(row):
    return jnp.broadcast_to(row, (BLOCK, BLOCK)).T


def chunk_of(rows, planes):
    chunk = -(-(-(-rows // planes)) // 16) * 16
    while rows % chunk:
        chunk += 16
    return chunk


SET_ROWS = (HALF, 512, HALF)
SET_WIDTH = (MODEL, MODEL, 640)
QUARTER = HALF // GROUP


def scratch_plan(planes):
    steps = planes.bit_length() - 1
    buffers = dict(
        wq=((MODEL, 3 * MODEL), BF16),
        wo=((MODEL, MODEL), BF16),
        wi=((MODEL, FF), BF16),
        wb=((FF, MODEL), BF16),
        bias_own=((16, HALF), BF16),
        bias2=((2, 16, HALF), BF16),
        dout_far=((BLOCK, MODEL), BF16),
        ids=((3, GROUP, 8, BLOCK), F32),
        acc=((PLANE, 3 * 256), F32),
        qp=((PLANE, 256), BF16),
        kv=((3 * PLANE, 2 * LANES), BF16),
        out_t=((GROUP_HEADS, HEAD_DIM, PLANE), F32),
        peaks=((2 * GROUP_HEADS, 8, PLANE), F32),
        asend=((GROUP, BLOCK, 256), BF16),
        arecv=((GROUP, BLOCK, 256), BF16),
        tok_plane=((PLANE, MODEL), BF16),
        tok2=((BOTH, MODEL), BF16),
        att2=((BOTH, MODEL), BF16),
        unit_one=((BOTH, MODEL), F32),
        norm_low=((BOTH, MODEL), BF16),
        act=((BOTH, FF), BF16),
        d_inner=((BOTH, FF), BF16),
        d_second=((BOTH, MODEL), BF16),
        d_first=((BOTH, MODEL), BF16),
        second=((BOTH, MODEL), F32),
        slope=((4 * BOTH + HALF, MODEL), F32),
        out_tile=((HALF, MODEL), F32),
        dsend=((GROUP, BLOCK, 256), BF16),
        do=((PLANE, 256), BF16),
        grads=((3 * PLANE, 2 * LANES), F32),
        dq=((PLANE, 256), F32),
        k_ids=((3 * PLANE, BLOCK), F32),
        stats=((2 * GROUP_HEADS, 8, PLANE), F32),
        halo_send=((2, PLANE, 2 * LANES), BF16),
        halo=((2, PLANE, 2 * LANES), BF16),
        d_group=((PLANE, 640), BF16),
        d_recv=((GROUP, BLOCK, 640), BF16),
        d_packed=((BLOCK, 3 * MODEL), BF16),
        q_sum=((HALF, 640), F32),
        x_send=((HALF, 640), BF16),
        x_recv=((HALF, 640), BF16),
        small_recv=((2 + steps, 24, MODEL), F32),
        line_send=((8, 640), F32),
        line_recv=((8, 640), F32),
    )
    for g, (rows, width) in enumerate(zip(SET_ROWS, SET_WIDTH)):
        chunk = chunk_of(rows, planes)
        if g < 2:
            buffers[f"core_send{g}"] = ((2, rows, width), BF16)
            buffers[f"core_recv{g}"] = ((2, rows, width), BF16)
            buffers[f"y_send{g}"] = ((rows, width), BF16)
            buffers[f"y_recv{g}"] = ((rows, width), BF16)
        buffers[f"z_send{g}"] = ((rows, width), BF16)
        buffers[f"up_recv{g}"] = ((rows, width), BF16)
        buffers[f"down_recv{g}"] = ((rows, width), BF16)
        buffers[f"final{g}"] = ((chunk, width), BF16)
    semaphores = dict(
        local=(4 + 3,),
        qx=(3,),
        qz=(3,),
        qc=(2, 3),
        late_x=(3,),
        late_c=(3,),
        wx=(4, 2),
        wy=(4, 2),
        wz=(4, 2),
        wc=(4, 5),
        ex=(5,),
        tp=(4,),
        a2a=(6, 4),
        halo_f=(2, 5),
        halo_b=(2,),
        core=(4,),
        xs=(planes,),
        ys=(2, planes),
        up=(3, planes),
        down=(3, planes),
        gu=(3, planes),
        gd=(3, planes),
        gy=(3, planes),
        gc=(3, planes),
        gf=(3, planes),
        sm=(2 + steps,),
    )
    return buffers, semaphores


ARGS = ["tokens", "doc_ids", "w_qkv", "b_query", "b_value", "w_out", "b_out", "ln1_gain"]
ARGS += ["ln1_bias", "w_in", "b_in", "w_back", "b_back", "ln2_gain", "ln2_bias", "d_out"]
RESULTS = ["result", "d_tokens", "sums0", "sums1", "sums2", "small"]


def layer_kernel(planes, names, sem_names, *refs):
    split = len(ARGS) + len(RESULTS) + len(names)
    b = types.SimpleNamespace(**dict(zip(ARGS + RESULTS + names, refs[:split])))
    pairs = refs[split:]
    s = types.SimpleNamespace(
        **{n: (pairs[2 * i], pairs[2 * i + 1]) for i, n in enumerate(sem_names)}
    )
    at = Place(planes)
    sent = []

    def start(copy):
        copy.start()
        sent.append(copy)

    def block_rows(first, i):
        return pl.ds(pl.multiple_of(first + i * BLOCK, BLOCK), BLOCK)

    b.ids[1, at.r] = jnp.broadcast_to(b.doc_ids[...].astype(F32), (8, BLOCK))
    b.tok_plane[block_rows(0, at.r), :] = b.tokens[0]

    @pl.when(jnp.logical_not(at.has_down))
    def _():
        b.kv[pl.ds(0, PLANE), :] = jnp.zeros((PLANE, 2 * LANES), BF16)
        b.ids[0] = jnp.full((GROUP, 8, BLOCK), -1.0, F32)

    @pl.when(jnp.logical_not(at.has_up))
    def _():
        b.kv[pl.ds(2 * PLANE, PLANE), :] = jnp.zeros((PLANE, 2 * LANES), BF16)
        b.ids[2] = jnp.full((GROUP, 8, BLOCK), -1.0, F32)

    vectors = [b.b_query, b.b_value, b.b_out, b.ln1_gain, b.ln1_bias]
    lines = [v[...].astype(F32).reshape(1, HALF) for v in vectors]
    lines += [
        b.b_in[pl.ds(i * HALF, HALF)].astype(F32).reshape(1, HALF) for i in range(4)
    ]
    lines += [
        v[...].astype(F32).reshape(1, HALF) for v in (b.b_back, b.ln2_gain, b.ln2_bias)
    ]
    lines.append(jnp.zeros((4, HALF), F32))
    packed_bias = jnp.concatenate(lines, axis=0).astype(BF16)
    b.bias_own[...] = packed_bias
    b.bias2[at.x] = packed_bias
    greet(at)

    shards = (b.w_qkv, b.w_out, b.w_in, b.w_back)
    wholes = (b.wq, b.wo, b.wi, b.wb)
    direct = (True, True, True, False)
    own_q = at.y * 2 + at.parity
    diag_q = (1 - at.y) * 2 + (1 - at.parity)
    beside_q = (1 - at.y) * 2 + at.parity
    pair_q = at.y * 2 + (1 - at.parity)

    def rows(w, quarter, core):
        eighth = shards[w].shape[0] // 8
        return pl.multiple_of((quarter * 2 + core) * eighth, 16), eighth

    def far(w, quarter, core, part=None):
        first, size = rows(w, quarter, core)
        base = (1 - at.x) * shards[w].shape[0]
        lines = pl.ds(pl.multiple_of(base + first, 16), size)
        if part is None:
            return wholes[w].at[lines]
        width = shards[w].shape[1] // 2
        return wholes[w].at[lines, pl.ds(part * width, width)]

    def across_copy(w, i):
        first, size = rows(w, (own_q, diag_q)[i], at.k)
        base = at.x * shards[w].shape[0]
        return remote(
            shards[w].at[pl.ds(first, size)],
            wholes[w].at[pl.ds(pl.multiple_of(base + first, 16), size)],
            s.wx,
            (w, i),
            at.across,
        )

    def piece_copy(w, quarter, sems, index, device, part=None, core=None):
        piece = far(w, quarter, at.k if core is None else core, part)
        return remote(piece, piece, sems, (w, index), device)

    def relay_own(w):
        piece_copy(w, own_q, s.wx, 0, at.across).wait_recv()
        start(piece_copy(w, own_q, s.wy, 0, at.beside))
        start(piece_copy(w, own_q, s.wz, 0, at.pair))
        start(piece_copy(w, own_q, s.wc, 0, at.sister))

    def relay_rest(w):
        if direct[w]:
            piece_copy(w, diag_q, s.wx, 1, at.across).wait_recv()
            start(piece_copy(w, diag_q, s.wc, 1, at.sister))
        piece_copy(w, beside_q, s.wy, 0, at.beside).wait_recv()
        if not direct[w]:
            start(piece_copy(w, beside_q, s.wz, 1, at.pair, part=1))
        start(piece_copy(w, beside_q, s.wc, 2, at.sister))
        piece_copy(w, pair_q, s.wz, 0, at.pair).wait_recv()
        if not direct[w]:
            start(piece_copy(w, pair_q, s.wy, 1, at.beside, part=0))
        start(piece_copy(w, pair_q, s.wc, 3, at.sister))

    def relay_diagonal(w):
        piece_copy(w, diag_q, s.wy, 1, at.beside, part=0).wait_recv()
        start(piece_copy(w, diag_q, s.wc, 1, at.sister, part=0))
        piece_copy(w, diag_q, s.wz, 1, at.pair, part=1).wait_recv()
        start(piece_copy(w, diag_q, s.wc, 4, at.sister, part=1))

    def sister_arrivals(w):
        other = 1 - at.k
        piece_copy(w, own_q, s.wc, 0, at.sister, core=other).wait_recv()
        piece_copy(w, beside_q, s.wc, 2, at.sister, core=other).wait_recv()
        piece_copy(w, pair_q, s.wc, 3, at.sister, core=other).wait_recv()
        if direct[w]:
            piece_copy(w, diag_q, s.wc, 1, at.sister, core=other).wait_recv()
        else:
            piece_copy(w, diag_q, s.wc, 1, at.sister, part=0, core=other).wait_recv()
            piece_copy(w, diag_q, s.wc, 4, at.sister, part=1, core=other).wait_recv()

    near_tokens = pl.ds(0, BLOCK)
    far_tokens = pl.ds(BLOCK, BLOCK)
    bias_copy = remote(b.bias_own, b.bias2.at[at.x], s.ex, 0, at.across)
    tok_copy = remote(b.tokens.at[0], b.tok2.at[far_tokens], s.ex, 1, at.across)
    dout_copy = remote(b.d_out.at[0], b.dout_far, s.ex, 2, at.across)
    def q_piece(ref, first_row, size, j, side):
        return ref.at[
            pl.ds(pl.multiple_of(first_row, 16), size),
            pl.ds(pl.multiple_of(j * MODEL + side * HALF, 128), HALF),
        ]

    def q_rows(core, parity):
        return (core * 2 + parity) * QUARTER

    far_base = (1 - at.x) * HALF
    near_base = at.x * HALF

    def q_across(j):
        line = q_rows(at.k, at.parity)
        return remote(
            q_piece(b.w_qkv, line, QUARTER, j, at.y),
            q_piece(b.wq, near_base + line, QUARTER, j, at.y),
            s.qx,
            j,
            at.across,
        )

    def q_move(core, parity, j, sems, index, device):
        piece = q_piece(b.wq, far_base + q_rows(core, parity), QUARTER, j, at.y)
        return remote(piece, piece, sems, index, device)

    def late_across(j):
        line = at.k * 2 * QUARTER
        return remote(
            q_piece(b.w_qkv, line, 2 * QUARTER, j, 1 - at.y),
            q_piece(b.wq, near_base + line, 2 * QUARTER, j, 1 - at.y),
            s.late_x,
            j,
            at.across,
        )

    def late_move(core, j, sems, device):
        piece = q_piece(b.wq, far_base + core * 2 * QUARTER, 2 * QUARTER, j, 1 - at.y)
        return remote(piece, piece, sems, j, device)

    def tok_block(i, sem, device):
        piece = b.tok_plane.at[block_rows(0, i)]
        return remote(piece, piece, s.tp, sem, device)

    own_copies = []
    for w in range(4):
        size = shards[w].shape[0]
        own_copies.append(
            pltpu.make_async_copy(
                shards[w],
                wholes[w].at[pl.ds(pl.multiple_of(at.x * size, 16), size)],
                s.local[0].at[w],
            )
        )
    for j in range(3):
        start(q_across(j))
    start(bias_copy)
    start(tok_block(at.r, 0, at.beside))
    start(tok_block(at.r, 1, at.sister))
    own_copies[0].start()
    for d in (1, 2, 3):
        mine = b.ids.at[1, at.r]
        start(remote(mine, mine, s.a2a, (0, d), at.in_plane(at.peer(d))))

    near_rows = pl.multiple_of(at.x * HALF, HALF)
    far_rows = pl.multiple_of((1 - at.x) * HALF, HALF)
    b.tok2[near_tokens, :] = b.tokens[0]
    for j in range(3):
        q_move(at.k, at.parity, j, s.qx, j, at.across).wait_recv()
        start(q_move(at.k, at.parity, j, s.qz, j, at.pair))
        start(q_move(at.k, at.parity, j, s.qc, (0, j), at.sister))
    start(across_copy(2, 0))
    for i in range(2):
        start(across_copy(1, i))
    start(across_copy(3, 0))
    start(across_copy(2, 1))
    start(tok_copy)
    for w in (1, 2, 3):
        own_copies[w].start()
    tok_block(at.peer(2), 0, at.beside).wait_recv()
    start(tok_block(at.peer(2), 2, at.sister))
    for j in range(3):
        q_move(at.k, 1 - at.parity, j, s.qz, j, at.pair).wait_recv()
        start(q_move(at.k, 1 - at.parity, j, s.qc, (1, j), at.sister))
    tok_block(at.peer(1), 1, at.sister).wait_recv()
    tok_block(at.peer(3), 2, at.sister).wait_recv()
    own_copies[0].wait()
    window = [
        pl.ds(pl.multiple_of(j * MODEL + at.y * HALF + at.k * 128, 128), 256) for j in range(3)
    ]
    for j in range(3):
        b.acc[:, j * 256 : (j + 1) * 256] = jnp.dot(
            b.tok_plane[:, pl.ds(near_rows, HALF)],
            b.wq[pl.ds(near_rows, HALF), window[j]],
            preferred_element_type=F32,
        )
    remote(b.bias_own, b.bias2.at[1 - at.x], s.ex, 0, at.across).wait_recv()
    halves = (b.bias2[0].astype(F32), b.bias2[1].astype(F32))
    bias = jnp.concatenate(halves, axis=1)

    def group_bias(row):
        line = bias[row : row + 1, 0:LANES]
        for g in range(1, GROUP):
            line = jnp.where(at.r == g, bias[row : row + 1, g * LANES : (g + 1) * LANES], line)
        return line

    for j in range(3):
        q_move(1 - at.k, at.parity, j, s.qc, (0, j), at.sister).wait_recv()
        q_move(1 - at.k, 1 - at.parity, j, s.qc, (1, j), at.sister).wait_recv()
    made = []
    for j in range(3):
        part = b.acc[:, j * 256 : (j + 1) * 256] + jnp.dot(
            b.tok_plane[:, pl.ds(far_rows, HALF)],
            b.wq[pl.ds(far_rows, HALF), window[j]],
            preferred_element_type=F32,
        )
        made.append(jnp.where(at.k == 0, part[:, 0:LANES], part[:, HEAD_DIM:256]))
    b.kv[pl.ds(PLANE, PLANE), :] = jnp.concatenate(
        [made[1], made[2] + group_bias(1)], axis=1
    ).astype(BF16)

    def both_ways(up, down, act):
        @pl.when(at.has_up)
        def _():
            act(up)

        @pl.when(at.has_down)
        def _():
            act(down)

    def go(copy):
        copy.start()

    middle = b.kv.at[pl.ds(PLANE, PLANE)]
    up_kv = remote(middle, b.kv.at[pl.ds(0, PLANE)], s.halo_f, (0, 0), at.up)
    down_kv = remote(middle, b.kv.at[pl.ds(2 * PLANE, PLANE)], s.halo_f, (1, 0), at.down)
    up_ids = remote(b.ids.at[1], b.ids.at[0], s.halo_f, (0, 1), at.up)
    down_ids = remote(b.ids.at[1], b.ids.at[2], s.halo_f, (1, 1), at.down)

    def from_peer(piece, kind, d):
        remote(piece, piece, s.a2a, (kind, d), at.in_plane(at.peer(d))).wait_recv()

    both_ways(up_kv, down_kv, go)
    b.qp[...] = jnp.concatenate(
        [made[0] + group_bias(0), jnp.zeros((PLANE, HEAD_DIM), F32)], axis=1
    ).astype(BF16)
    for d in (1, 2, 3):
        from_peer(b.ids.at[1, at.peer(d)], 0, d)
    both_ways(up_ids, down_ids, go)

    q_ids = jnp.concatenate([b.ids[1, j][0:1, :] for j in range(GROUP)], axis=1)
    peaks = b.peaks

    def key_ids(i):
        for j in range(GROUP):
            b.k_ids[(i * GROUP + j) * BLOCK : (i * GROUP + j + 1) * BLOCK, :] = column_of(
                b.ids[i, j][0:1, :]
            )

    def attend(i):
        key_ids(i)
        span = pl.ds(i * PLANE, PLANE)
        same = b.k_ids[span, 0:1] == q_ids
        for h in range(GROUP_HEADS):
            q = b.qp[...] * SCALE
            q = jnp.where(lane_head((PLANE, 256), 0) == h, q, jnp.zeros_like(q))
            score = lax.dot_general(b.kv[span, 0:256], q, NT, preferred_element_type=F32)
            score = jnp.where(same, score, NEGATIVE)
            peak = jnp.max(score, axis=0, keepdims=True)
            if i != 1:
                old = peaks[h][0:1, :]
                peak = jnp.maximum(peak, old)
                factor = jnp.exp(old - peak)
            weight = jnp.exp(score - peak)
            summed = jnp.sum(weight, axis=0, keepdims=True)
            first_lane, line = ((128, HEAD_DIM), (256, 0), (256, HEAD_DIM))[h]
            out = lax.dot_general(
                b.kv[span, first_lane : first_lane + 128],
                weight.astype(BF16),
                TN,
                preferred_element_type=F32,
            )[line : line + HEAD_DIM, :]
            if i != 1:
                out = out + b.out_t[h] * factor
                summed = summed + peaks[GROUP_HEADS + h][0:1, :] * factor
            b.out_t[h] = out
            peaks[h] = jnp.broadcast_to(peak, (8, PLANE))
            peaks[GROUP_HEADS + h] = jnp.broadcast_to(summed, (8, PLANE))

    relay_own(2)
    attend(1)
    relay_own(1)

    @pl.when(at.has_down)
    def _():
        came = b.kv.at[pl.ds(0, PLANE)]
        remote(came, came, s.halo_f, (0, 0), at.down).wait_recv()
        remote(b.ids.at[0], b.ids.at[0], s.halo_f, (0, 1), at.down).wait_recv()

    attend(0)

    @pl.when(at.has_up)
    def _():
        came = b.kv.at[pl.ds(2 * PLANE, PLANE)]
        remote(came, came, s.halo_f, (1, 0), at.up).wait_recv()
        remote(b.ids.at[2], b.ids.at[2], s.halo_f, (1, 1), at.up).wait_recv()

    attend(2)
    outs = [jnp.zeros((HEAD_DIM, PLANE), F32)]
    for h in range(GROUP_HEADS):
        summed = peaks[GROUP_HEADS + h][0:1, :]
        out = b.out_t[h] / summed
        b.out_t[h] = out
        b.stats[h] = peaks[h] + jnp.log(peaks[GROUP_HEADS + h])
        outs.append(out)
    attended = jnp.concatenate(outs, axis=0).T.astype(BF16)
    for i in range(GROUP):
        b.asend[i] = attended[i * BLOCK : (i + 1) * BLOCK, :]

    for d in (1, 2, 3):
        i = at.peer(d)
        start(remote(b.asend.at[i], b.arecv.at[at.r], s.a2a, (3, d), at.in_plane(i)))
    b.arecv[at.r] = b.asend[at.r]
    relay_own(3)
    relay_rest(1)
    relay_rest(2)
    for d in (1, 2, 3):
        from_peer(b.arecv.at[at.peer(d)], 3, d)
    b.att2[near_tokens, :] = jnp.concatenate(
        [b.arecv[g].astype(F32)[:, HEAD_DIM : HEAD_DIM + LANES] for g in range(GROUP)], axis=1
    ).astype(BF16)
    att_copy = remote(b.att2.at[near_tokens], b.att2.at[far_tokens], s.ex, 3, at.across)
    start(att_copy)
    start(dout_copy)
    sister_arrivals(1)
    relay_rest(3)
    own_copies[1].wait()
    tok_copy.wait_recv()
    att_copy.wait_recv()

    def normalise(hidden):
        center = hidden - jnp.mean(hidden, -1, keepdims=True)
        inverse = lax.rsqrt(jnp.mean(center * center, -1, keepdims=True) + EPSILON)
        return center * inverse, inverse

    def norm_back(upstream, unit, inverse, gain):
        scaled = upstream * gain
        return inverse * (
            scaled
            - jnp.mean(scaled, -1, keepdims=True)
            - unit * jnp.mean(scaled * unit, -1, keepdims=True)
        )

    def column_sum(value):
        return jnp.sum(value, axis=0, keepdims=True)

    first = (
        b.tok2[...].astype(F32)
        + jnp.dot(b.att2[...], b.wo[...], preferred_element_type=F32)
        + bias[2:3]
    )
    unit_one, inverse_one = normalise(first)
    b.unit_one[...] = unit_one
    normed = unit_one * bias[3:4] + bias[4:5]
    b.norm_low[...] = normed.astype(BF16)
    b.second[...] = normed + bias[9:10]
    relay_diagonal(3)
    for w in (2, 3):
        own_copies[w].wait()
        sister_arrivals(w)
    for c in range(4):
        cols = slice(c * MODEL, (c + 1) * MODEL)
        part = halves[c // 2]
        i = 5 + 2 * (c % 2)
        line = jnp.concatenate([part[i : i + 1], part[i + 1 : i + 2]], axis=1)
        inner = jnp.dot(b.norm_low[...], b.wi[:, cols], preferred_element_type=F32) + line
        gate = 0.5 * (1.0 + lax.erf(inner * ROOT_HALF))
        activation = (inner * gate).astype(BF16)
        b.act[:, cols] = activation
        b.slope[c * BOTH : (c + 1) * BOTH, :] = (
            gate + inner * jnp.exp(-0.5 * inner * inner) * INV_ROOT_TAU
        )
        b.second[...] += jnp.dot(activation, b.wb[cols, :], preferred_element_type=F32)
    unit_two, inverse_two = normalise(b.second[...])
    b.result[...] = (unit_two[:BLOCK] * bias[10:11] + bias[11:12]).astype(BF16)
    dout_copy.wait_recv()
    upstream = jnp.concatenate([b.d_out[0], b.dout_far[...]], axis=0).astype(F32)
    b.small[...] = jnp.zeros_like(b.small)
    b.small[10:11, :] = column_sum(upstream * unit_two)
    b.small[11:12, :] = column_sum(upstream)
    d_second = norm_back(upstream, unit_two, inverse_two, bias[10:11])
    b.small[9:10, :] = column_sum(d_second)
    b.d_second[...] = d_second.astype(BF16)
    b.second[...] = d_second

    chunks = [chunk_of(rows, planes) for rows in SET_ROWS]
    owners = [rows // chunk for rows, chunk in zip(SET_ROWS, chunks)]

    def of(name, group):
        return getattr(b, f"{name}{group}")

    def tile(group, t):
        if group == 0:
            lanes = pl.multiple_of(at.x * (TILES * HALF) + t * HALF, 128)
            left, right = b.act[:, pl.ds(lanes, HALF)], b.d_second[...]
        else:
            left = b.norm_low[:, pl.ds(near_rows, HALF)]
            right = b.d_inner[:, pl.ds(pl.multiple_of(t * MODEL, 128), MODEL)]
        return lax.dot_general(left, right, TN, preferred_element_type=F32)

    def out_quarter(t):
        return b.out_tile[pl.ds(pl.multiple_of(t * QUARTER, 16), QUARTER), :]

    def chunk_rows(group, j):
        return pl.ds(pl.multiple_of(j * chunks[group], 16), chunks[group])

    def own_chunk(group, j):
        if group == 2:
            return b.q_sum.at[chunk_rows(2, j)]
        first_row = OWN_ROWS[group] + j * chunks[group]
        return b.slope.at[pl.ds(pl.multiple_of(first_row, 16), chunks[group])]

    def core_copy(group, i):
        return remote(
            of("core_send", group).at[i],
            of("core_recv", group).at[i],
            s.core,
            group * 2 + i,
            at.sister,
        )

    def y_copy(group, j):
        lines = chunk_rows(group, j)
        return remote(
            of("y_send", group).at[lines],
            of("y_recv", group).at[lines],
            s.ys,
            (group, j),
            at.beside,
        )

    def up_copy(group, j):
        lines = chunk_rows(group, j)
        return remote(
            of("z_send", group).at[lines],
            of("up_recv", group).at[lines],
            s.up,
            (group, j),
            at.up,
        )

    def down_copy(group, j):
        lines = chunk_rows(group, j)
        return remote(
            of("z_send", group).at[lines],
            of("down_recv", group).at[lines],
            s.down,
            (group, j),
            at.down,
        )

    middle_step = planes // 2 + 1
    early, late = (1, middle_step), (middle_step, planes + 1)
    whole_way = (1, planes + 1)

    def each_owner(group, act, span):
        def one(d, carry):
            j = (at.p + d) % planes

            @pl.when(j < owners[group])
            def _():
                act(j)

            return carry

        lax.fori_loop(*span, one, 0)

    def make(group):
        base = OWN_ROWS[group]
        for i, t in enumerate((at.peer(3), at.peer(1))):
            of("core_send", group)[i, 0:HALF, :] = tile(group, t).astype(BF16)
            if group == 1:
                of("core_send", group)[i, HALF : HALF + QUARTER, :] = out_quarter(t).astype(BF16)
            start(core_copy(group, i))
        b.slope[base : base + HALF, :] = tile(group, at.r)
        if group == 1:
            b.slope[base + HALF : base + HALF + QUARTER, :] = out_quarter(at.r)

    def go_over_y(group, span):
        each_owner(group, lambda j: y_copy(group, j).start(), span)

    def exchange(group):
        base = OWN_ROWS[group]
        passing = tile(group, at.peer(2))
        core_copy(group, 0).wait_recv()
        come = of("core_recv", group)
        of("y_send", group)[0:HALF, :] = (passing + come[0, 0:HALF, :].astype(F32)).astype(BF16)
        if group == 1:
            lines = slice(HALF, HALF + QUARTER)
            b.y_send1[HALF + QUARTER :, :] = jnp.zeros((BLOCK - QUARTER, MODEL), BF16)
            of("y_send", group)[lines, :] = (
                out_quarter(at.peer(2)) + come[0, lines, :].astype(F32)
            ).astype(BF16)
        go_over_y(group, early)
        core_copy(group, 1).wait_recv()
        used = SET_ROWS[0] if group == 0 else HALF + QUARTER
        b.slope[base : base + used, :] += come[1, 0:used, :].astype(F32)

    def scatter(group, span):
        def act(j):
            mine = own_chunk(group, j)
            if group == 2:
                x_copy(j).wait_recv()
                came = b.x_recv[chunk_rows(2, j), :]
            else:
                y_copy(group, j).wait_recv()
                came = of("y_recv", group)[chunk_rows(group, j), :]
            total = mine[...] + came.astype(F32)
            mine[...] = total

            @pl.when(jnp.logical_and(at.p == 0, j > 0))
            def _():
                of("z_send", group)[chunk_rows(group, j), :] = total.astype(BF16)
                up_copy(group, j).start()

            @pl.when(jnp.logical_and(at.p == planes - 1, j < planes - 1))
            def _():
                of("z_send", group)[chunk_rows(group, j), :] = total.astype(BF16)
                down_copy(group, j).start()

        each_owner(group, act, span)

    def add_arrived(group, j, name, sems, device):
        lines = chunk_rows(group, j)
        came = of(name, group).at[lines]
        remote(came, came, sems, (group, j), device).wait_recv()
        return came[...].astype(F32)

    def relay_sums(group, h):
        @pl.when(at.p == h)
        def _():
            def one(i, carry):
                j = owners[group] - 1 - i
                total = own_chunk(group, j)[...] + add_arrived(
                    group, j, "up_recv", s.up, at.down
                )
                of("z_send", group)[chunk_rows(group, j), :] = total.astype(BF16)
                up_copy(group, j).start()
                return carry

            lax.fori_loop(0, owners[group] - 1 - at.p, one, 0)

        @pl.when(at.p == planes - 1 - h)
        def _():
            def one(j, carry):
                total = own_chunk(group, j)[...] + add_arrived(
                    group, j, "down_recv", s.down, at.up
                )
                of("z_send", group)[chunk_rows(group, j), :] = total.astype(BF16)
                down_copy(group, j).start()
                return carry

            lax.fori_loop(0, jnp.minimum(at.p, owners[group]), one, 0)

    def x_copy(j):
        lines = chunk_rows(2, j)
        return remote(b.x_send.at[lines], b.x_recv.at[lines], s.xs, j, at.across)

    def more_sums(group):
        def one(h, carry):
            relay_sums(group, h)
            return carry

        lax.fori_loop(3, planes - 1, one, 0)

    def place(group, t, j):
        first_row = t * SET_ROWS[group] + j * chunks[group]
        return of("sums", group).at[pl.ds(pl.multiple_of(first_row, 16), chunks[group])]

    def gather_copy(group, t, j, sems, device, source=None):
        piece = place(group, t, j)
        return remote(piece if source is None else source, piece, sems, (group, j), device)

    def spread(group, j, source=None):
        @pl.when(jnp.logical_and(j <= at.p, at.has_up))
        def _():
            gather_copy(group, at.r, j, s.gu, at.up, source).start()

        @pl.when(jnp.logical_and(j >= at.p, at.has_down))
        def _():
            gather_copy(group, at.r, j, s.gd, at.down, source).start()

        gather_copy(group, at.r, j, s.gy, at.beside, source).start()
        gather_copy(group, at.r, j, s.gc, at.sister, source).start()

    def settle_copy(group):
        return pltpu.make_async_copy(
            of("final", group), place(group, at.r, at.p), s.local[0].at[4 + group]
        )

    def settle(group):
        @pl.when(at.p < owners[group])
        def _():
            mine = own_chunk(group, at.p)

            @pl.when(at.has_down)
            def _():
                mine[...] += add_arrived(group, at.p, "up_recv", s.up, at.down)

            @pl.when(at.has_up)
            def _():
                mine[...] += add_arrived(group, at.p, "down_recv", s.down, at.up)

            total = mine[...]
            of("final", group)[...] = total.astype(BF16)
            spread(group, at.p, of("final", group))
            settle_copy(group).start()

    def around(group, d, act):
        @pl.when(jnp.logical_and(at.p - d >= 0, at.p - d < owners[group]))
        def _():
            act(at.p - d, s.gu, at.down)

        @pl.when(jnp.logical_and(d > 0, at.p + d < owners[group]))
        def _():
            act(at.p + d, s.gd, at.up)

    def come_in(group, d):
        def act(j, sems, device):
            gather_copy(group, at.r, j, sems, device).wait_recv()
            spread(group, j)

        around(group, d, act)

    def hand_over(group, d):
        def act(j, sems, device):
            gather_copy(group, at.peer(2), j, s.gy, at.beside).wait_recv()
            gather_copy(group, at.peer(2), j, s.gf, at.sister).start()

        around(group, d, act)

    def more_gathers():
        def one(d, carry):
            for group in range(3):
                come_in(group, d)
                hand_over(group, d)
            return carry

        lax.fori_loop(4, planes, one, 0)

    make(0)
    for c in range(4):
        if c == 2:
            exchange(0)
        cols = slice(c * MODEL, (c + 1) * MODEL)
        d_inner = (
            lax.dot_general(b.d_second[...], b.wb[cols, :], NT, preferred_element_type=F32)
            * b.slope[c * BOTH : (c + 1) * BOTH, :]
        )
        b.small[5 + c : 6 + c, :] = column_sum(d_inner)
        low = d_inner.astype(BF16)
        b.d_inner[:, cols] = low
        b.second[...] += lax.dot_general(low, b.wi[:, cols], NT, preferred_element_type=F32)
    d_normed = b.second[...]
    unit_one = b.unit_one[...]
    b.small[3:4, :] = column_sum(d_normed * unit_one)
    b.small[4:5, :] = column_sum(d_normed)
    d_first = norm_back(d_normed, unit_one, inverse_one, bias[3:4])
    b.small[2:3, :] = column_sum(d_first)
    d_first_low = d_first.astype(BF16)
    b.d_first[...] = d_first_low
    b.d_tokens[...] = d_first[:BLOCK]
    d_attn = lax.dot_general(d_first_low[:BLOCK], b.wo[...], NT, preferred_element_type=F32)
    for g in range(GROUP):
        b.dsend[g] = jnp.concatenate(
            [jnp.zeros((BLOCK, HEAD_DIM), F32), d_attn[:, g * LANES : (g + 1) * LANES]], axis=1
        ).astype(BF16)
    for d in (1, 2, 3):
        g = at.peer(d)
        start(
            remote(
                b.dsend.at[g], b.do.at[block_rows(0, at.r)], s.a2a, (4, d), at.in_plane(g)
            )
        )
    go_over_y(0, late)
    b.do[block_rows(0, at.r), :] = b.dsend[at.r]

    for j in range(3):
        start(late_across(j))
    b.out_tile[...] = lax.dot_general(
        b.att2[:, pl.ds(near_rows, HALF)], b.d_first[...], TN, preferred_element_type=F32
    )
    make(1)

    b.grads[...] = jnp.zeros_like(b.grads)
    b.dq[...] = jnp.zeros_like(b.dq)
    for d in (1, 2, 3):
        from_peer(b.do.at[block_rows(0, at.peer(d))], 4, d)
    do_t = b.do[...].astype(F32).T
    for h in range(GROUP_HEADS):
        lines = slice(HEAD_DIM * (h + 1), HEAD_DIM * (h + 2))
        b.stats[GROUP_HEADS + h] = jnp.broadcast_to(
            column_sum(do_t[lines, :] * b.out_t[h]), (8, PLANE)
        )

    def visit(h, i):
        span = pl.ds(i * PLANE, PLANE)
        pick_q = lane_head((PLANE, 256), 0) == h
        q = b.qp[...]
        q = jnp.where(pick_q, q, jnp.zeros_like(q))
        dout = b.do[...]
        dout = jnp.where(lane_head((PLANE, 256), 1) == h, dout, jnp.zeros_like(dout))
        keys = b.kv[span, 0:256]
        score = lax.dot_general(keys, q * SCALE, NT, preferred_element_type=F32)
        same = b.k_ids[span, 0:1] == q_ids
        prob = jnp.where(same, jnp.exp(score - b.stats[h][0:1, :]), 0.0)
        d_prob = lax.dot_general(b.kv[span, 128:384], dout, NT, preferred_element_type=F32)
        d_score = (prob * (d_prob - b.stats[GROUP_HEADS + h][0:1, :]) * SCALE).astype(BF16)
        b.grads[span, 0:256] += jnp.dot(d_score, q, preferred_element_type=F32)
        b.grads[span, 128:384] += jnp.dot(
            prob.astype(BF16), dout, preferred_element_type=F32
        )
        b.dq[...] += jnp.where(
            pick_q, lax.dot_general(d_score, keys, TN, preferred_element_type=F32), 0.0
        )

    def visit_plane(i):
        def one(h, carry):
            visit(h, i)
            return carry

        lax.fori_loop(0, GROUP_HEADS, one, 0)

    down_grads = remote(b.halo_send.at[0], b.halo.at[1], s.halo_b, 0, at.down)
    up_grads = remote(b.halo_send.at[1], b.halo.at[0], s.halo_b, 1, at.up)
    scatter(0, early)
    visit_plane(0)
    b.halo_send[0] = b.grads[pl.ds(0, PLANE), :].astype(BF16)

    @pl.when(at.has_down)
    def _():
        down_grads.start()

    exchange(1)
    visit_plane(2)
    b.halo_send[1] = b.grads[pl.ds(2 * PLANE, PLANE), :].astype(BF16)

    @pl.when(at.has_up)
    def _():
        up_grads.start()

    scatter(0, late)
    go_over_y(1, late)
    visit_plane(1)
    b.d_group[:, 0:256] = b.dq[...].astype(BF16)
    relay_sums(0, 1)

    @pl.when(at.has_up)
    def _():
        remote(b.halo.at[1], b.halo.at[1], s.halo_b, 0, at.up).wait_recv()
        b.grads[pl.ds(PLANE, PLANE), :] += b.halo[1].astype(F32)

    @pl.when(at.has_down)
    def _():
        remote(b.halo.at[0], b.halo.at[0], s.halo_b, 1, at.down).wait_recv()
        b.grads[pl.ds(PLANE, PLANE), :] += b.halo[0].astype(F32)

    b.d_group[:, 256:640] = b.grads[pl.ds(PLANE, PLANE), :].astype(BF16)

    b.line_send[...] = jnp.broadcast_to(column_sum(b.d_group[...].astype(F32)), (8, 640))
    line_copy = remote(b.line_send, b.line_recv, s.ex, 4, at.across)
    start(line_copy)
    b.x_send[...] = lax.dot_general(
        b.tok_plane[:, pl.ds(far_rows, HALF)], b.d_group[...], TN, preferred_element_type=F32
    ).astype(BF16)
    each_owner(2, lambda j: x_copy(j).start(), whole_way)
    for d in (1, 2, 3):
        i = at.peer(d)
        start(
            remote(
                b.d_group.at[block_rows(0, i)],
                b.d_recv.at[at.r],
                s.a2a,
                (5, d),
                at.in_plane(i),
            )
        )
    b.d_recv[at.r] = b.d_group[block_rows(0, at.r), :]
    b.q_sum[...] = lax.dot_general(
        b.tok_plane[:, pl.ds(near_rows, HALF)], b.d_group[...], TN, preferred_element_type=F32
    )
    partners = [at.sister, at.beside]
    span = 1
    while span < planes:
        partners.append((at.c + GROUP * span * (1 - 2 * ((at.p // span) % 2)), at.x))
        span *= 2

    def small_copy(i):
        return remote(b.small, b.small_recv.at[i], s.sm, i, partners[i])

    def small_finish(i):
        small_copy(i).wait()
        b.small[...] += b.small_recv[i]

    relay_sums(0, 2)
    scatter(1, early)
    more_sums(0)
    settle(0)
    line_copy.wait_recv()
    line = b.line_send[...] + b.line_recv[...]
    mine = lax.broadcasted_iota(jnp.int32, (8, 640), 0) == at.r
    b.small[16:24, 0:640] = jnp.where(mine, line, 0.0)
    small_copy(0).start()
    scatter(1, late)
    relay_sums(1, 1)
    small_finish(0)
    small_copy(1).start()
    come_in(0, 1)
    scatter(2, early)
    relay_sums(1, 2)
    hand_over(0, 0)
    scatter(2, late)
    relay_sums(2, 1)
    come_in(0, 2)
    more_sums(1)
    settle(1)
    relay_sums(2, 2)
    more_sums(2)
    small_finish(1)
    small_copy(2).start()
    for j in range(3):
        late_move(at.k, j, s.late_x, at.across).wait_recv()
        start(late_move(at.k, j, s.late_c, at.sister))
    hand_over(0, 1)
    come_in(0, 3)
    settle(2)
    come_in(1, 1)
    small_finish(2)
    small_copy(3).start()
    hand_over(0, 2)

    for d in (1, 2, 3):
        from_peer(b.d_recv.at[at.peer(d)], 5, d)
    for j, first_lane in enumerate((0, 256, 448)):
        b.d_packed[:, j * MODEL : (j + 1) * MODEL] = jnp.concatenate(
            [
                b.d_recv[g].astype(F32)[:, first_lane : first_lane + LANES]
                for g in range(GROUP)
            ],
            axis=1,
        ).astype(BF16)
    for j in range(3):
        late_move(1 - at.k, j, s.late_c, at.sister).wait_recv()
    b.d_tokens[...] += lax.dot_general(
        b.d_packed[...], b.wq[...], NT, preferred_element_type=F32
    )
    come_in(1, 2)
    come_in(2, 1)
    hand_over(0, 3)
    hand_over(1, 0)
    come_in(1, 3)
    come_in(2, 2)
    hand_over(2, 0)
    hand_over(1, 1)
    come_in(2, 3)
    small_finish(3)
    hand_over(2, 1)
    hand_over(1, 2)
    hand_over(2, 2)
    hand_over(1, 3)
    hand_over(2, 3)
    more_gathers()
    for i in range(4, len(partners)):
        small_copy(i).start()
        small_finish(i)

    for group in range(3):

        def last(j, carry, group=group):
            gather_copy(group, at.peer(1), j, s.gc, at.sister).wait_recv()
            gather_copy(group, at.peer(3), j, s.gf, at.sister).wait_recv()
            gather_copy(group, at.r, j, s.gy, at.beside).wait_send()
            gather_copy(group, at.r, j, s.gc, at.sister).wait_send()
            gather_copy(group, at.peer(2), j, s.gf, at.sister).wait_send()
            if group == 2:
                x_copy(j).wait_send()
            else:
                y_copy(group, j).wait_send()

            @pl.when(jnp.logical_and(j <= at.p, at.has_up))
            def _():
                gather_copy(group, at.r, j, s.gu, at.up).wait_send()

            @pl.when(jnp.logical_and(j >= at.p, at.has_down))
            def _():
                gather_copy(group, at.r, j, s.gd, at.down).wait_send()

            @pl.when(at.p < j)
            def _():
                up_copy(group, j).wait_send()

            @pl.when(at.p > j)
            def _():
                down_copy(group, j).wait_send()

            return carry

        lax.fori_loop(0, owners[group], last, 0)

        @pl.when(at.p < owners[group])
        def _(group=group):
            settle_copy(group).wait()

    for copy in sent:
        copy.wait_send()

    def finish(copy):
        copy.wait_send()

    both_ways(up_kv, down_kv, finish)
    both_ways(up_ids, down_ids, finish)
    both_ways(up_grads, down_grads, finish)


def layer_call(planes, args):
    buffers, semaphores = scratch_plan(planes)
    hbm = pl.BlockSpec(memory_space=pltpu.HBM)
    vmem = pl.BlockSpec(memory_space=pltpu.VMEM)
    weights = ("w_qkv", "w_out", "w_in", "w_back")
    scratch = [pltpu.VMEM(shape, kind) for shape, kind in buffers.values()]
    for shape in semaphores.values():
        scratch += [pltpu.SemaphoreType.DMA(shape)] * 2
    return pl.pallas_call(
        functools.partial(layer_kernel, planes, list(buffers), list(semaphores)),
        out_shape=[
            jax.ShapeDtypeStruct((BLOCK, MODEL), BF16),
            jax.ShapeDtypeStruct((BLOCK, MODEL), F32),
        ]
        + [
            jax.ShapeDtypeStruct((TILES * rows, width), BF16)
            for rows, width in zip(SET_ROWS, SET_WIDTH)
        ]
        + [jax.ShapeDtypeStruct((24, MODEL), F32)],
        in_specs=[hbm if name in weights else vmem for name in ARGS],
        out_specs=[vmem, vmem, hbm, hbm, hbm, vmem],
        scratch_shapes=scratch,
        compiler_params=pltpu.CompilerParams(
            collective_id=0, has_side_effects=True, vmem_limit_bytes=60 * 2**20
        ),
        name="layer",
    )(*args)


def unpack_kernel(result_in, tokens_in, sums0, sums1, sums2, small, *refs):
    result, d_tokens, w_qkv, bq, bv, w_out, bo, g1, o1, w_in, bi, w_back, bb, g2, o2 = refs[:15]
    in0, in1, in2, out_q, out_o, out_i, out_b, come, go = refs[15:]
    loads = []
    for g, (sums, held) in enumerate(((sums0, in0), (sums1, in1), (sums2, in2))):
        for t in range(TILES):
            lines = pl.ds(t * SET_ROWS[g], SET_ROWS[g])
            loads.append(
                pltpu.make_async_copy(sums.at[lines], held.at[t], come.at[g * TILES + t])
            )
    for load in loads:
        load.start()
    stores = [
        pltpu.make_async_copy(result_in, result, go.at[14]),
        pltpu.make_async_copy(tokens_in, d_tokens, go.at[15]),
    ]
    for store in stores:
        store.start()

    def put(source, target, i):
        store = pltpu.make_async_copy(source, target, go.at[i])
        store.start()
        stores.append(store)

    x = lax.axis_index("wsh")
    half = small[0:16, pl.ds(pl.multiple_of(x * HALF, 128), HALF)]
    for ref, row in zip((bo, g1, o1, bb, g2, o2), (2, 3, 4, 9, 10, 11)):
        ref[...] = half[row, :]
    whole = jnp.where(x == 0, small[5:7, :], small[7:9, :])
    bi[pl.ds(0, MODEL)] = whole[0, :]
    bi[pl.ds(MODEL, MODEL)] = whole[1, :]
    for ref, first in ((bq, 0), (bv, 448)):
        row = jnp.concatenate(
            [small[16 + g : 17 + g, first : first + LANES] for g in range(GROUP)], axis=1
        )
        ref[...] = jnp.where(x == 0, row[:, :HALF], row[:, HALF:])[0, :]

    for t in range(TILES):
        loads[t].wait()
        lines = pl.ds(t * HALF, HALF)
        out_b[lines, :] = in0[t].astype(F32)
        put(out_b.at[lines], w_back.at[lines], t)
    for t in range(TILES):
        loads[TILES + t].wait()
        out_i[t] = in1[t, 0:HALF, :].astype(F32)
        put(out_i.at[t], w_in.at[:, pl.ds(t * MODEL, MODEL)], 4 + t)
        lines = pl.ds(t * QUARTER, QUARTER)
        out_o[lines, :] = in1[t, HALF : HALF + QUARTER, :].astype(F32)
        put(out_o.at[lines], w_out.at[lines], 8 + t)
    for pair in range(2):
        loads[2 * TILES + 2 * pair].wait()
        loads[2 * TILES + 2 * pair + 1].wait()
        for j, first in enumerate((0, 256, 448)):
            out_q[:, j * MODEL + pair * HALF : j * MODEL + (pair + 1) * HALF] = (
                jnp.concatenate(
                    [
                        in2[2 * pair + i].astype(F32)[:, first : first + LANES]
                        for i in range(2)
                    ],
                    axis=1,
                )
            )
    put(out_q, w_qkv, 12)
    for store in stores:
        store.wait()


def unpack_call(*arrays):
    shape = jax.ShapeDtypeStruct
    vmem = pl.BlockSpec(memory_space=pltpu.VMEM)
    hbm = pl.BlockSpec(memory_space=pltpu.HBM)
    vector = (shape((HALF,), F32), vmem)
    outs = [
        (shape((BLOCK, MODEL), BF16), hbm),
        (shape((BLOCK, MODEL), F32), hbm),
        (shape((HALF, 3 * MODEL), F32), hbm),
        vector,
        vector,
        (shape((HALF, MODEL), F32), hbm),
        vector,
        vector,
        vector,
        (shape((HALF, FF), F32), hbm),
        (shape((FF // 2,), F32), vmem),
        (shape((FF // 2, MODEL), F32), hbm),
        vector,
        vector,
        vector,
    ]
    return pl.pallas_call(
        unpack_kernel,
        out_shape=[o[0] for o in outs],
        in_specs=[vmem, vmem, hbm, hbm, hbm, vmem],
        out_specs=[o[1] for o in outs],
        scratch_shapes=[
            pltpu.VMEM((TILES, rows, width), BF16)
            for rows, width in zip(SET_ROWS, SET_WIDTH)
        ]
        + [
            pltpu.VMEM((HALF, 3 * MODEL), F32),
            pltpu.VMEM((HALF, MODEL), F32),
            pltpu.VMEM((TILES, HALF, MODEL), F32),
            pltpu.VMEM((FF // 2, MODEL), F32),
            pltpu.SemaphoreType.DMA((3 * TILES,)),
            pltpu.SemaphoreType.DMA((16,)),
        ],
        compiler_params=pltpu.CompilerParams(vmem_limit_bytes=60 * 2**20),
        name="unpack",
    )(*arrays)


def body(*args):
    planes = lax.axis_size("ctx") // GROUP
    result, d_tokens, *rest = unpack_call(*layer_call(planes, args))
    return (result[None], d_tokens[None], *rest)


def solution(mesh):
    token_spec = P("wsh", "ctx", None)
    matrix, vector = P("wsh", None), P("wsh")
    in_specs = (
        token_spec,
        P("wsh", "ctx"),
        matrix,
        vector,
        vector,
        matrix,
        vector,
        vector,
        vector,
        matrix,
        vector,
        matrix,
        vector,
        vector,
        vector,
        token_spec,
    )
    out_specs = (
        token_spec,
        token_spec,
        matrix,
        vector,
        vector,
        matrix,
        vector,
        vector,
        vector,
        matrix,
        vector,
        matrix,
        vector,
        vector,
        vector,
    )
    return jax.shard_map(body, mesh=mesh, in_specs=in_specs, out_specs=out_specs, check_vma=False)
```

```python
import functools
import types

import jax
import jax.numpy as jnp
from jax import lax
from jax.experimental import pallas as pl
from jax.experimental.pallas import tpu as pltpu
from jax.sharding import PartitionSpec as P

HEAD_DIM = 64
GROUP = 4
GROUP_HEADS = 3
BLOCK = 128
PLANE = GROUP * BLOCK
MODEL = 768
FF = 3072
HALF = MODEL // 2
LANES = GROUP_HEADS * HEAD_DIM
TILES = 4
OWN_ROWS = (4 * 2 * BLOCK, 0)
BOTH = 2 * BLOCK
EPSILON = 1e-05
NEGATIVE = -1e30
ROOT_HALF = 0.7071067811865476
INV_ROOT_TAU = 0.3989422804014327
SCALE = HEAD_DIM**-0.5
MESH = pl.DeviceIdType.MESH
F32 = jnp.float32
BF16 = jnp.bfloat16
NT = (((1,), (1,)), ((), ()))
TN = (((0,), (0,)), ((), ()))


class Place:
    def __init__(self, planes):
        self.n = planes
        self.c = lax.axis_index("ctx")
        self.x = lax.axis_index("wsh")
        self.p = self.c // GROUP
        self.r = self.c % GROUP
        self.y = self.r // 2
        self.k = self.r % 2
        self.parity = self.p % 2
        self.sister = (self.c + 1 - 2 * self.k, self.x)
        self.beside = (self.c + 2 - 4 * self.y, self.x)
        self.across = (self.c, 1 - self.x)
        self.pair = (self.c + GROUP * (1 - 2 * self.parity), self.x)
        self.up = (self.c + GROUP, self.x)
        self.down = (self.c - GROUP, self.x)
        self.has_up = self.p < planes - 1
        self.has_down = self.p > 0

    def peer(self, d):
        if d == 1:
            return self.y * 2 + (1 - self.k)
        if d == 2:
            return (1 - self.y) * 2 + self.k
        return (1 - self.y) * 2 + (1 - self.k)

    def in_plane(self, position):
        return (self.p * GROUP + position, self.x)

    def plane(self, p):
        return (p * GROUP + self.r, self.x)


def signal(sem, device):
    pl.semaphore_signal(sem, inc=1, device_id=device, device_id_type=MESH)


def greet(at):
    barrier = pltpu.get_barrier_semaphore()
    for d in (1, 2, 3):
        signal(barrier, at.in_plane(at.peer(d)))
    signal(barrier, at.across)

    def other_plane(d, carry):
        signal(barrier, at.plane((at.p + d) % at.n))
        return carry

    lax.fori_loop(1, at.n, other_plane, 0)
    pl.semaphore_wait(barrier, 4 + at.n - 1)


def remote(src, dst, sems, index, device, recv_index=None):
    send, recv = sems
    return pltpu.make_async_remote_copy(
        src_ref=src,
        dst_ref=dst,
        send_sem=send.at[index],
        recv_sem=recv.at[index if recv_index is None else recv_index],
        device_id=device,
        device_id_type=MESH,
    )


def lane_head(shape, first):
    return lax.broadcasted_iota(jnp.int32, shape, 1) // HEAD_DIM - first


def column_of(row):
    return jnp.broadcast_to(row, (BLOCK, BLOCK)).T


def chunk_of(rows, planes):
    chunk = -(-(-(-rows // planes)) // 16) * 16
    while rows % chunk:
        chunk += 16
    return chunk


SET_ROWS = (HALF, 512, HALF)
SET_WIDTH = (MODEL, MODEL, 640)
QUARTER = HALF // GROUP


def scratch_plan(planes):
    steps = planes.bit_length() - 1
    buffers = dict(
        wq=((MODEL, 3 * MODEL), BF16),
        wo=((MODEL, MODEL), BF16),
        wi=((MODEL, FF), BF16),
        wb=((FF, MODEL), BF16),
        bias_own=((16, HALF), BF16),
        bias2=((2, 16, HALF), BF16),
        dout_far=((BLOCK, MODEL), BF16),
        ids=((3, GROUP, 8, BLOCK), F32),
        acc=((PLANE, 3 * 256), F32),
        qp=((PLANE, 256), BF16),
        kv=((3 * PLANE, 2 * LANES), BF16),
        out_t=((GROUP_HEADS, HEAD_DIM, PLANE), F32),
        peaks=((2 * GROUP_HEADS, 8, PLANE), F32),
        asend=((GROUP, BLOCK, 256), BF16),
        arecv=((GROUP, BLOCK, 256), BF16),
        tok_plane=((PLANE, MODEL), BF16),
        tok2=((BOTH, MODEL), BF16),
        att2=((BOTH, MODEL), BF16),
        unit_one=((BOTH, MODEL), F32),
        norm_low=((BOTH, MODEL), BF16),
        act=((BOTH, FF), BF16),
        d_inner=((BOTH, FF), BF16),
        d_second=((BOTH, MODEL), BF16),
        d_first=((BOTH, MODEL), BF16),
        second=((BOTH, MODEL), F32),
        slope=((4 * BOTH + HALF, MODEL), F32),
        out_tile=((HALF, MODEL), F32),
        dsend=((GROUP, BLOCK, 256), BF16),
        do=((PLANE, 256), BF16),
        grads=((3 * PLANE, 2 * LANES), F32),
        dq=((PLANE, 256), F32),
        k_ids=((3 * PLANE, BLOCK), F32),
        stats=((2 * GROUP_HEADS, 8, PLANE), F32),
        halo_send=((2, PLANE, 2 * LANES), BF16),
        halo=((2, PLANE, 2 * LANES), BF16),
        d_group=((PLANE, 640), BF16),
        d_recv=((GROUP, BLOCK, 640), BF16),
        d_packed=((BLOCK, 3 * MODEL), BF16),
        q_sum=((HALF, 640), F32),
        x_send=((HALF, 640), BF16),
        x_recv=((HALF, 640), BF16),
        small_recv=((2 + steps, 24, MODEL), F32),
        line_send=((8, 640), F32),
        line_recv=((8, 640), F32),
    )
    for g, (rows, width) in enumerate(zip(SET_ROWS, SET_WIDTH)):
        chunk = chunk_of(rows, planes)
        if g < 2:
            buffers[f"core_send{g}"] = ((2, rows, width), BF16)
            buffers[f"core_recv{g}"] = ((2, rows, width), BF16)
            buffers[f"y_send{g}"] = ((rows, width), BF16)
            buffers[f"y_recv{g}"] = ((rows, width), BF16)
        buffers[f"z_send{g}"] = ((rows, width), BF16)
        buffers[f"up_recv{g}"] = ((rows, width), BF16)
        buffers[f"down_recv{g}"] = ((rows, width), BF16)
        buffers[f"final{g}"] = ((chunk, width), BF16)
    semaphores = dict(
        local=(4 + 3,),
        qx=(3,),
        qz=(3,),
        qc=(2, 3),
        late_x=(3,),
        late_c=(3,),
        wx=(4, 2),
        wy=(4, 2),
        wz=(4, 2),
        wc=(4, 5),
        ex=(5,),
        tp=(4,),
        a2a=(6, 4),
        halo_f=(2, 5),
        halo_b=(2,),
        core=(4,),
        xs=(planes,),
        ys=(2, planes),
        up=(3, planes),
        down=(3, planes),
        gu=(3, planes),
        gd=(3, planes),
        gy=(3, planes),
        gc=(3, planes),
        gf=(3, planes),
        sm=(2 + steps,),
    )
    return buffers, semaphores


ARGS = ["tokens", "doc_ids", "w_qkv", "b_query", "b_value", "w_out", "b_out", "ln1_gain"]
ARGS += ["ln1_bias", "w_in", "b_in", "w_back", "b_back", "ln2_gain", "ln2_bias", "d_out"]
RESULTS = ["result", "d_tokens", "sums0", "sums1", "sums2", "small"]


def layer_kernel(planes, names, sem_names, *refs):
    split = len(ARGS) + len(RESULTS) + len(names)
    b = types.SimpleNamespace(**dict(zip(ARGS + RESULTS + names, refs[:split])))
    pairs = refs[split:]
    s = types.SimpleNamespace(
        **{n: (pairs[2 * i], pairs[2 * i + 1]) for i, n in enumerate(sem_names)}
    )
    at = Place(planes)
    sent = []

    def start(copy):
        copy.start()
        sent.append(copy)

    def block_rows(first, i):
        return pl.ds(pl.multiple_of(first + i * BLOCK, BLOCK), BLOCK)

    b.ids[1, at.r] = jnp.broadcast_to(b.doc_ids[...].astype(F32), (8, BLOCK))
    b.tok_plane[block_rows(0, at.r), :] = b.tokens[0]

    @pl.when(jnp.logical_not(at.has_down))
    def _():
        b.kv[pl.ds(0, PLANE), :] = jnp.zeros((PLANE, 2 * LANES), BF16)
        b.ids[0] = jnp.full((GROUP, 8, BLOCK), -1.0, F32)

    @pl.when(jnp.logical_not(at.has_up))
    def _():
        b.kv[pl.ds(2 * PLANE, PLANE), :] = jnp.zeros((PLANE, 2 * LANES), BF16)
        b.ids[2] = jnp.full((GROUP, 8, BLOCK), -1.0, F32)

    vectors = [b.b_query, b.b_value, b.b_out, b.ln1_gain, b.ln1_bias]
    lines = [v[...].astype(F32).reshape(1, HALF) for v in vectors]
    lines += [
        b.b_in[pl.ds(i * HALF, HALF)].astype(F32).reshape(1, HALF) for i in range(4)
    ]
    lines += [
        v[...].astype(F32).reshape(1, HALF) for v in (b.b_back, b.ln2_gain, b.ln2_bias)
    ]
    lines.append(jnp.zeros((4, HALF), F32))
    packed_bias = jnp.concatenate(lines, axis=0).astype(BF16)
    b.bias_own[...] = packed_bias
    b.bias2[at.x] = packed_bias
    greet(at)

    shards = (b.w_qkv, b.w_out, b.w_in, b.w_back)
    wholes = (b.wq, b.wo, b.wi, b.wb)
    direct = (True, True, True, False)
    own_q = at.y * 2 + at.parity
    diag_q = (1 - at.y) * 2 + (1 - at.parity)
    beside_q = (1 - at.y) * 2 + at.parity
    pair_q = at.y * 2 + (1 - at.parity)

    def rows(w, quarter, core):
        eighth = shards[w].shape[0] // 8
        return pl.multiple_of((quarter * 2 + core) * eighth, 16), eighth

    def far(w, quarter, core, part=None):
        first, size = rows(w, quarter, core)
        base = (1 - at.x) * shards[w].shape[0]
        lines = pl.ds(pl.multiple_of(base + first, 16), size)
        if part is None:
            return wholes[w].at[lines]
        width = shards[w].shape[1] // 2
        return wholes[w].at[lines, pl.ds(part * width, width)]

    def across_copy(w, i):
        first, size = rows(w, (own_q, diag_q)[i], at.k)
        base = at.x * shards[w].shape[0]
        return remote(
            shards[w].at[pl.ds(first, size)],
            wholes[w].at[pl.ds(pl.multiple_of(base + first, 16), size)],
            s.wx,
            (w, i),
            at.across,
        )

    def piece_copy(w, quarter, sems, index, device, part=None, core=None):
        piece = far(w, quarter, at.k if core is None else core, part)
        return remote(piece, piece, sems, (w, index), device)

    def relay_own(w):
        piece_copy(w, own_q, s.wx, 0, at.across).wait_recv()
        start(piece_copy(w, own_q, s.wy, 0, at.beside))
        start(piece_copy(w, own_q, s.wz, 0, at.pair))
        start(piece_copy(w, own_q, s.wc, 0, at.sister))

    def relay_rest(w):
        if direct[w]:
            piece_copy(w, diag_q, s.wx, 1, at.across).wait_recv()
            start(piece_copy(w, diag_q, s.wc, 1, at.sister))
        piece_copy(w, beside_q, s.wy, 0, at.beside).wait_recv()
        if not direct[w]:
            start(piece_copy(w, beside_q, s.wz, 1, at.pair, part=1))
        start(piece_copy(w, beside_q, s.wc, 2, at.sister))
        piece_copy(w, pair_q, s.wz, 0, at.pair).wait_recv()
        if not direct[w]:
            start(piece_copy(w, pair_q, s.wy, 1, at.beside, part=0))
        start(piece_copy(w, pair_q, s.wc, 3, at.sister))

    def relay_diagonal(w):
        piece_copy(w, diag_q, s.wy, 1, at.beside, part=0).wait_recv()
        start(piece_copy(w, diag_q, s.wc, 1, at.sister, part=0))
        piece_copy(w, diag_q, s.wz, 1, at.pair, part=1).wait_recv()
        start(piece_copy(w, diag_q, s.wc, 4, at.sister, part=1))

    def sister_arrivals(w):
        other = 1 - at.k
        piece_copy(w, own_q, s.wc, 0, at.sister, core=other).wait_recv()
        piece_copy(w, beside_q, s.wc, 2, at.sister, core=other).wait_recv()
        piece_copy(w, pair_q, s.wc, 3, at.sister, core=other).wait_recv()
        if direct[w]:
            piece_copy(w, diag_q, s.wc, 1, at.sister, core=other).wait_recv()
        else:
            piece_copy(w, diag_q, s.wc, 1, at.sister, part=0, core=other).wait_recv()
            piece_copy(w, diag_q, s.wc, 4, at.sister, part=1, core=other).wait_recv()

    near_tokens = pl.ds(0, BLOCK)
    far_tokens = pl.ds(BLOCK, BLOCK)
    bias_copy = remote(b.bias_own, b.bias2.at[at.x], s.ex, 0, at.across)
    tok_copy = remote(b.tokens.at[0], b.tok2.at[far_tokens], s.ex, 1, at.across)
    dout_copy = remote(b.d_out.at[0], b.dout_far, s.ex, 2, at.across)
    def q_piece(ref, first_row, size, j, side):
        return ref.at[
            pl.ds(pl.multiple_of(first_row, 16), size),
            pl.ds(pl.multiple_of(j * MODEL + side * HALF, 128), HALF),
        ]

    def q_rows(core, parity):
        return (core * 2 + parity) * QUARTER

    far_base = (1 - at.x) * HALF
    near_base = at.x * HALF

    def q_across(j):
        line = q_rows(at.k, at.parity)
        return remote(
            q_piece(b.w_qkv, line, QUARTER, j, at.y),
            q_piece(b.wq, near_base + line, QUARTER, j, at.y),
            s.qx,
            j,
            at.across,
        )

    def q_move(core, parity, j, sems, index, device):
        piece = q_piece(b.wq, far_base + q_rows(core, parity), QUARTER, j, at.y)
        return remote(piece, piece, sems, index, device)

    def late_across(j):
        line = at.k * 2 * QUARTER
        return remote(
            q_piece(b.w_qkv, line, 2 * QUARTER, j, 1 - at.y),
            q_piece(b.wq, near_base + line, 2 * QUARTER, j, 1 - at.y),
            s.late_x,
            j,
            at.across,
        )

    def late_move(core, j, sems, device):
        piece = q_piece(b.wq, far_base + core * 2 * QUARTER, 2 * QUARTER, j, 1 - at.y)
        return remote(piece, piece, sems, j, device)

    def tok_block(i, sem, device):
        piece = b.tok_plane.at[block_rows(0, i)]
        return remote(piece, piece, s.tp, sem, device)

    own_copies = []
    for w in range(4):
        size = shards[w].shape[0]
        own_copies.append(
            pltpu.make_async_copy(
                shards[w],
                wholes[w].at[pl.ds(pl.multiple_of(at.x * size, 16), size)],
                s.local[0].at[w],
            )
        )
    for j in range(3):
        start(q_across(j))
    start(bias_copy)
    start(tok_block(at.r, 0, at.beside))
    start(tok_block(at.r, 1, at.sister))
    own_copies[0].start()
    for d in (1, 2, 3):
        mine = b.ids.at[1, at.r]
        start(remote(mine, mine, s.a2a, (0, d), at.in_plane(at.peer(d))))

    near_rows = pl.multiple_of(at.x * HALF, HALF)
    far_rows = pl.multiple_of((1 - at.x) * HALF, HALF)
    b.tok2[near_tokens, :] = b.tokens[0]
    for j in range(3):
        q_move(at.k, at.parity, j, s.qx, j, at.across).wait_recv()
        start(q_move(at.k, at.parity, j, s.qz, j, at.pair))
        start(q_move(at.k, at.parity, j, s.qc, (0, j), at.sister))
    start(across_copy(2, 0))
    for i in range(2):
        start(across_copy(1, i))
    start(across_copy(3, 0))
    start(across_copy(2, 1))
    start(tok_copy)
    for w in (1, 2, 3):
        own_copies[w].start()
    tok_block(at.peer(2), 0, at.beside).wait_recv()
    start(tok_block(at.peer(2), 2, at.sister))
    for j in range(3):
        q_move(at.k, 1 - at.parity, j, s.qz, j, at.pair).wait_recv()
        start(q_move(at.k, 1 - at.parity, j, s.qc, (1, j), at.sister))
    tok_block(at.peer(1), 1, at.sister).wait_recv()
    tok_block(at.peer(3), 2, at.sister).wait_recv()
    own_copies[0].wait()
    window = [
        pl.ds(pl.multiple_of(j * MODEL + at.y * HALF + at.k * 128, 128), 256) for j in range(3)
    ]
    for j in range(3):
        b.acc[:, j * 256 : (j + 1) * 256] = jnp.dot(
            b.tok_plane[:, pl.ds(near_rows, HALF)],
            b.wq[pl.ds(near_rows, HALF), window[j]],
            preferred_element_type=F32,
        )
    remote(b.bias_own, b.bias2.at[1 - at.x], s.ex, 0, at.across).wait_recv()
    halves = (b.bias2[0].astype(F32), b.bias2[1].astype(F32))
    bias = jnp.concatenate(halves, axis=1)

    def group_bias(row):
        line = bias[row : row + 1, 0:LANES]
        for g in range(1, GROUP):
            line = jnp.where(at.r == g, bias[row : row + 1, g * LANES : (g + 1) * LANES], line)
        return line

    for j in range(3):
        q_move(1 - at.k, at.parity, j, s.qc, (0, j), at.sister).wait_recv()
        q_move(1 - at.k, 1 - at.parity, j, s.qc, (1, j), at.sister).wait_recv()
    made = []
    for j in range(3):
        part = b.acc[:, j * 256 : (j + 1) * 256] + jnp.dot(
            b.tok_plane[:, pl.ds(far_rows, HALF)],
            b.wq[pl.ds(far_rows, HALF), window[j]],
            preferred_element_type=F32,
        )
        made.append(jnp.where(at.k == 0, part[:, 0:LANES], part[:, HEAD_DIM:256]))
    b.kv[pl.ds(PLANE, PLANE), :] = jnp.concatenate(
        [made[1], made[2] + group_bias(1)], axis=1
    ).astype(BF16)

    def both_ways(up, down, act):
        @pl.when(at.has_up)
        def _():
            act(up)

        @pl.when(at.has_down)
        def _():
            act(down)

    def go(copy):
        copy.start()

    middle = b.kv.at[pl.ds(PLANE, PLANE)]
    up_kv = remote(middle, b.kv.at[pl.ds(0, PLANE)], s.halo_f, (0, 0), at.up)
    down_kv = remote(middle, b.kv.at[pl.ds(2 * PLANE, PLANE)], s.halo_f, (1, 0), at.down)
    up_ids = remote(b.ids.at[1], b.ids.at[0], s.halo_f, (0, 1), at.up)
    down_ids = remote(b.ids.at[1], b.ids.at[2], s.halo_f, (1, 1), at.down)

    def from_peer(piece, kind, d):
        remote(piece, piece, s.a2a, (kind, d), at.in_plane(at.peer(d))).wait_recv()

    both_ways(up_kv, down_kv, go)
    b.qp[...] = jnp.concatenate(
        [made[0] + group_bias(0), jnp.zeros((PLANE, HEAD_DIM), F32)], axis=1
    ).astype(BF16)
    for d in (1, 2, 3):
        from_peer(b.ids.at[1, at.peer(d)], 0, d)
    both_ways(up_ids, down_ids, go)

    q_ids = jnp.concatenate([b.ids[1, j][0:1, :] for j in range(GROUP)], axis=1)
    peaks = b.peaks

    def key_ids(i):
        for j in range(GROUP):
            b.k_ids[(i * GROUP + j) * BLOCK : (i * GROUP + j + 1) * BLOCK, :] = column_of(
                b.ids[i, j][0:1, :]
            )

    def attend(i):
        key_ids(i)
        span = pl.ds(i * PLANE, PLANE)
        same = b.k_ids[span, 0:1] == q_ids
        for h in range(GROUP_HEADS):
            q = b.qp[...] * SCALE
            q = jnp.where(lane_head((PLANE, 256), 0) == h, q, jnp.zeros_like(q))
            score = lax.dot_general(b.kv[span, 0:256], q, NT, preferred_element_type=F32)
            score = jnp.where(same, score, NEGATIVE)
            peak = jnp.max(score, axis=0, keepdims=True)
            if i != 1:
                old = peaks[h][0:1, :]
                peak = jnp.maximum(peak, old)
                factor = jnp.exp(old - peak)
            weight = jnp.exp(score - peak)
            summed = jnp.sum(weight, axis=0, keepdims=True)
            first_lane, line = ((128, HEAD_DIM), (256, 0), (256, HEAD_DIM))[h]
            out = lax.dot_general(
                b.kv[span, first_lane : first_lane + 128],
                weight.astype(BF16),
                TN,
                preferred_element_type=F32,
            )[line : line + HEAD_DIM, :]
            if i != 1:
                out = out + b.out_t[h] * factor
                summed = summed + peaks[GROUP_HEADS + h][0:1, :] * factor
            b.out_t[h] = out
            peaks[h] = jnp.broadcast_to(peak, (8, PLANE))
            peaks[GROUP_HEADS + h] = jnp.broadcast_to(summed, (8, PLANE))

    relay_own(2)
    attend(1)
    relay_own(1)

    @pl.when(at.has_down)
    def _():
        came = b.kv.at[pl.ds(0, PLANE)]
        remote(came, came, s.halo_f, (0, 0), at.down).wait_recv()
        remote(b.ids.at[0], b.ids.at[0], s.halo_f, (0, 1), at.down).wait_recv()

    attend(0)

    @pl.when(at.has_up)
    def _():
        came = b.kv.at[pl.ds(2 * PLANE, PLANE)]
        remote(came, came, s.halo_f, (1, 0), at.up).wait_recv()
        remote(b.ids.at[2], b.ids.at[2], s.halo_f, (1, 1), at.up).wait_recv()

    attend(2)
    outs = [jnp.zeros((HEAD_DIM, PLANE), F32)]
    for h in range(GROUP_HEADS):
        summed = peaks[GROUP_HEADS + h][0:1, :]
        out = b.out_t[h] / summed
        b.out_t[h] = out
        b.stats[h] = peaks[h] + jnp.log(peaks[GROUP_HEADS + h])
        outs.append(out)
    attended = jnp.concatenate(outs, axis=0).T.astype(BF16)
    for i in range(GROUP):
        b.asend[i] = attended[i * BLOCK : (i + 1) * BLOCK, :]

    for d in (1, 2, 3):
        i = at.peer(d)
        start(remote(b.asend.at[i], b.arecv.at[at.r], s.a2a, (3, d), at.in_plane(i)))
    b.arecv[at.r] = b.asend[at.r]
    relay_own(3)
    relay_rest(1)
    relay_rest(2)
    for d in (1, 2, 3):
        from_peer(b.arecv.at[at.peer(d)], 3, d)
    b.att2[near_tokens, :] = jnp.concatenate(
        [b.arecv[g].astype(F32)[:, HEAD_DIM : HEAD_DIM + LANES] for g in range(GROUP)], axis=1
    ).astype(BF16)
    att_copy = remote(b.att2.at[near_tokens], b.att2.at[far_tokens], s.ex, 3, at.across)
    start(att_copy)
    start(dout_copy)
    for w in (1, 2):
        own_copies[w].wait()
        sister_arrivals(w)

    def normalise(hidden):
        center = hidden - jnp.mean(hidden, -1, keepdims=True)
        inverse = lax.rsqrt(jnp.mean(center * center, -1, keepdims=True) + EPSILON)
        return center * inverse, inverse

    def norm_back(upstream, unit, inverse, gain):
        scaled = upstream * gain
        return inverse * (
            scaled
            - jnp.mean(scaled, -1, keepdims=True)
            - unit * jnp.mean(scaled * unit, -1, keepdims=True)
        )

    def column_sum(value):
        return jnp.sum(value, axis=0, keepdims=True)

    def dense_forward(side):
        lines = (near_tokens, far_tokens)[side]
        first = (
            b.tok2[lines, :].astype(F32)
            + jnp.dot(b.att2[lines, :], b.wo[...], preferred_element_type=F32)
            + bias[2:3]
        )
        unit, inverse = normalise(first)
        b.unit_one[lines, :] = unit
        normed = unit * bias[3:4] + bias[4:5]
        b.norm_low[lines, :] = normed.astype(BF16)
        b.second[lines, :] = normed + bias[9:10]
        for c in range(4):
            if side == 1 and c == 2:
                relay_diagonal(3)
            cols = slice(c * MODEL, (c + 1) * MODEL)
            part = halves[c // 2]
            i = 5 + 2 * (c % 2)
            line = jnp.concatenate([part[i : i + 1], part[i + 1 : i + 2]], axis=1)
            inner = line + jnp.dot(
                b.norm_low[lines, :], b.wi[:, cols], preferred_element_type=F32
            )
            gate = 0.5 * (1.0 + lax.erf(inner * ROOT_HALF))
            b.act[lines, cols] = (inner * gate).astype(BF16)
            b.slope[pl.ds(c * BOTH + side * BLOCK, BLOCK), :] = (
                gate + inner * jnp.exp(-0.5 * inner * inner) * INV_ROOT_TAU
            )
        return inverse

    near_inverse = dense_forward(0)
    relay_rest(3)
    tok_copy.wait_recv()
    att_copy.wait_recv()
    inverse_one = jnp.concatenate([near_inverse, dense_forward(1)], axis=0)
    own_copies[3].wait()
    sister_arrivals(3)
    b.second[...] += jnp.dot(b.act[...], b.wb[...], preferred_element_type=F32)
    unit_two, inverse_two = normalise(b.second[...])
    b.result[...] = (unit_two[:BLOCK] * bias[10:11] + bias[11:12]).astype(BF16)
    dout_copy.wait_recv()
    upstream = jnp.concatenate([b.d_out[0], b.dout_far[...]], axis=0).astype(F32)
    b.small[...] = jnp.zeros_like(b.small)
    b.small[10:11, :] = column_sum(upstream * unit_two)
    b.small[11:12, :] = column_sum(upstream)
    d_second = norm_back(upstream, unit_two, inverse_two, bias[10:11])
    b.small[9:10, :] = column_sum(d_second)
    b.d_second[...] = d_second.astype(BF16)
    b.second[...] = d_second

    chunks = [chunk_of(rows, planes) for rows in SET_ROWS]
    owners = [rows // chunk for rows, chunk in zip(SET_ROWS, chunks)]

    def of(name, group):
        return getattr(b, f"{name}{group}")

    def tile(group, t):
        if group == 0:
            lanes = pl.multiple_of(at.x * (TILES * HALF) + t * HALF, 128)
            left, right = b.act[:, pl.ds(lanes, HALF)], b.d_second[...]
        else:
            left = b.norm_low[:, pl.ds(near_rows, HALF)]
            right = b.d_inner[:, pl.ds(pl.multiple_of(t * MODEL, 128), MODEL)]
        return lax.dot_general(left, right, TN, preferred_element_type=F32)

    def out_quarter(t):
        return b.out_tile[pl.ds(pl.multiple_of(t * QUARTER, 16), QUARTER), :]

    def chunk_rows(group, j):
        return pl.ds(pl.multiple_of(j * chunks[group], 16), chunks[group])

    def own_chunk(group, j):
        if group == 2:
            return b.q_sum.at[chunk_rows(2, j)]
        first_row = OWN_ROWS[group] + j * chunks[group]
        return b.slope.at[pl.ds(pl.multiple_of(first_row, 16), chunks[group])]

    def core_copy(group, i):
        return remote(
            of("core_send", group).at[i],
            of("core_recv", group).at[i],
            s.core,
            group * 2 + i,
            at.sister,
        )

    def y_copy(group, j):
        lines = chunk_rows(group, j)
        return remote(
            of("y_send", group).at[lines],
            of("y_recv", group).at[lines],
            s.ys,
            (group, j),
            at.beside,
        )

    def up_copy(group, j):
        lines = chunk_rows(group, j)
        return remote(
            of("z_send", group).at[lines],
            of("up_recv", group).at[lines],
            s.up,
            (group, j),
            at.up,
        )

    def down_copy(group, j):
        lines = chunk_rows(group, j)
        return remote(
            of("z_send", group).at[lines],
            of("down_recv", group).at[lines],
            s.down,
            (group, j),
            at.down,
        )

    middle_step = planes // 2 + 1
    early, late = (1, middle_step), (middle_step, planes + 1)
    whole_way = (1, planes + 1)

    def each_owner(group, act, span):
        def one(d, carry):
            j = jnp.where(at.p < planes // 2, planes - d, d - 1)

            @pl.when(j < owners[group])
            def _():
                act(j)

            return carry

        lax.fori_loop(*span, one, 0)

    def make(group):
        base = OWN_ROWS[group]
        for i, t in enumerate((at.peer(3), at.peer(1))):
            of("core_send", group)[i, 0:HALF, :] = tile(group, t).astype(BF16)
            if group == 1:
                of("core_send", group)[i, HALF : HALF + QUARTER, :] = out_quarter(t).astype(BF16)
            start(core_copy(group, i))
        b.slope[base : base + HALF, :] = tile(group, at.r)
        if group == 1:
            b.slope[base + HALF : base + HALF + QUARTER, :] = out_quarter(at.r)

    def go_over_y(group, span):
        each_owner(group, lambda j: y_copy(group, j).start(), span)

    def exchange(group):
        base = OWN_ROWS[group]
        passing = tile(group, at.peer(2))
        core_copy(group, 0).wait_recv()
        come = of("core_recv", group)
        of("y_send", group)[0:HALF, :] = (passing + come[0, 0:HALF, :].astype(F32)).astype(BF16)
        if group == 1:
            lines = slice(HALF, HALF + QUARTER)
            b.y_send1[HALF + QUARTER :, :] = jnp.zeros((BLOCK - QUARTER, MODEL), BF16)
            of("y_send", group)[lines, :] = (
                out_quarter(at.peer(2)) + come[0, lines, :].astype(F32)
            ).astype(BF16)
        go_over_y(group, (1, 2) if group == 0 else early)
        core_copy(group, 1).wait_recv()
        used = SET_ROWS[0] if group == 0 else HALF + QUARTER
        b.slope[base : base + used, :] += come[1, 0:used, :].astype(F32)

    def scatter(group, span):
        def act(j):
            mine = own_chunk(group, j)
            if group == 2:
                x_copy(j).wait_recv()
                came = b.x_recv[chunk_rows(2, j), :]
            else:
                y_copy(group, j).wait_recv()
                came = of("y_recv", group)[chunk_rows(group, j), :]
            total = mine[...] + came.astype(F32)
            mine[...] = total

            @pl.when(jnp.logical_and(at.p == 0, j > 0))
            def _():
                of("z_send", group)[chunk_rows(group, j), :] = total.astype(BF16)
                up_copy(group, j).start()

            @pl.when(jnp.logical_and(at.p == planes - 1, j < planes - 1))
            def _():
                of("z_send", group)[chunk_rows(group, j), :] = total.astype(BF16)
                down_copy(group, j).start()

        each_owner(group, act, span)

    def add_arrived(group, j, name, sems, device):
        lines = chunk_rows(group, j)
        came = of(name, group).at[lines]
        remote(came, came, sems, (group, j), device).wait_recv()
        return came[...].astype(F32)

    def relay_sums(group, h):
        @pl.when(at.p == h)
        def _():
            def one(i, carry):
                j = owners[group] - 1 - i
                total = own_chunk(group, j)[...] + add_arrived(
                    group, j, "up_recv", s.up, at.down
                )
                of("z_send", group)[chunk_rows(group, j), :] = total.astype(BF16)
                up_copy(group, j).start()
                return carry

            lax.fori_loop(0, owners[group] - 1 - at.p, one, 0)

        @pl.when(at.p == planes - 1 - h)
        def _():
            def one(j, carry):
                total = own_chunk(group, j)[...] + add_arrived(
                    group, j, "down_recv", s.down, at.up
                )
                of("z_send", group)[chunk_rows(group, j), :] = total.astype(BF16)
                down_copy(group, j).start()
                return carry

            lax.fori_loop(0, jnp.minimum(at.p, owners[group]), one, 0)

    def x_copy(j):
        lines = chunk_rows(2, j)
        return remote(b.x_send.at[lines], b.x_recv.at[lines], s.xs, j, at.across)

    def more_sums(group):
        def one(h, carry):
            relay_sums(group, h)
            return carry

        lax.fori_loop(3, planes - 1, one, 0)

    def place(group, t, j):
        first_row = t * SET_ROWS[group] + j * chunks[group]
        return of("sums", group).at[pl.ds(pl.multiple_of(first_row, 16), chunks[group])]

    def gather_copy(group, t, j, sems, device, source=None):
        piece = place(group, t, j)
        return remote(piece if source is None else source, piece, sems, (group, j), device)

    def spread(group, j, source=None):
        @pl.when(jnp.logical_and(j <= at.p, at.has_up))
        def _():
            gather_copy(group, at.r, j, s.gu, at.up, source).start()

        @pl.when(jnp.logical_and(j >= at.p, at.has_down))
        def _():
            gather_copy(group, at.r, j, s.gd, at.down, source).start()

        gather_copy(group, at.r, j, s.gy, at.beside, source).start()
        gather_copy(group, at.r, j, s.gc, at.sister, source).start()

    def settle_copy(group):
        return pltpu.make_async_copy(
            of("final", group), place(group, at.r, at.p), s.local[0].at[4 + group]
        )

    def settle(group):
        @pl.when(at.p < owners[group])
        def _():
            mine = own_chunk(group, at.p)

            @pl.when(at.has_down)
            def _():
                mine[...] += add_arrived(group, at.p, "up_recv", s.up, at.down)

            @pl.when(at.has_up)
            def _():
                mine[...] += add_arrived(group, at.p, "down_recv", s.down, at.up)

            total = mine[...]
            of("final", group)[...] = total.astype(BF16)
            spread(group, at.p, of("final", group))
            settle_copy(group).start()

    def around(group, d, act):
        @pl.when(jnp.logical_and(at.p - d >= 0, at.p - d < owners[group]))
        def _():
            act(at.p - d, s.gu, at.down)

        @pl.when(jnp.logical_and(d > 0, at.p + d < owners[group]))
        def _():
            act(at.p + d, s.gd, at.up)

    def come_in(group, d):
        def act(j, sems, device):
            gather_copy(group, at.r, j, sems, device).wait_recv()
            spread(group, j)

        around(group, d, act)

    def hand_over(group, d):
        def act(j, sems, device):
            gather_copy(group, at.peer(2), j, s.gy, at.beside).wait_recv()
            gather_copy(group, at.peer(2), j, s.gf, at.sister).start()

        around(group, d, act)

    def more_gathers():
        def one(d, carry):
            for group in range(3):
                come_in(group, d)
                hand_over(group, d)
            return carry

        lax.fori_loop(4, planes, one, 0)

    make(0)
    for c in range(4):
        if c == 2:
            exchange(0)
        cols = slice(c * MODEL, (c + 1) * MODEL)
        d_inner = (
            lax.dot_general(b.d_second[...], b.wb[cols, :], NT, preferred_element_type=F32)
            * b.slope[c * BOTH : (c + 1) * BOTH, :]
        )
        b.small[5 + c : 6 + c, :] = column_sum(d_inner)
        low = d_inner.astype(BF16)
        b.d_inner[:, cols] = low
        b.second[...] += lax.dot_general(low, b.wi[:, cols], NT, preferred_element_type=F32)
    d_normed = b.second[...]
    unit_one = b.unit_one[...]
    b.small[3:4, :] = column_sum(d_normed * unit_one)
    b.small[4:5, :] = column_sum(d_normed)
    d_first = norm_back(d_normed, unit_one, inverse_one, bias[3:4])
    b.small[2:3, :] = column_sum(d_first)
    d_first_low = d_first.astype(BF16)
    b.d_first[...] = d_first_low
    b.d_tokens[...] = d_first[:BLOCK]
    d_attn = lax.dot_general(d_first_low[:BLOCK], b.wo[...], NT, preferred_element_type=F32)
    for g in range(GROUP):
        b.dsend[g] = jnp.concatenate(
            [jnp.zeros((BLOCK, HEAD_DIM), F32), d_attn[:, g * LANES : (g + 1) * LANES]], axis=1
        ).astype(BF16)
    for d in (1, 2, 3):
        g = at.peer(d)
        start(
            remote(
                b.dsend.at[g], b.do.at[block_rows(0, at.r)], s.a2a, (4, d), at.in_plane(g)
            )
        )
    go_over_y(0, (2, planes + 1))
    b.do[block_rows(0, at.r), :] = b.dsend[at.r]

    for j in range(3):
        start(late_across(j))
    b.out_tile[...] = lax.dot_general(
        b.att2[:, pl.ds(near_rows, HALF)], b.d_first[...], TN, preferred_element_type=F32
    )
    make(1)
    scatter(0, (1, 2))

    b.grads[...] = jnp.zeros_like(b.grads)
    b.dq[...] = jnp.zeros_like(b.dq)
    for d in (1, 2, 3):
        from_peer(b.do.at[block_rows(0, at.peer(d))], 4, d)
    do_t = b.do[...].astype(F32).T
    for h in range(GROUP_HEADS):
        lines = slice(HEAD_DIM * (h + 1), HEAD_DIM * (h + 2))
        b.stats[GROUP_HEADS + h] = jnp.broadcast_to(
            column_sum(do_t[lines, :] * b.out_t[h]), (8, PLANE)
        )

    def visit(h, i):
        span = pl.ds(i * PLANE, PLANE)
        pick_q = lane_head((PLANE, 256), 0) == h
        q = b.qp[...]
        q = jnp.where(pick_q, q, jnp.zeros_like(q))
        dout = b.do[...]
        dout = jnp.where(lane_head((PLANE, 256), 1) == h, dout, jnp.zeros_like(dout))
        keys = b.kv[span, 0:256]
        score = lax.dot_general(keys, q * SCALE, NT, preferred_element_type=F32)
        same = b.k_ids[span, 0:1] == q_ids
        prob = jnp.where(same, jnp.exp(score - b.stats[h][0:1, :]), 0.0)
        d_prob = lax.dot_general(b.kv[span, 128:384], dout, NT, preferred_element_type=F32)
        d_score = (prob * (d_prob - b.stats[GROUP_HEADS + h][0:1, :]) * SCALE).astype(BF16)
        b.grads[span, 0:256] += jnp.dot(d_score, q, preferred_element_type=F32)
        b.grads[span, 128:384] += jnp.dot(
            prob.astype(BF16), dout, preferred_element_type=F32
        )
        b.dq[...] += jnp.where(
            pick_q, lax.dot_general(d_score, keys, TN, preferred_element_type=F32), 0.0
        )

    def visit_plane(i):
        def one(h, carry):
            visit(h, i)
            return carry

        lax.fori_loop(0, GROUP_HEADS, one, 0)

    down_grads = remote(b.halo_send.at[0], b.halo.at[1], s.halo_b, 0, at.down)
    up_grads = remote(b.halo_send.at[1], b.halo.at[0], s.halo_b, 1, at.up)
    visit_plane(0)
    b.halo_send[0] = b.grads[pl.ds(0, PLANE), :].astype(BF16)

    @pl.when(at.has_down)
    def _():
        down_grads.start()

    scatter(0, (2, 3))
    exchange(1)
    visit_plane(2)
    b.halo_send[1] = b.grads[pl.ds(2 * PLANE, PLANE), :].astype(BF16)

    @pl.when(at.has_up)
    def _():
        up_grads.start()

    go_over_y(1, late)
    scatter(0, (3, planes + 1))
    relay_sums(0, 1)
    visit_plane(1)
    b.d_group[:, 0:256] = b.dq[...].astype(BF16)

    @pl.when(at.has_up)
    def _():
        remote(b.halo.at[1], b.halo.at[1], s.halo_b, 0, at.up).wait_recv()
        b.grads[pl.ds(PLANE, PLANE), :] += b.halo[1].astype(F32)

    relay_sums(0, 2)
    scatter(1, early)

    @pl.when(at.has_down)
    def _():
        remote(b.halo.at[0], b.halo.at[0], s.halo_b, 1, at.down).wait_recv()
        b.grads[pl.ds(PLANE, PLANE), :] += b.halo[0].astype(F32)

    b.d_group[:, 256:640] = b.grads[pl.ds(PLANE, PLANE), :].astype(BF16)

    b.line_send[...] = jnp.broadcast_to(column_sum(b.d_group[...].astype(F32)), (8, 640))
    line_copy = remote(b.line_send, b.line_recv, s.ex, 4, at.across)
    start(line_copy)
    b.x_send[...] = lax.dot_general(
        b.tok_plane[:, pl.ds(far_rows, HALF)], b.d_group[...], TN, preferred_element_type=F32
    ).astype(BF16)
    each_owner(2, lambda j: x_copy(j).start(), whole_way)
    for d in (1, 2, 3):
        i = at.peer(d)
        start(
            remote(
                b.d_group.at[block_rows(0, i)],
                b.d_recv.at[at.r],
                s.a2a,
                (5, d),
                at.in_plane(i),
            )
        )
    b.d_recv[at.r] = b.d_group[block_rows(0, at.r), :]
    b.q_sum[...] = lax.dot_general(
        b.tok_plane[:, pl.ds(near_rows, HALF)], b.d_group[...], TN, preferred_element_type=F32
    )
    partners = [at.sister, at.beside]
    span = 1
    while span < planes:
        partners.append((at.c + GROUP * span * (1 - 2 * ((at.p // span) % 2)), at.x))
        span *= 2

    def small_copy(i):
        return remote(b.small, b.small_recv.at[i], s.sm, i, partners[i])

    def small_finish(i):
        small_copy(i).wait()
        b.small[...] += b.small_recv[i]

    more_sums(0)
    settle(0)
    line_copy.wait_recv()
    line = b.line_send[...] + b.line_recv[...]
    mine = lax.broadcasted_iota(jnp.int32, (8, 640), 0) == at.r
    b.small[16:24, 0:640] = jnp.where(mine, line, 0.0)
    small_copy(0).start()
    small_finish(0)
    small_copy(1).start()
    scatter(1, late)
    relay_sums(1, 1)
    come_in(0, 1)
    scatter(2, early)
    relay_sums(1, 2)
    hand_over(0, 0)
    scatter(2, late)
    relay_sums(2, 1)
    come_in(0, 2)
    more_sums(1)
    settle(1)
    relay_sums(2, 2)
    more_sums(2)
    small_finish(1)
    small_copy(2).start()
    for j in range(3):
        late_move(at.k, j, s.late_x, at.across).wait_recv()
        start(late_move(at.k, j, s.late_c, at.sister))
    hand_over(0, 1)
    come_in(0, 3)
    settle(2)
    come_in(1, 1)
    small_finish(2)
    small_copy(3).start()
    hand_over(0, 2)

    for d in (1, 2, 3):
        from_peer(b.d_recv.at[at.peer(d)], 5, d)
    for j, first_lane in enumerate((0, 256, 448)):
        b.d_packed[:, j * MODEL : (j + 1) * MODEL] = jnp.concatenate(
            [
                b.d_recv[g].astype(F32)[:, first_lane : first_lane + LANES]
                for g in range(GROUP)
            ],
            axis=1,
        ).astype(BF16)
    for j in range(3):
        late_move(1 - at.k, j, s.late_c, at.sister).wait_recv()
    b.d_tokens[...] += lax.dot_general(
        b.d_packed[...], b.wq[...], NT, preferred_element_type=F32
    )
    come_in(1, 2)
    come_in(2, 1)
    hand_over(0, 3)
    hand_over(1, 0)
    come_in(1, 3)
    come_in(2, 2)
    hand_over(2, 0)
    hand_over(1, 1)
    come_in(2, 3)
    small_finish(3)
    hand_over(2, 1)
    hand_over(1, 2)
    hand_over(2, 2)
    hand_over(1, 3)
    hand_over(2, 3)
    more_gathers()
    for i in range(4, len(partners)):
        small_copy(i).start()
        small_finish(i)

    for group in range(3):

        def last(j, carry, group=group):
            gather_copy(group, at.peer(1), j, s.gc, at.sister).wait_recv()
            gather_copy(group, at.peer(3), j, s.gf, at.sister).wait_recv()
            gather_copy(group, at.r, j, s.gy, at.beside).wait_send()
            gather_copy(group, at.r, j, s.gc, at.sister).wait_send()
            gather_copy(group, at.peer(2), j, s.gf, at.sister).wait_send()
            if group == 2:
                x_copy(j).wait_send()
            else:
                y_copy(group, j).wait_send()

            @pl.when(jnp.logical_and(j <= at.p, at.has_up))
            def _():
                gather_copy(group, at.r, j, s.gu, at.up).wait_send()

            @pl.when(jnp.logical_and(j >= at.p, at.has_down))
            def _():
                gather_copy(group, at.r, j, s.gd, at.down).wait_send()

            @pl.when(at.p < j)
            def _():
                up_copy(group, j).wait_send()

            @pl.when(at.p > j)
            def _():
                down_copy(group, j).wait_send()

            return carry

        lax.fori_loop(0, owners[group], last, 0)

        @pl.when(at.p < owners[group])
        def _(group=group):
            settle_copy(group).wait()

    for copy in sent:
        copy.wait_send()

    def finish(copy):
        copy.wait_send()

    both_ways(up_kv, down_kv, finish)
    both_ways(up_ids, down_ids, finish)
    both_ways(up_grads, down_grads, finish)


def layer_call(planes, args):
    buffers, semaphores = scratch_plan(planes)
    hbm = pl.BlockSpec(memory_space=pltpu.HBM)
    vmem = pl.BlockSpec(memory_space=pltpu.VMEM)
    weights = ("w_qkv", "w_out", "w_in", "w_back")
    scratch = [pltpu.VMEM(shape, kind) for shape, kind in buffers.values()]
    for shape in semaphores.values():
        scratch += [pltpu.SemaphoreType.DMA(shape)] * 2
    return pl.pallas_call(
        functools.partial(layer_kernel, planes, list(buffers), list(semaphores)),
        out_shape=[
            jax.ShapeDtypeStruct((BLOCK, MODEL), BF16),
            jax.ShapeDtypeStruct((BLOCK, MODEL), F32),
        ]
        + [
            jax.ShapeDtypeStruct((TILES * rows, width), BF16)
            for rows, width in zip(SET_ROWS, SET_WIDTH)
        ]
        + [jax.ShapeDtypeStruct((24, MODEL), F32)],
        in_specs=[hbm if name in weights else vmem for name in ARGS],
        out_specs=[vmem, vmem, hbm, hbm, hbm, vmem],
        scratch_shapes=scratch,
        compiler_params=pltpu.CompilerParams(
            collective_id=0, has_side_effects=True, vmem_limit_bytes=60 * 2**20
        ),
        name="layer",
    )(*args)


def unpack_kernel(result_in, tokens_in, sums0, sums1, sums2, small, *refs):
    result, d_tokens, w_qkv, bq, bv, w_out, bo, g1, o1, w_in, bi, w_back, bb, g2, o2 = refs[:15]
    in0, in1, in2, out_q, out_o, out_i, out_b, come, go = refs[15:]
    loads = []
    for g, (sums, held) in enumerate(((sums0, in0), (sums1, in1), (sums2, in2))):
        for t in range(TILES):
            lines = pl.ds(t * SET_ROWS[g], SET_ROWS[g])
            loads.append(
                pltpu.make_async_copy(sums.at[lines], held.at[t], come.at[g * TILES + t])
            )
    for load in loads:
        load.start()
    stores = [
        pltpu.make_async_copy(result_in, result, go.at[14]),
        pltpu.make_async_copy(tokens_in, d_tokens, go.at[15]),
    ]
    for store in stores:
        store.start()

    def put(source, target, i):
        store = pltpu.make_async_copy(source, target, go.at[i])
        store.start()
        stores.append(store)

    x = lax.axis_index("wsh")
    half = small[0:16, pl.ds(pl.multiple_of(x * HALF, 128), HALF)]
    for ref, row in zip((bo, g1, o1, bb, g2, o2), (2, 3, 4, 9, 10, 11)):
        ref[...] = half[row, :]
    whole = jnp.where(x == 0, small[5:7, :], small[7:9, :])
    bi[pl.ds(0, MODEL)] = whole[0, :]
    bi[pl.ds(MODEL, MODEL)] = whole[1, :]
    for ref, first in ((bq, 0), (bv, 448)):
        row = jnp.concatenate(
            [small[16 + g : 17 + g, first : first + LANES] for g in range(GROUP)], axis=1
        )
        ref[...] = jnp.where(x == 0, row[:, :HALF], row[:, HALF:])[0, :]

    for t in range(TILES):
        loads[t].wait()
        lines = pl.ds(t * HALF, HALF)
        out_b[lines, :] = in0[t].astype(F32)
        put(out_b.at[lines], w_back.at[lines], t)
    for t in range(TILES):
        loads[TILES + t].wait()
        out_i[t] = in1[t, 0:HALF, :].astype(F32)
        put(out_i.at[t], w_in.at[:, pl.ds(t * MODEL, MODEL)], 4 + t)
        lines = pl.ds(t * QUARTER, QUARTER)
        out_o[lines, :] = in1[t, HALF : HALF + QUARTER, :].astype(F32)
        put(out_o.at[lines], w_out.at[lines], 8 + t)
    for pair in range(2):
        loads[2 * TILES + 2 * pair].wait()
        loads[2 * TILES + 2 * pair + 1].wait()
        for j, first in enumerate((0, 256, 448)):
            out_q[:, j * MODEL + pair * HALF : j * MODEL + (pair + 1) * HALF] = (
                jnp.concatenate(
                    [
                        in2[2 * pair + i].astype(F32)[:, first : first + LANES]
                        for i in range(2)
                    ],
                    axis=1,
                )
            )
    put(out_q, w_qkv, 12)
    for store in stores:
        store.wait()


def unpack_call(*arrays):
    shape = jax.ShapeDtypeStruct
    vmem = pl.BlockSpec(memory_space=pltpu.VMEM)
    hbm = pl.BlockSpec(memory_space=pltpu.HBM)
    vector = (shape((HALF,), F32), vmem)
    outs = [
        (shape((BLOCK, MODEL), BF16), hbm),
        (shape((BLOCK, MODEL), F32), hbm),
        (shape((HALF, 3 * MODEL), F32), hbm),
        vector,
        vector,
        (shape((HALF, MODEL), F32), hbm),
        vector,
        vector,
        vector,
        (shape((HALF, FF), F32), hbm),
        (shape((FF // 2,), F32), vmem),
        (shape((FF // 2, MODEL), F32), hbm),
        vector,
        vector,
        vector,
    ]
    return pl.pallas_call(
        unpack_kernel,
        out_shape=[o[0] for o in outs],
        in_specs=[vmem, vmem, hbm, hbm, hbm, vmem],
        out_specs=[o[1] for o in outs],
        scratch_shapes=[
            pltpu.VMEM((TILES, rows, width), BF16)
            for rows, width in zip(SET_ROWS, SET_WIDTH)
        ]
        + [
            pltpu.VMEM((HALF, 3 * MODEL), F32),
            pltpu.VMEM((HALF, MODEL), F32),
            pltpu.VMEM((TILES, HALF, MODEL), F32),
            pltpu.VMEM((FF // 2, MODEL), F32),
            pltpu.SemaphoreType.DMA((3 * TILES,)),
            pltpu.SemaphoreType.DMA((16,)),
        ],
        compiler_params=pltpu.CompilerParams(vmem_limit_bytes=60 * 2**20),
        name="unpack",
    )(*arrays)


def body(*args):
    planes = lax.axis_size("ctx") // GROUP
    result, d_tokens, *rest = unpack_call(*layer_call(planes, args))
    return (result[None], d_tokens[None], *rest)


def solution(mesh):
    token_spec = P("wsh", "ctx", None)
    matrix, vector = P("wsh", None), P("wsh")
    in_specs = (
        token_spec,
        P("wsh", "ctx"),
        matrix,
        vector,
        vector,
        matrix,
        vector,
        vector,
        vector,
        matrix,
        vector,
        matrix,
        vector,
        vector,
        vector,
        token_spec,
    )
    out_specs = (
        token_spec,
        token_spec,
        matrix,
        vector,
        vector,
        matrix,
        vector,
        vector,
        vector,
        matrix,
        vector,
        matrix,
        vector,
        vector,
        vector,
    )
    return jax.shard_map(body, mesh=mesh, in_specs=in_specs, out_specs=out_specs, check_vma=False)
```

```python
import functools
import types

import jax
import jax.numpy as jnp
from jax import lax
from jax.experimental import pallas as pl
from jax.experimental.pallas import tpu as pltpu
from jax.sharding import PartitionSpec as P

HEAD_DIM = 64
GROUP = 4
GROUP_HEADS = 3
BLOCK = 128
PLANE = GROUP * BLOCK
MODEL = 768
FF = 3072
HALF = MODEL // 2
LANES = GROUP_HEADS * HEAD_DIM
TILES = 4
OWN_ROWS = (4 * 2 * BLOCK, 0)
BOTH = 2 * BLOCK
EPSILON = 1e-05
NEGATIVE = -1e30
ROOT_HALF = 0.7071067811865476
INV_ROOT_TAU = 0.3989422804014327
SCALE = HEAD_DIM**-0.5
MESH = pl.DeviceIdType.MESH
F32 = jnp.float32
BF16 = jnp.bfloat16
NT = (((1,), (1,)), ((), ()))
TN = (((0,), (0,)), ((), ()))


class Place:
    def __init__(self, planes):
        self.n = planes
        self.c = lax.axis_index("ctx")
        self.x = lax.axis_index("wsh")
        self.p = self.c // GROUP
        self.r = self.c % GROUP
        self.y = self.r // 2
        self.k = self.r % 2
        self.parity = self.p % 2
        self.sister = (self.c + 1 - 2 * self.k, self.x)
        self.beside = (self.c + 2 - 4 * self.y, self.x)
        self.across = (self.c, 1 - self.x)
        self.pair = (self.c + GROUP * (1 - 2 * self.parity), self.x)
        self.up = (self.c + GROUP, self.x)
        self.down = (self.c - GROUP, self.x)
        self.has_up = self.p < planes - 1
        self.has_down = self.p > 0

    def peer(self, d):
        if d == 1:
            return self.y * 2 + (1 - self.k)
        if d == 2:
            return (1 - self.y) * 2 + self.k
        return (1 - self.y) * 2 + (1 - self.k)

    def in_plane(self, position):
        return (self.p * GROUP + position, self.x)

    def plane(self, p):
        return (p * GROUP + self.r, self.x)


def signal(sem, device):
    pl.semaphore_signal(sem, inc=1, device_id=device, device_id_type=MESH)


def greet(at):
    barrier = pltpu.get_barrier_semaphore()
    for d in (1, 2, 3):
        signal(barrier, at.in_plane(at.peer(d)))
    signal(barrier, at.across)

    def other_plane(d, carry):
        signal(barrier, at.plane((at.p + d) % at.n))
        return carry

    lax.fori_loop(1, at.n, other_plane, 0)
    pl.semaphore_wait(barrier, 4 + at.n - 1)


def remote(src, dst, sems, index, device, recv_index=None):
    send, recv = sems
    return pltpu.make_async_remote_copy(
        src_ref=src,
        dst_ref=dst,
        send_sem=send.at[index],
        recv_sem=recv.at[index if recv_index is None else recv_index],
        device_id=device,
        device_id_type=MESH,
    )


def lane_head(shape, first):
    return lax.broadcasted_iota(jnp.int32, shape, 1) // HEAD_DIM - first


def column_of(row):
    return jnp.broadcast_to(row, (BLOCK, BLOCK)).T


def chunk_of(rows, planes):
    chunk = -(-(-(-rows // planes)) // 16) * 16
    while rows % chunk:
        chunk += 16
    return chunk


SET_ROWS = (HALF, 512, HALF)
SET_WIDTH = (MODEL, MODEL, 640)
QUARTER = HALF // GROUP


def scratch_plan(planes):
    steps = planes.bit_length() - 1
    buffers = dict(
        wq=((MODEL, 3 * MODEL), BF16),
        wo=((MODEL, MODEL), BF16),
        wi=((MODEL, FF), BF16),
        wb=((FF, MODEL), BF16),
        bias_own=((16, HALF), BF16),
        bias2=((2, 16, HALF), BF16),
        dout_far=((BLOCK, MODEL), BF16),
        ids=((3, GROUP, 8, BLOCK), F32),
        acc=((PLANE, 3 * 256), F32),
        qp=((PLANE, 256), BF16),
        kv=((3 * PLANE, 2 * LANES), BF16),
        out_t=((GROUP_HEADS, HEAD_DIM, PLANE), F32),
        peaks=((2 * GROUP_HEADS, 8, PLANE), F32),
        asend=((GROUP, BLOCK, 256), BF16),
        arecv=((GROUP, BLOCK, 256), BF16),
        tok_plane=((PLANE, MODEL), BF16),
        tok2=((BOTH, MODEL), BF16),
        att2=((BOTH, MODEL), BF16),
        unit_one=((BOTH, MODEL), F32),
        norm_low=((BOTH, MODEL), BF16),
        act=((BOTH, FF), BF16),
        d_inner=((BOTH, FF), BF16),
        d_second=((BOTH, MODEL), BF16),
        d_first=((BOTH, MODEL), BF16),
        second=((BOTH, MODEL), F32),
        slope=((4 * BOTH + HALF, MODEL), F32),
        out_tile=((HALF, MODEL), F32),
        dsend=((GROUP, BLOCK, 256), BF16),
        do=((PLANE, 256), BF16),
        grads=((3 * PLANE, 2 * LANES), F32),
        dq=((PLANE, 256), F32),
        k_ids=((3 * PLANE, BLOCK), F32),
        stats=((2 * GROUP_HEADS, 8, PLANE), F32),
        halo_send=((2, PLANE, 2 * LANES), BF16),
        halo=((2, PLANE, 2 * LANES), BF16),
        d_group=((PLANE, 640), BF16),
        dt_send=((3, BLOCK, MODEL), BF16),
        dt_recv=((3, BLOCK, MODEL), BF16),
        q_sum=((HALF, 640), F32),
        x_send=((HALF, 640), BF16),
        x_recv=((HALF, 640), BF16),
        small_recv=((2 + steps, 24, MODEL), F32),
        line_send=((8, 640), F32),
        line_recv=((8, 640), F32),
    )
    for g, (rows, width) in enumerate(zip(SET_ROWS, SET_WIDTH)):
        chunk = chunk_of(rows, planes)
        if g < 2:
            buffers[f"core_send{g}"] = ((2, rows, width), BF16)
            buffers[f"core_recv{g}"] = ((2, rows, width), BF16)
            buffers[f"y_send{g}"] = ((rows, width), BF16)
            buffers[f"y_recv{g}"] = ((rows, width), BF16)
        buffers[f"z_send{g}"] = ((rows, width), BF16)
        buffers[f"up_recv{g}"] = ((rows, width), BF16)
        buffers[f"down_recv{g}"] = ((rows, width), BF16)
        buffers[f"final{g}"] = ((chunk, width), BF16)
    semaphores = dict(
        local=(4,),
        qx=(3,),
        qz=(3,),
        qc=(2, 3),
        dt=(3,),
        wx=(5,),
        wy=(4,),
        wz=(4,),
        wc=(13,),
        ex=(5,),
        tp=(3,),
        a2a=(3, 3),
        halo_f=(2, 2),
        halo_b=(2,),
        core=(4,),
        xs=(planes,),
        ys=(2, planes),
        up=(3, planes),
        down=(3, planes),
        gu=(3, planes),
        gd=(3, planes),
        gy=(3, planes),
        gc=(3, planes),
        gf=(3, planes),
        sm=(2 + steps,),
    )
    return buffers, semaphores


ARGS = ["tokens", "doc_ids", "w_qkv", "b_query", "b_value", "w_out", "b_out", "ln1_gain"]
ARGS += ["ln1_bias", "w_in", "b_in", "w_back", "b_back", "ln2_gain", "ln2_bias", "d_out"]
RESULTS = ["result", "d_tokens", "sums0", "sums1", "sums2", "small"]


def layer_kernel(planes, names, sem_names, *refs):
    split = len(ARGS) + len(RESULTS) + len(names)
    b = types.SimpleNamespace(**dict(zip(ARGS + RESULTS + names, refs[:split])))
    pairs = refs[split:]
    s = types.SimpleNamespace(
        **{n: (pairs[2 * i], pairs[2 * i + 1]) for i, n in enumerate(sem_names)}
    )
    at = Place(planes)
    sent = []

    def start(copy):
        copy.start()
        sent.append(copy)

    def block_rows(first, i):
        return pl.ds(pl.multiple_of(first + i * BLOCK, BLOCK), BLOCK)

    b.ids[1, at.r] = jnp.broadcast_to(b.doc_ids[...].astype(F32), (8, BLOCK))
    b.tok_plane[block_rows(0, at.r), :] = b.tokens[0]

    @pl.when(jnp.logical_not(at.has_down))
    def _():
        b.kv[pl.ds(0, PLANE), :] = jnp.zeros((PLANE, 2 * LANES), BF16)
        b.ids[0] = jnp.full((GROUP, 8, BLOCK), -1.0, F32)

    @pl.when(jnp.logical_not(at.has_up))
    def _():
        b.kv[pl.ds(2 * PLANE, PLANE), :] = jnp.zeros((PLANE, 2 * LANES), BF16)
        b.ids[2] = jnp.full((GROUP, 8, BLOCK), -1.0, F32)

    vectors = [b.b_query, b.b_value, b.b_out, b.ln1_gain, b.ln1_bias]
    lines = [v[...].astype(F32).reshape(1, HALF) for v in vectors]
    lines += [
        b.b_in[pl.ds(i * HALF, HALF)].astype(F32).reshape(1, HALF) for i in range(4)
    ]
    lines += [
        v[...].astype(F32).reshape(1, HALF) for v in (b.b_back, b.ln2_gain, b.ln2_bias)
    ]
    lines.append(jnp.zeros((4, HALF), F32))
    packed_bias = jnp.concatenate(lines, axis=0).astype(BF16)
    b.bias_own[...] = packed_bias
    b.bias2[at.x] = packed_bias
    greet(at)

    shards = (b.w_qkv, b.w_out, b.w_in, b.w_back)
    wholes = (b.wq, b.wo, b.wi, b.wb)
    direct = (True, True, True, False)
    own_q = at.y * 2 + at.parity
    diag_q = (1 - at.y) * 2 + (1 - at.parity)
    beside_q = (1 - at.y) * 2 + at.parity
    pair_q = at.y * 2 + (1 - at.parity)

    def rows(w, quarter, core):
        eighth = shards[w].shape[0] // 8
        return pl.multiple_of((quarter * 2 + core) * eighth, 16), eighth

    def far(w, quarter, core, part=None):
        first, size = rows(w, quarter, core)
        base = (1 - at.x) * shards[w].shape[0]
        lines = pl.ds(pl.multiple_of(base + first, 16), size)
        if part is None:
            return wholes[w].at[lines]
        width = shards[w].shape[1] // 2
        return wholes[w].at[lines, pl.ds(part * width, width)]

    def across_copy(w, i):
        first, size = rows(w, (own_q, diag_q)[i], at.k)
        base = at.x * shards[w].shape[0]
        return remote(
            shards[w].at[pl.ds(first, size)],
            wholes[w].at[pl.ds(pl.multiple_of(base + first, 16), size)],
            s.wx,
            2 * (w - 1) + i,
            at.across,
        )

    def piece_copy(w, quarter, sems, index, device, part=None, core=None):
        piece = far(w, quarter, at.k if core is None else core, part)
        if sems is s.wx:
            slot = 2 * (w - 1) + index
        elif sems is s.wc:
            slot = 12 if index == 4 else 4 * (w - 1) + index
        else:
            slot = 3 if index else w - 1
        return remote(piece, piece, sems, slot, device)

    def relay_own(w):
        piece_copy(w, own_q, s.wx, 0, at.across).wait_recv()
        start(piece_copy(w, own_q, s.wy, 0, at.beside))
        start(piece_copy(w, own_q, s.wz, 0, at.pair))
        start(piece_copy(w, own_q, s.wc, 0, at.sister))

    def relay_rest(w):
        if direct[w]:
            piece_copy(w, diag_q, s.wx, 1, at.across).wait_recv()
            start(piece_copy(w, diag_q, s.wc, 1, at.sister))
        piece_copy(w, beside_q, s.wy, 0, at.beside).wait_recv()
        if not direct[w]:
            start(piece_copy(w, beside_q, s.wz, 1, at.pair, part=1))
        start(piece_copy(w, beside_q, s.wc, 2, at.sister))
        piece_copy(w, pair_q, s.wz, 0, at.pair).wait_recv()
        if not direct[w]:
            start(piece_copy(w, pair_q, s.wy, 1, at.beside, part=0))
        start(piece_copy(w, pair_q, s.wc, 3, at.sister))

    def relay_diagonal(w):
        piece_copy(w, diag_q, s.wy, 1, at.beside, part=0).wait_recv()
        start(piece_copy(w, diag_q, s.wc, 1, at.sister, part=0))
        piece_copy(w, diag_q, s.wz, 1, at.pair, part=1).wait_recv()
        start(piece_copy(w, diag_q, s.wc, 4, at.sister, part=1))

    def sister_arrivals(w):
        other = 1 - at.k
        piece_copy(w, own_q, s.wc, 0, at.sister, core=other).wait_recv()
        piece_copy(w, beside_q, s.wc, 2, at.sister, core=other).wait_recv()
        piece_copy(w, pair_q, s.wc, 3, at.sister, core=other).wait_recv()
        if direct[w]:
            piece_copy(w, diag_q, s.wc, 1, at.sister, core=other).wait_recv()
        else:
            piece_copy(w, diag_q, s.wc, 1, at.sister, part=0, core=other).wait_recv()
            piece_copy(w, diag_q, s.wc, 4, at.sister, part=1, core=other).wait_recv()

    near_tokens = pl.ds(0, BLOCK)
    far_tokens = pl.ds(BLOCK, BLOCK)
    bias_copy = remote(b.bias_own, b.bias2.at[at.x], s.ex, 0, at.across)
    tok_copy = remote(b.tokens.at[0], b.tok2.at[far_tokens], s.ex, 1, at.across)
    dout_copy = remote(b.d_out.at[0], b.dout_far, s.ex, 2, at.across)
    def q_piece(ref, first_row, size, j, side):
        return ref.at[
            pl.ds(pl.multiple_of(first_row, 16), size),
            pl.ds(pl.multiple_of(j * MODEL + side * HALF, 128), HALF),
        ]

    def q_rows(core, parity):
        return (core * 2 + parity) * QUARTER

    far_base = (1 - at.x) * HALF
    near_base = at.x * HALF

    def q_across(j):
        line = q_rows(at.k, at.parity)
        return remote(
            q_piece(b.w_qkv, line, QUARTER, j, at.y),
            q_piece(b.wq, near_base + line, QUARTER, j, at.y),
            s.qx,
            j,
            at.across,
        )

    def q_move(core, parity, j, sems, index, device):
        piece = q_piece(b.wq, far_base + q_rows(core, parity), QUARTER, j, at.y)
        return remote(piece, piece, sems, index, device)

    def tok_block(i, sem, device):
        piece = b.tok_plane.at[block_rows(0, i)]
        return remote(piece, piece, s.tp, sem, device)

    own_copies = []
    for w in range(4):
        size = shards[w].shape[0]
        own_copies.append(
            pltpu.make_async_copy(
                shards[w],
                wholes[w].at[pl.ds(pl.multiple_of(at.x * size, 16), size)],
                s.local[0].at[w],
            )
        )
    for j in range(3):
        start(q_across(j))
    start(bias_copy)
    start(tok_block(at.r, 0, at.beside))
    start(tok_block(at.r, 1, at.sister))
    own_copies[0].start()
    for d in (1, 2, 3):
        mine = b.ids.at[1, at.r]
        start(remote(mine, mine, s.a2a, (0, d - 1), at.in_plane(at.peer(d))))

    near_rows = pl.multiple_of(at.x * HALF, HALF)
    far_rows = pl.multiple_of((1 - at.x) * HALF, HALF)
    b.tok2[near_tokens, :] = b.tokens[0]
    for j in range(3):
        q_move(at.k, at.parity, j, s.qx, j, at.across).wait_recv()
        start(q_move(at.k, at.parity, j, s.qz, j, at.pair))
        start(q_move(at.k, at.parity, j, s.qc, (0, j), at.sister))
    start(across_copy(2, 0))
    for i in range(2):
        start(across_copy(1, i))
    start(across_copy(3, 0))
    start(across_copy(2, 1))
    start(tok_copy)
    for w in (1, 2, 3):
        own_copies[w].start()
    tok_block(at.peer(2), 0, at.beside).wait_recv()
    start(tok_block(at.peer(2), 2, at.sister))
    for j in range(3):
        q_move(at.k, 1 - at.parity, j, s.qz, j, at.pair).wait_recv()
        start(q_move(at.k, 1 - at.parity, j, s.qc, (1, j), at.sister))
    tok_block(at.peer(1), 1, at.sister).wait_recv()
    tok_block(at.peer(3), 2, at.sister).wait_recv()
    own_copies[0].wait()
    window = [
        pl.ds(pl.multiple_of(j * MODEL + at.y * HALF + at.k * 128, 128), 256) for j in range(3)
    ]
    for j in range(3):
        b.acc[:, j * 256 : (j + 1) * 256] = jnp.dot(
            b.tok_plane[:, pl.ds(near_rows, HALF)],
            b.wq[pl.ds(near_rows, HALF), window[j]],
            preferred_element_type=F32,
        )
    remote(b.bias_own, b.bias2.at[1 - at.x], s.ex, 0, at.across).wait_recv()
    halves = (b.bias2[0].astype(F32), b.bias2[1].astype(F32))
    bias = jnp.concatenate(halves, axis=1)

    def group_bias(row):
        line = bias[row : row + 1, 0:LANES]
        for g in range(1, GROUP):
            line = jnp.where(at.r == g, bias[row : row + 1, g * LANES : (g + 1) * LANES], line)
        return line

    for j in range(3):
        q_move(1 - at.k, at.parity, j, s.qc, (0, j), at.sister).wait_recv()
        q_move(1 - at.k, 1 - at.parity, j, s.qc, (1, j), at.sister).wait_recv()
    made = []
    for j in range(3):
        part = b.acc[:, j * 256 : (j + 1) * 256] + jnp.dot(
            b.tok_plane[:, pl.ds(far_rows, HALF)],
            b.wq[pl.ds(far_rows, HALF), window[j]],
            preferred_element_type=F32,
        )
        made.append(jnp.where(at.k == 0, part[:, 0:LANES], part[:, HEAD_DIM:256]))
    b.kv[pl.ds(PLANE, PLANE), :] = jnp.concatenate(
        [made[1], made[2] + group_bias(1)], axis=1
    ).astype(BF16)

    def both_ways(up, down, act):
        @pl.when(at.has_up)
        def _():
            act(up)

        @pl.when(at.has_down)
        def _():
            act(down)

    def go(copy):
        copy.start()

    middle = b.kv.at[pl.ds(PLANE, PLANE)]
    up_kv = remote(middle, b.kv.at[pl.ds(0, PLANE)], s.halo_f, (0, 0), at.up)
    down_kv = remote(middle, b.kv.at[pl.ds(2 * PLANE, PLANE)], s.halo_f, (1, 0), at.down)
    up_ids = remote(b.ids.at[1], b.ids.at[0], s.halo_f, (0, 1), at.up)
    down_ids = remote(b.ids.at[1], b.ids.at[2], s.halo_f, (1, 1), at.down)

    def from_peer(piece, kind, d):
        remote(piece, piece, s.a2a, (kind, d - 1), at.in_plane(at.peer(d))).wait_recv()

    both_ways(up_kv, down_kv, go)
    b.qp[...] = jnp.concatenate(
        [made[0] + group_bias(0), jnp.zeros((PLANE, HEAD_DIM), F32)], axis=1
    ).astype(BF16)
    for d in (1, 2, 3):
        from_peer(b.ids.at[1, at.peer(d)], 0, d)
    both_ways(up_ids, down_ids, go)

    q_ids = jnp.concatenate([b.ids[1, j][0:1, :] for j in range(GROUP)], axis=1)
    peaks = b.peaks

    def key_ids(i):
        for j in range(GROUP):
            b.k_ids[(i * GROUP + j) * BLOCK : (i * GROUP + j + 1) * BLOCK, :] = column_of(
                b.ids[i, j][0:1, :]
            )

    def attend(i):
        key_ids(i)
        span = pl.ds(i * PLANE, PLANE)
        same = b.k_ids[span, 0:1] == q_ids
        for h in range(GROUP_HEADS):
            q = b.qp[...] * SCALE
            q = jnp.where(lane_head((PLANE, 256), 0) == h, q, jnp.zeros_like(q))
            score = lax.dot_general(b.kv[span, 0:256], q, NT, preferred_element_type=F32)
            score = jnp.where(same, score, NEGATIVE)
            peak = jnp.max(score, axis=0, keepdims=True)
            if i != 1:
                old = peaks[h][0:1, :]
                peak = jnp.maximum(peak, old)
                factor = jnp.exp(old - peak)
            weight = jnp.exp(score - peak)
            summed = jnp.sum(weight, axis=0, keepdims=True)
            first_lane, line = ((128, HEAD_DIM), (256, 0), (256, HEAD_DIM))[h]
            out = lax.dot_general(
                b.kv[span, first_lane : first_lane + 128],
                weight.astype(BF16),
                TN,
                preferred_element_type=F32,
            )[line : line + HEAD_DIM, :]
            if i != 1:
                out = out + b.out_t[h] * factor
                summed = summed + peaks[GROUP_HEADS + h][0:1, :] * factor
            b.out_t[h] = out
            peaks[h] = jnp.broadcast_to(peak, (8, PLANE))
            peaks[GROUP_HEADS + h] = jnp.broadcast_to(summed, (8, PLANE))

    relay_own(2)
    attend(1)
    relay_own(1)

    @pl.when(at.has_down)
    def _():
        came = b.kv.at[pl.ds(0, PLANE)]
        remote(came, came, s.halo_f, (0, 0), at.down).wait_recv()
        remote(b.ids.at[0], b.ids.at[0], s.halo_f, (0, 1), at.down).wait_recv()

    attend(0)

    @pl.when(at.has_up)
    def _():
        came = b.kv.at[pl.ds(2 * PLANE, PLANE)]
        remote(came, came, s.halo_f, (1, 0), at.up).wait_recv()
        remote(b.ids.at[2], b.ids.at[2], s.halo_f, (1, 1), at.up).wait_recv()

    attend(2)
    outs = [jnp.zeros((HEAD_DIM, PLANE), F32)]
    for h in range(GROUP_HEADS):
        summed = peaks[GROUP_HEADS + h][0:1, :]
        out = b.out_t[h] / summed
        b.out_t[h] = out
        b.stats[h] = peaks[h] + jnp.log(peaks[GROUP_HEADS + h])
        outs.append(out)
    attended = jnp.concatenate(outs, axis=0).T.astype(BF16)
    for i in range(GROUP):
        b.asend[i] = attended[i * BLOCK : (i + 1) * BLOCK, :]

    for d in (1, 2, 3):
        i = at.peer(d)
        start(remote(b.asend.at[i], b.arecv.at[at.r], s.a2a, (1, d - 1), at.in_plane(i)))
    b.arecv[at.r] = b.asend[at.r]
    relay_own(3)
    relay_rest(1)
    relay_rest(2)
    for d in (1, 2, 3):
        from_peer(b.arecv.at[at.peer(d)], 1, d)
    b.att2[near_tokens, :] = jnp.concatenate(
        [b.arecv[g].astype(F32)[:, HEAD_DIM : HEAD_DIM + LANES] for g in range(GROUP)], axis=1
    ).astype(BF16)
    att_copy = remote(b.att2.at[near_tokens], b.att2.at[far_tokens], s.ex, 3, at.across)
    start(att_copy)
    start(dout_copy)
    for w in (1, 2):
        own_copies[w].wait()
        sister_arrivals(w)

    def normalise(hidden):
        center = hidden - jnp.mean(hidden, -1, keepdims=True)
        inverse = lax.rsqrt(jnp.mean(center * center, -1, keepdims=True) + EPSILON)
        return center * inverse, inverse

    def norm_back(upstream, unit, inverse, gain):
        scaled = upstream * gain
        return inverse * (
            scaled
            - jnp.mean(scaled, -1, keepdims=True)
            - unit * jnp.mean(scaled * unit, -1, keepdims=True)
        )

    def column_sum(value):
        return jnp.sum(value, axis=0, keepdims=True)

    def dense_forward(side):
        lines = (near_tokens, far_tokens)[side]
        first = (
            b.tok2[lines, :].astype(F32)
            + jnp.dot(b.att2[lines, :], b.wo[...], preferred_element_type=F32)
            + bias[2:3]
        )
        unit, inverse = normalise(first)
        b.unit_one[lines, :] = unit
        normed = unit * bias[3:4] + bias[4:5]
        b.norm_low[lines, :] = normed.astype(BF16)
        b.second[lines, :] = normed + bias[9:10]
        for c in range(4):
            if side == 1 and c == 2:
                relay_diagonal(3)
            cols = slice(c * MODEL, (c + 1) * MODEL)
            part = halves[c // 2]
            i = 5 + 2 * (c % 2)
            line = jnp.concatenate([part[i : i + 1], part[i + 1 : i + 2]], axis=1)
            inner = line + jnp.dot(
                b.norm_low[lines, :], b.wi[:, cols], preferred_element_type=F32
            )
            gate = 0.5 * (1.0 + lax.erf(inner * ROOT_HALF))
            b.act[lines, cols] = (inner * gate).astype(BF16)
            b.slope[pl.ds(c * BOTH + side * BLOCK, BLOCK), :] = (
                gate + inner * jnp.exp(-0.5 * inner * inner) * INV_ROOT_TAU
            )
        return inverse

    near_inverse = dense_forward(0)
    relay_rest(3)
    tok_copy.wait_recv()
    att_copy.wait_recv()
    inverse_one = jnp.concatenate([near_inverse, dense_forward(1)], axis=0)
    own_copies[3].wait()
    sister_arrivals(3)
    b.second[...] += jnp.dot(b.act[...], b.wb[...], preferred_element_type=F32)
    unit_two, inverse_two = normalise(b.second[...])
    b.result[...] = (unit_two[:BLOCK] * bias[10:11] + bias[11:12]).astype(BF16)
    dout_copy.wait_recv()
    upstream = jnp.concatenate([b.d_out[0], b.dout_far[...]], axis=0).astype(F32)
    b.small[...] = jnp.zeros_like(b.small)
    b.small[10:11, :] = column_sum(upstream * unit_two)
    b.small[11:12, :] = column_sum(upstream)
    d_second = norm_back(upstream, unit_two, inverse_two, bias[10:11])
    b.small[9:10, :] = column_sum(d_second)
    b.d_second[...] = d_second.astype(BF16)
    b.second[...] = d_second

    chunks = [chunk_of(rows, planes) for rows in SET_ROWS]
    owners = [rows // chunk for rows, chunk in zip(SET_ROWS, chunks)]

    def of(name, group):
        return getattr(b, f"{name}{group}")

    def tile(group, t):
        if group == 0:
            lanes = pl.multiple_of(at.x * (TILES * HALF) + t * HALF, 128)
            left, right = b.act[:, pl.ds(lanes, HALF)], b.d_second[...]
        else:
            left = b.norm_low[:, pl.ds(near_rows, HALF)]
            right = b.d_inner[:, pl.ds(pl.multiple_of(t * MODEL, 128), MODEL)]
        return lax.dot_general(left, right, TN, preferred_element_type=F32)

    def out_quarter(t):
        return b.out_tile[pl.ds(pl.multiple_of(t * QUARTER, 16), QUARTER), :]

    def chunk_rows(group, j):
        return pl.ds(pl.multiple_of(j * chunks[group], 16), chunks[group])

    def own_chunk(group, j):
        if group == 2:
            return b.q_sum.at[chunk_rows(2, j)]
        first_row = OWN_ROWS[group] + j * chunks[group]
        return b.slope.at[pl.ds(pl.multiple_of(first_row, 16), chunks[group])]

    def core_copy(group, i):
        return remote(
            of("core_send", group).at[i],
            of("core_recv", group).at[i],
            s.core,
            group * 2 + i,
            at.sister,
        )

    def y_copy(group, j):
        lines = chunk_rows(group, j)
        return remote(
            of("y_send", group).at[lines],
            of("y_recv", group).at[lines],
            s.ys,
            (group, j),
            at.beside,
        )

    def up_copy(group, j):
        lines = chunk_rows(group, j)
        return remote(
            of("z_send", group).at[lines],
            of("up_recv", group).at[lines],
            s.up,
            (group, j),
            at.up,
        )

    def down_copy(group, j):
        lines = chunk_rows(group, j)
        return remote(
            of("z_send", group).at[lines],
            of("down_recv", group).at[lines],
            s.down,
            (group, j),
            at.down,
        )

    middle_step = planes // 2 + 1
    early, late = (1, middle_step), (middle_step, planes + 1)
    whole_way = (1, planes + 1)

    def each_owner(group, act, span):
        def one(d, carry):
            j = jnp.where(at.p < planes // 2, planes - d, d - 1)

            @pl.when(j < owners[group])
            def _():
                act(j)

            return carry

        lax.fori_loop(*span, one, 0)

    def make(group):
        base = OWN_ROWS[group]
        for i, t in enumerate((at.peer(3), at.peer(1))):
            of("core_send", group)[i, 0:HALF, :] = tile(group, t).astype(BF16)
            if group == 1:
                of("core_send", group)[i, HALF : HALF + QUARTER, :] = out_quarter(t).astype(BF16)
            start(core_copy(group, i))
        b.slope[base : base + HALF, :] = tile(group, at.r)
        if group == 1:
            b.slope[base + HALF : base + HALF + QUARTER, :] = out_quarter(at.r)

    def go_over_y(group, span):
        each_owner(group, lambda j: y_copy(group, j).start(), span)

    def exchange(group):
        base = OWN_ROWS[group]
        passing = tile(group, at.peer(2))
        core_copy(group, 0).wait_recv()
        come = of("core_recv", group)
        of("y_send", group)[0:HALF, :] = (passing + come[0, 0:HALF, :].astype(F32)).astype(BF16)
        if group == 1:
            lines = slice(HALF, HALF + QUARTER)
            b.y_send1[HALF + QUARTER :, :] = jnp.zeros((BLOCK - QUARTER, MODEL), BF16)
            of("y_send", group)[lines, :] = (
                out_quarter(at.peer(2)) + come[0, lines, :].astype(F32)
            ).astype(BF16)
        go_over_y(group, (1, 2) if group == 0 else early)
        core_copy(group, 1).wait_recv()
        used = SET_ROWS[0] if group == 0 else HALF + QUARTER
        b.slope[base : base + used, :] += come[1, 0:used, :].astype(F32)

    def scatter(group, span):
        def act(j):
            mine = own_chunk(group, j)
            if group == 2:
                x_copy(j).wait_recv()
                came = b.x_recv[chunk_rows(2, j), :]
            else:
                y_copy(group, j).wait_recv()
                came = of("y_recv", group)[chunk_rows(group, j), :]
            total = mine[...] + came.astype(F32)
            mine[...] = total

            @pl.when(jnp.logical_and(at.p == 0, j > 0))
            def _():
                of("z_send", group)[chunk_rows(group, j), :] = total.astype(BF16)
                up_copy(group, j).start()

            @pl.when(jnp.logical_and(at.p == planes - 1, j < planes - 1))
            def _():
                of("z_send", group)[chunk_rows(group, j), :] = total.astype(BF16)
                down_copy(group, j).start()

        each_owner(group, act, span)

    def add_arrived(group, j, name, sems, device):
        lines = chunk_rows(group, j)
        came = of(name, group).at[lines]
        remote(came, came, sems, (group, j), device).wait_recv()
        return came[...].astype(F32)

    def relay_sums(group, h):
        @pl.when(at.p == h)
        def _():
            def one(i, carry):
                j = owners[group] - 1 - i
                total = own_chunk(group, j)[...] + add_arrived(
                    group, j, "up_recv", s.up, at.down
                )
                of("z_send", group)[chunk_rows(group, j), :] = total.astype(BF16)
                up_copy(group, j).start()
                return carry

            lax.fori_loop(0, owners[group] - 1 - at.p, one, 0)

        @pl.when(at.p == planes - 1 - h)
        def _():
            def one(j, carry):
                total = own_chunk(group, j)[...] + add_arrived(
                    group, j, "down_recv", s.down, at.up
                )
                of("z_send", group)[chunk_rows(group, j), :] = total.astype(BF16)
                down_copy(group, j).start()
                return carry

            lax.fori_loop(0, jnp.minimum(at.p, owners[group]), one, 0)

    def x_copy(j):
        lines = chunk_rows(2, j)
        return remote(b.x_send.at[lines], b.x_recv.at[lines], s.xs, j, at.across)

    def more_sums(group):
        def one(h, carry):
            relay_sums(group, h)
            return carry

        lax.fori_loop(3, planes - 1, one, 0)

    def place(group, t, j):
        first_row = t * SET_ROWS[group] + j * chunks[group]
        return of("sums", group).at[pl.ds(pl.multiple_of(first_row, 16), chunks[group])]

    def gather_copy(group, t, j, sems, device, source=None):
        piece = place(group, t, j)
        return remote(piece if source is None else source, piece, sems, (group, j), device)

    def spread(group, j, source=None):
        @pl.when(jnp.logical_and(j <= at.p, at.has_up))
        def _():
            gather_copy(group, at.r, j, s.gu, at.up, source).start()

        @pl.when(jnp.logical_and(j >= at.p, at.has_down))
        def _():
            gather_copy(group, at.r, j, s.gd, at.down, source).start()

        gather_copy(group, at.r, j, s.gy, at.beside, source).start()
        gather_copy(group, at.r, j, s.gc, at.sister, source).start()

    def settle_copy(group):
        return pltpu.make_async_copy(
            of("final", group), place(group, at.r, at.p), s.local[1].at[group]
        )

    def settle(group):
        @pl.when(at.p < owners[group])
        def _():
            mine = own_chunk(group, at.p)

            @pl.when(at.has_down)
            def _():
                mine[...] += add_arrived(group, at.p, "up_recv", s.up, at.down)

            @pl.when(at.has_up)
            def _():
                mine[...] += add_arrived(group, at.p, "down_recv", s.down, at.up)

            total = mine[...]
            of("final", group)[...] = total.astype(BF16)
            spread(group, at.p, of("final", group))
            settle_copy(group).start()

    def around(group, d, act):
        @pl.when(jnp.logical_and(at.p - d >= 0, at.p - d < owners[group]))
        def _():
            act(at.p - d, s.gu, at.down)

        @pl.when(jnp.logical_and(d > 0, at.p + d < owners[group]))
        def _():
            act(at.p + d, s.gd, at.up)

    def come_in(group, d):
        def act(j, sems, device):
            gather_copy(group, at.r, j, sems, device).wait_recv()
            spread(group, j)

        around(group, d, act)

    def hand_over(group, d):
        def act(j, sems, device):
            gather_copy(group, at.peer(2), j, s.gy, at.beside).wait_recv()
            gather_copy(group, at.peer(2), j, s.gf, at.sister).start()

        around(group, d, act)

    def more_gathers():
        def one(d, carry):
            for group in range(3):
                come_in(group, d)
                hand_over(group, d)
            return carry

        lax.fori_loop(4, planes, one, 0)

    make(0)
    for c in range(4):
        if c == 2:
            exchange(0)
        cols = slice(c * MODEL, (c + 1) * MODEL)
        d_inner = (
            lax.dot_general(b.d_second[...], b.wb[cols, :], NT, preferred_element_type=F32)
            * b.slope[c * BOTH : (c + 1) * BOTH, :]
        )
        b.small[5 + c : 6 + c, :] = column_sum(d_inner)
        low = d_inner.astype(BF16)
        b.d_inner[:, cols] = low
        b.second[...] += lax.dot_general(low, b.wi[:, cols], NT, preferred_element_type=F32)
    d_normed = b.second[...]
    unit_one = b.unit_one[...]
    b.small[3:4, :] = column_sum(d_normed * unit_one)
    b.small[4:5, :] = column_sum(d_normed)
    d_first = norm_back(d_normed, unit_one, inverse_one, bias[3:4])
    b.small[2:3, :] = column_sum(d_first)
    d_first_low = d_first.astype(BF16)
    b.d_first[...] = d_first_low
    b.d_tokens[...] = d_first[:BLOCK]
    d_attn = lax.dot_general(d_first_low[:BLOCK], b.wo[...], NT, preferred_element_type=F32)
    for g in range(GROUP):
        b.dsend[g] = jnp.concatenate(
            [jnp.zeros((BLOCK, HEAD_DIM), F32), d_attn[:, g * LANES : (g + 1) * LANES]], axis=1
        ).astype(BF16)
    for d in (1, 2, 3):
        g = at.peer(d)
        start(
            remote(
                b.dsend.at[g], b.do.at[block_rows(0, at.r)], s.a2a, (2, d - 1), at.in_plane(g)
            )
        )
    go_over_y(0, (2, planes + 1))
    b.do[block_rows(0, at.r), :] = b.dsend[at.r]

    b.out_tile[...] = lax.dot_general(
        b.att2[:, pl.ds(near_rows, HALF)], b.d_first[...], TN, preferred_element_type=F32
    )
    make(1)
    scatter(0, (1, 2))

    b.grads[...] = jnp.zeros_like(b.grads)
    b.dq[...] = jnp.zeros_like(b.dq)
    for d in (1, 2, 3):
        from_peer(b.do.at[block_rows(0, at.peer(d))], 2, d)
    do_t = b.do[...].astype(F32).T
    for h in range(GROUP_HEADS):
        lines = slice(HEAD_DIM * (h + 1), HEAD_DIM * (h + 2))
        b.stats[GROUP_HEADS + h] = jnp.broadcast_to(
            column_sum(do_t[lines, :] * b.out_t[h]), (8, PLANE)
        )

    def visit(h, i):
        span = pl.ds(i * PLANE, PLANE)
        pick_q = lane_head((PLANE, 256), 0) == h
        q = b.qp[...]
        q = jnp.where(pick_q, q, jnp.zeros_like(q))
        dout = b.do[...]
        dout = jnp.where(lane_head((PLANE, 256), 1) == h, dout, jnp.zeros_like(dout))
        keys = b.kv[span, 0:256]
        score = lax.dot_general(keys, q * SCALE, NT, preferred_element_type=F32)
        same = b.k_ids[span, 0:1] == q_ids
        prob = jnp.where(same, jnp.exp(score - b.stats[h][0:1, :]), 0.0)
        d_prob = lax.dot_general(b.kv[span, 128:384], dout, NT, preferred_element_type=F32)
        d_score = (prob * (d_prob - b.stats[GROUP_HEADS + h][0:1, :]) * SCALE).astype(BF16)
        b.grads[span, 0:256] += jnp.dot(d_score, q, preferred_element_type=F32)
        b.grads[span, 128:384] += jnp.dot(
            prob.astype(BF16), dout, preferred_element_type=F32
        )
        b.dq[...] += jnp.where(
            pick_q, lax.dot_general(d_score, keys, TN, preferred_element_type=F32), 0.0
        )

    def visit_plane(i):
        def one(h, carry):
            visit(h, i)
            return carry

        lax.fori_loop(0, GROUP_HEADS, one, 0)

    down_grads = remote(b.halo_send.at[0], b.halo.at[1], s.halo_b, 0, at.down)
    up_grads = remote(b.halo_send.at[1], b.halo.at[0], s.halo_b, 1, at.up)
    visit_plane(0)
    b.halo_send[0] = b.grads[pl.ds(0, PLANE), :].astype(BF16)

    @pl.when(at.has_down)
    def _():
        down_grads.start()

    scatter(0, (2, 3))
    exchange(1)
    visit_plane(2)
    b.halo_send[1] = b.grads[pl.ds(2 * PLANE, PLANE), :].astype(BF16)

    @pl.when(at.has_up)
    def _():
        up_grads.start()

    go_over_y(1, late)
    scatter(0, (3, planes + 1))
    relay_sums(0, 1)
    visit_plane(1)
    b.d_group[:, 0:256] = b.dq[...].astype(BF16)

    @pl.when(at.has_up)
    def _():
        remote(b.halo.at[1], b.halo.at[1], s.halo_b, 0, at.up).wait_recv()
        b.grads[pl.ds(PLANE, PLANE), :] += b.halo[1].astype(F32)

    relay_sums(0, 2)
    scatter(1, early)

    @pl.when(at.has_down)
    def _():
        remote(b.halo.at[0], b.halo.at[0], s.halo_b, 1, at.down).wait_recv()
        b.grads[pl.ds(PLANE, PLANE), :] += b.halo[0].astype(F32)

    b.d_group[:, 256:640] = b.grads[pl.ds(PLANE, PLANE), :].astype(BF16)

    b.line_send[...] = jnp.broadcast_to(column_sum(b.d_group[...].astype(F32)), (8, 640))
    line_copy = remote(b.line_send, b.line_recv, s.ex, 4, at.across)
    start(line_copy)
    b.x_send[...] = lax.dot_general(
        b.tok_plane[:, pl.ds(far_rows, HALF)], b.d_group[...], TN, preferred_element_type=F32
    ).astype(BF16)
    each_owner(2, lambda j: x_copy(j).start(), whole_way)
    b.q_sum[...] = lax.dot_general(
        b.tok_plane[:, pl.ds(near_rows, HALF)], b.d_group[...], TN, preferred_element_type=F32
    )

    partners = [at.sister, at.beside]
    span = 1
    while span < planes:
        partners.append((at.c + GROUP * span * (1 - 2 * ((at.p // span) % 2)), at.x))
        span *= 2

    def small_copy(i):
        return remote(b.small, b.small_recv.at[i], s.sm, i, partners[i])

    def small_finish(i):
        small_copy(i).wait()
        b.small[...] += b.small_recv[i]

    def sums_sent(group):
        def one(j, carry):
            if group == 2:
                x_copy(j).wait_send()
            else:
                y_copy(group, j).wait_send()

            @pl.when(at.p < j)
            def _():
                up_copy(group, j).wait_send()

            @pl.when(at.p > j)
            def _():
                down_copy(group, j).wait_send()

            return carry

        lax.fori_loop(0, owners[group], one, 0)

        @pl.when(at.p < owners[group])
        def _():
            settle_copy(group).wait()

    def gathers_done(group):
        def one(j, carry):
            gather_copy(group, at.peer(1), j, s.gc, at.sister).wait_recv()
            gather_copy(group, at.peer(3), j, s.gf, at.sister).wait_recv()
            gather_copy(group, at.r, j, s.gy, at.beside).wait_send()
            gather_copy(group, at.r, j, s.gc, at.sister).wait_send()
            gather_copy(group, at.peer(2), j, s.gf, at.sister).wait_send()

            @pl.when(jnp.logical_and(j <= at.p, at.has_up))
            def _():
                gather_copy(group, at.r, j, s.gu, at.up).wait_send()

            @pl.when(jnp.logical_and(j >= at.p, at.has_down))
            def _():
                gather_copy(group, at.r, j, s.gd, at.down).wait_send()

            return carry

        lax.fori_loop(0, owners[group], one, 0)

    def finish(copy):
        copy.wait_send()

    more_sums(0)
    settle(0)
    relay_sums(1, 1)
    line_copy.wait_recv()
    line = b.line_send[...] + b.line_recv[...]
    mine = lax.broadcasted_iota(jnp.int32, (8, 640), 0) == at.r
    b.small[16:24, 0:640] = jnp.where(mine, line, 0.0)
    small_copy(0).start()
    scatter(2, early)
    small_finish(0)
    small_copy(1).start()
    scatter(1, late)

    spare = 2 * BOTH
    gap = jnp.zeros((PLANE, HEAD_DIM), F32)
    for j, first_lane in enumerate((0, 256, 448)):
        piece = b.d_group[...].astype(F32)[:, first_lane : first_lane + LANES]
        wide = jnp.where(
            at.k == 0,
            jnp.concatenate([piece, gap], axis=1),
            jnp.concatenate([gap, piece], axis=1),
        ).astype(BF16)
        part = lax.dot_general(wide, b.wq[:, window[j]], NT, preferred_element_type=F32)
        if j == 0:
            b.slope[spare : spare + PLANE, :] = part
        else:
            b.slope[spare : spare + PLANE, :] += part

    def dt_block(i):
        return b.slope[block_rows(spare, i), :]

    def dt_copy(i):
        device = at.beside if i == 2 else at.sister
        return remote(b.dt_send.at[i], b.dt_recv.at[i], s.dt, i, device)

    for i, block in enumerate((at.peer(3), at.peer(1))):
        b.dt_send[i] = dt_block(block).astype(BF16)
        start(dt_copy(i))

    come_in(0, 1)
    relay_sums(1, 2)
    relay_sums(2, 1)
    hand_over(0, 0)
    scatter(2, late)
    relay_sums(2, 2)
    dt_copy(0).wait_recv()
    b.dt_send[2] = (dt_block(at.peer(2)) + b.dt_recv[0].astype(F32)).astype(BF16)
    start(dt_copy(2))
    more_sums(1)
    settle(1)
    come_in(0, 2)
    more_sums(2)
    settle(2)
    small_finish(1)
    small_copy(2).start()
    hand_over(0, 1)
    come_in(1, 1)
    come_in(0, 3)
    come_in(2, 1)
    for copy in sent:
        copy.wait_send()
    both_ways(up_kv, down_kv, finish)
    both_ways(up_ids, down_ids, finish)
    both_ways(up_grads, down_grads, finish)
    for group in range(3):
        sums_sent(group)
    hand_over(0, 2)
    dt_copy(1).wait_recv()
    dt_copy(2).wait_recv()
    b.d_tokens[...] += (
        dt_block(at.r) + b.dt_recv[1].astype(F32) + b.dt_recv[2].astype(F32)
    )
    come_in(1, 2)
    come_in(2, 2)
    small_finish(2)
    small_copy(3).start()
    hand_over(0, 3)
    hand_over(1, 0)
    come_in(1, 3)
    come_in(2, 3)
    hand_over(2, 0)
    hand_over(1, 1)
    if planes <= GROUP:
        gathers_done(0)
    hand_over(2, 1)
    hand_over(1, 2)
    small_finish(3)
    hand_over(2, 2)
    hand_over(1, 3)
    if planes <= GROUP:
        gathers_done(1)
    hand_over(2, 3)
    more_gathers()
    for i in range(4, len(partners)):
        small_copy(i).start()
        small_finish(i)

    if planes > GROUP:
        gathers_done(0)
        gathers_done(1)
    gathers_done(2)


def layer_call(planes, args):
    buffers, semaphores = scratch_plan(planes)
    hbm = pl.BlockSpec(memory_space=pltpu.HBM)
    vmem = pl.BlockSpec(memory_space=pltpu.VMEM)
    weights = ("w_qkv", "w_out", "w_in", "w_back")
    scratch = [pltpu.VMEM(shape, kind) for shape, kind in buffers.values()]
    for shape in semaphores.values():
        scratch += [pltpu.SemaphoreType.DMA(shape)] * 2
    return pl.pallas_call(
        functools.partial(layer_kernel, planes, list(buffers), list(semaphores)),
        out_shape=[
            jax.ShapeDtypeStruct((BLOCK, MODEL), BF16),
            jax.ShapeDtypeStruct((BLOCK, MODEL), F32),
        ]
        + [
            jax.ShapeDtypeStruct((TILES * rows, width), BF16)
            for rows, width in zip(SET_ROWS, SET_WIDTH)
        ]
        + [jax.ShapeDtypeStruct((24, MODEL), F32)],
        in_specs=[hbm if name in weights else vmem for name in ARGS],
        out_specs=[vmem, vmem, hbm, hbm, hbm, vmem],
        scratch_shapes=scratch,
        compiler_params=pltpu.CompilerParams(
            collective_id=0, has_side_effects=True, vmem_limit_bytes=60 * 2**20
        ),
        name="layer",
    )(*args)


def unpack_kernel(result_in, tokens_in, sums0, sums1, sums2, small, *refs):
    result, d_tokens, w_qkv, bq, bv, w_out, bo, g1, o1, w_in, bi, w_back, bb, g2, o2 = refs[:15]
    in0, in1, in2, out_q, out_o, out_i, out_b, come, go = refs[15:]
    loads = []
    for g, (sums, held) in enumerate(((sums0, in0), (sums1, in1), (sums2, in2))):
        for t in range(TILES):
            lines = pl.ds(t * SET_ROWS[g], SET_ROWS[g])
            loads.append(
                pltpu.make_async_copy(sums.at[lines], held.at[t], come.at[g * TILES + t])
            )
    for load in loads:
        load.start()
    stores = [
        pltpu.make_async_copy(result_in, result, go.at[14]),
        pltpu.make_async_copy(tokens_in, d_tokens, go.at[15]),
    ]
    for store in stores:
        store.start()

    def put(source, target, i):
        store = pltpu.make_async_copy(source, target, go.at[i])
        store.start()
        stores.append(store)

    x = lax.axis_index("wsh")
    half = small[0:16, pl.ds(pl.multiple_of(x * HALF, 128), HALF)]
    for ref, row in zip((bo, g1, o1, bb, g2, o2), (2, 3, 4, 9, 10, 11)):
        ref[...] = half[row, :]
    whole = jnp.where(x == 0, small[5:7, :], small[7:9, :])
    bi[pl.ds(0, MODEL)] = whole[0, :]
    bi[pl.ds(MODEL, MODEL)] = whole[1, :]
    for ref, first in ((bq, 0), (bv, 448)):
        row = jnp.concatenate(
            [small[16 + g : 17 + g, first : first + LANES] for g in range(GROUP)], axis=1
        )
        ref[...] = jnp.where(x == 0, row[:, :HALF], row[:, HALF:])[0, :]

    for t in range(TILES):
        loads[t].wait()
        lines = pl.ds(t * HALF, HALF)
        out_b[lines, :] = in0[t].astype(F32)
        put(out_b.at[lines], w_back.at[lines], t)
    for t in range(TILES):
        loads[TILES + t].wait()
        out_i[t] = in1[t, 0:HALF, :].astype(F32)
        put(out_i.at[t], w_in.at[:, pl.ds(t * MODEL, MODEL)], 4 + t)
        lines = pl.ds(t * QUARTER, QUARTER)
        out_o[lines, :] = in1[t, HALF : HALF + QUARTER, :].astype(F32)
        put(out_o.at[lines], w_out.at[lines], 8 + t)
    for pair in range(2):
        loads[2 * TILES + 2 * pair].wait()
        loads[2 * TILES + 2 * pair + 1].wait()
        for j, first in enumerate((0, 256, 448)):
            out_q[:, j * MODEL + pair * HALF : j * MODEL + (pair + 1) * HALF] = (
                jnp.concatenate(
                    [
                        in2[2 * pair + i].astype(F32)[:, first : first + LANES]
                        for i in range(2)
                    ],
                    axis=1,
                )
            )
    put(out_q, w_qkv, 12)
    for store in stores:
        store.wait()


def unpack_call(*arrays):
    shape = jax.ShapeDtypeStruct
    vmem = pl.BlockSpec(memory_space=pltpu.VMEM)
    hbm = pl.BlockSpec(memory_space=pltpu.HBM)
    vector = (shape((HALF,), F32), vmem)
    outs = [
        (shape((BLOCK, MODEL), BF16), hbm),
        (shape((BLOCK, MODEL), F32), hbm),
        (shape((HALF, 3 * MODEL), F32), hbm),
        vector,
        vector,
        (shape((HALF, MODEL), F32), hbm),
        vector,
        vector,
        vector,
        (shape((HALF, FF), F32), hbm),
        (shape((FF // 2,), F32), vmem),
        (shape((FF // 2, MODEL), F32), hbm),
        vector,
        vector,
        vector,
    ]
    return pl.pallas_call(
        unpack_kernel,
        out_shape=[o[0] for o in outs],
        in_specs=[vmem, vmem, hbm, hbm, hbm, vmem],
        out_specs=[o[1] for o in outs],
        scratch_shapes=[
            pltpu.VMEM((TILES, rows, width), BF16)
            for rows, width in zip(SET_ROWS, SET_WIDTH)
        ]
        + [
            pltpu.VMEM((HALF, 3 * MODEL), F32),
            pltpu.VMEM((HALF, MODEL), F32),
            pltpu.VMEM((TILES, HALF, MODEL), F32),
            pltpu.VMEM((FF // 2, MODEL), F32),
            pltpu.SemaphoreType.DMA((3 * TILES,)),
            pltpu.SemaphoreType.DMA((16,)),
        ],
        compiler_params=pltpu.CompilerParams(vmem_limit_bytes=60 * 2**20),
        name="unpack",
    )(*arrays)


def body(*args):
    planes = lax.axis_size("ctx") // GROUP
    result, d_tokens, *rest = unpack_call(*layer_call(planes, args))
    return (result[None], d_tokens[None], *rest)


def solution(mesh):
    token_spec = P("wsh", "ctx", None)
    matrix, vector = P("wsh", None), P("wsh")
    in_specs = (
        token_spec,
        P("wsh", "ctx"),
        matrix,
        vector,
        vector,
        matrix,
        vector,
        vector,
        vector,
        matrix,
        vector,
        matrix,
        vector,
        vector,
        vector,
        token_spec,
    )
    out_specs = (
        token_spec,
        token_spec,
        matrix,
        vector,
        vector,
        matrix,
        vector,
        vector,
        vector,
        matrix,
        vector,
        matrix,
        vector,
        vector,
        vector,
    )
    return jax.shard_map(body, mesh=mesh, in_specs=in_specs, out_specs=out_specs, check_vma=False)
```

```python
import functools
import types

import jax
import jax.numpy as jnp
from jax import lax
from jax.experimental import pallas as pl
from jax.experimental.pallas import tpu as pltpu
from jax.sharding import PartitionSpec as P

HEAD_DIM = 64
GROUP = 4
GROUP_HEADS = 3
BLOCK = 128
PLANE = GROUP * BLOCK
MODEL = 768
FF = 3072
HALF = MODEL // 2
LANES = GROUP_HEADS * HEAD_DIM
TILES = 4
OWN_ROWS = (4 * 2 * BLOCK, 0)
BOTH = 2 * BLOCK
EPSILON = 1e-05
NEGATIVE = -1e30
ROOT_HALF = 0.7071067811865476
INV_ROOT_TAU = 0.3989422804014327
SCALE = HEAD_DIM**-0.5
MESH = pl.DeviceIdType.MESH
F32 = jnp.float32
BF16 = jnp.bfloat16
NT = (((1,), (1,)), ((), ()))
TN = (((0,), (0,)), ((), ()))


class Place:
    def __init__(self, planes):
        self.n = planes
        self.c = lax.axis_index("ctx")
        self.x = lax.axis_index("wsh")
        self.p = self.c // GROUP
        self.r = self.c % GROUP
        self.y = self.r // 2
        self.k = self.r % 2
        self.parity = self.p % 2
        self.sister = (self.c + 1 - 2 * self.k, self.x)
        self.beside = (self.c + 2 - 4 * self.y, self.x)
        self.across = (self.c, 1 - self.x)
        self.pair = (self.c + GROUP * (1 - 2 * self.parity), self.x)
        self.up = (self.c + GROUP, self.x)
        self.down = (self.c - GROUP, self.x)
        self.has_up = self.p < planes - 1
        self.has_down = self.p > 0

    def peer(self, d):
        if d == 1:
            return self.y * 2 + (1 - self.k)
        if d == 2:
            return (1 - self.y) * 2 + self.k
        return (1 - self.y) * 2 + (1 - self.k)

    def in_plane(self, position):
        return (self.p * GROUP + position, self.x)

    def plane(self, p):
        return (p * GROUP + self.r, self.x)


def signal(sem, device):
    pl.semaphore_signal(sem, inc=1, device_id=device, device_id_type=MESH)


def greet(at):
    barrier = pltpu.get_barrier_semaphore()
    for d in (1, 2, 3):
        signal(barrier, at.in_plane(at.peer(d)))
    signal(barrier, at.across)

    def other_plane(d, carry):
        signal(barrier, at.plane((at.p + d) % at.n))
        return carry

    lax.fori_loop(1, at.n, other_plane, 0)
    pl.semaphore_wait(barrier, 4 + at.n - 1)


def remote(src, dst, sems, index, device, recv_index=None):
    send, recv = sems
    return pltpu.make_async_remote_copy(
        src_ref=src,
        dst_ref=dst,
        send_sem=send.at[index],
        recv_sem=recv.at[index if recv_index is None else recv_index],
        device_id=device,
        device_id_type=MESH,
    )


def lane_head(shape, first):
    return lax.broadcasted_iota(jnp.int32, shape, 1) // HEAD_DIM - first


def column_of(row):
    return jnp.broadcast_to(row, (BLOCK, BLOCK)).T


def chunk_of(rows, planes):
    chunk = -(-(-(-rows // planes)) // 16) * 16
    while rows % chunk:
        chunk += 16
    return chunk


SET_ROWS = (HALF, 512, HALF)
SET_WIDTH = (MODEL, MODEL, 640)
QUARTER = HALF // GROUP


def scratch_plan(planes):
    steps = planes.bit_length() - 1
    buffers = dict(
        wq=((MODEL, 3 * MODEL), BF16),
        wo=((MODEL, MODEL), BF16),
        wi=((MODEL, FF), BF16),
        wb=((FF, MODEL), BF16),
        bias_own=((16, HALF), BF16),
        bias2=((2, 16, HALF), BF16),
        dout_far=((BLOCK, MODEL), BF16),
        ids=((3, GROUP, 8, BLOCK), F32),
        acc=((PLANE, 3 * 256), F32),
        qp=((PLANE, 256), BF16),
        kv=((3 * PLANE, 2 * LANES), BF16),
        out_t=((GROUP_HEADS, HEAD_DIM, PLANE), F32),
        peaks=((2 * GROUP_HEADS, 8, PLANE), F32),
        asend=((GROUP, BLOCK, 256), BF16),
        arecv=((GROUP, BLOCK, 256), BF16),
        tok_plane=((PLANE, MODEL), BF16),
        tok2=((BOTH, MODEL), BF16),
        att2=((BOTH, MODEL), BF16),
        unit_one=((BOTH, MODEL), F32),
        norm_low=((BOTH, MODEL), BF16),
        act=((BOTH, FF), BF16),
        d_inner=((BOTH, FF), BF16),
        d_second=((BOTH, MODEL), BF16),
        d_first=((BOTH, MODEL), BF16),
        second=((BOTH, MODEL), F32),
        slope=((4 * BOTH + HALF, MODEL), F32),
        out_tile=((HALF, MODEL), F32),
        dsend=((GROUP, BLOCK, 256), BF16),
        do=((PLANE, 256), BF16),
        grads=((3 * PLANE, 2 * LANES), F32),
        dq=((PLANE, 256), F32),
        k_ids=((3 * PLANE, BLOCK), F32),
        stats=((2 * GROUP_HEADS, 8, PLANE), F32),
        halo_send=((2, PLANE, 2 * LANES), BF16),
        halo=((2, PLANE, 2 * LANES), BF16),
        d_group=((PLANE, 640), BF16),
        dt_send=((3, BLOCK, MODEL), BF16),
        dt_recv=((3, BLOCK, MODEL), BF16),
        q_sum=((HALF, 640), F32),
        x_send=((HALF, 640), BF16),
        x_recv=((HALF, 640), BF16),
        small_recv=((2 + steps, 24, MODEL), F32),
        line_send=((8, 640), F32),
        line_recv=((8, 640), F32),
    )
    for g, (rows, width) in enumerate(zip(SET_ROWS, SET_WIDTH)):
        chunk = chunk_of(rows, planes)
        if g < 2:
            buffers[f"core_send{g}"] = ((2, rows, width), BF16)
            buffers[f"core_recv{g}"] = ((2, rows, width), BF16)
            buffers[f"y_send{g}"] = ((rows, width), BF16)
            buffers[f"y_recv{g}"] = ((rows, width), BF16)
        buffers[f"z_send{g}"] = ((rows, width), BF16)
        buffers[f"up_recv{g}"] = ((rows, width), BF16)
        buffers[f"down_recv{g}"] = ((rows, width), BF16)
        buffers[f"final{g}"] = ((chunk, width), BF16)
    semaphores = dict(
        local=(4,),
        qx=(3,),
        qz=(3,),
        qc=(2, 3),
        dt=(3,),
        wx=(5,),
        wy=(4,),
        wz=(4,),
        wc=(13,),
        ex=(5,),
        tp=(3,),
        a2a=(3, 3),
        halo_f=(2, 2),
        halo_b=(2,),
        core=(4,),
        xs=(planes,),
        ys=(2, planes),
        up=(3, planes),
        down=(3, planes),
        gu=(3, planes),
        gd=(3, planes),
        gy=(3, planes),
        gc=(3, planes),
        gf=(3, planes),
        sm=(2 + steps,),
    )
    return buffers, semaphores


ARGS = ["tokens", "doc_ids", "w_qkv", "b_query", "b_value", "w_out", "b_out", "ln1_gain"]
ARGS += ["ln1_bias", "w_in", "b_in", "w_back", "b_back", "ln2_gain", "ln2_bias", "d_out"]
RESULTS = ["result", "d_tokens", "sums0", "sums1", "sums2", "small"]


def layer_kernel(planes, names, sem_names, *refs):
    split = len(ARGS) + len(RESULTS) + len(names)
    b = types.SimpleNamespace(**dict(zip(ARGS + RESULTS + names, refs[:split])))
    pairs = refs[split:]
    s = types.SimpleNamespace(
        **{n: (pairs[2 * i], pairs[2 * i + 1]) for i, n in enumerate(sem_names)}
    )
    at = Place(planes)
    sent = []

    def start(copy):
        copy.start()
        sent.append(copy)

    def block_rows(first, i):
        return pl.ds(pl.multiple_of(first + i * BLOCK, BLOCK), BLOCK)

    b.ids[1, at.r] = jnp.broadcast_to(b.doc_ids[...].astype(F32), (8, BLOCK))
    b.tok_plane[block_rows(0, at.r), :] = b.tokens[0]

    @pl.when(jnp.logical_not(at.has_down))
    def _():
        b.kv[pl.ds(0, PLANE), :] = jnp.zeros((PLANE, 2 * LANES), BF16)
        b.ids[0] = jnp.full((GROUP, 8, BLOCK), -1.0, F32)

    @pl.when(jnp.logical_not(at.has_up))
    def _():
        b.kv[pl.ds(2 * PLANE, PLANE), :] = jnp.zeros((PLANE, 2 * LANES), BF16)
        b.ids[2] = jnp.full((GROUP, 8, BLOCK), -1.0, F32)

    vectors = [b.b_query, b.b_value, b.b_out, b.ln1_gain, b.ln1_bias]
    lines = [v[...].astype(F32).reshape(1, HALF) for v in vectors]
    lines += [
        b.b_in[pl.ds(i * HALF, HALF)].astype(F32).reshape(1, HALF) for i in range(4)
    ]
    lines += [
        v[...].astype(F32).reshape(1, HALF) for v in (b.b_back, b.ln2_gain, b.ln2_bias)
    ]
    lines.append(jnp.zeros((4, HALF), F32))
    packed_bias = jnp.concatenate(lines, axis=0).astype(BF16)
    b.bias_own[...] = packed_bias
    b.bias2[at.x] = packed_bias
    greet(at)

    shards = (b.w_qkv, b.w_out, b.w_in, b.w_back)
    wholes = (b.wq, b.wo, b.wi, b.wb)
    direct = (True, True, True, False)
    own_q = at.y * 2 + at.parity
    diag_q = (1 - at.y) * 2 + (1 - at.parity)
    beside_q = (1 - at.y) * 2 + at.parity
    pair_q = at.y * 2 + (1 - at.parity)

    def rows(w, quarter, core):
        eighth = shards[w].shape[0] // 8
        return pl.multiple_of((quarter * 2 + core) * eighth, 16), eighth

    def far(w, quarter, core, part=None):
        first, size = rows(w, quarter, core)
        base = (1 - at.x) * shards[w].shape[0]
        lines = pl.ds(pl.multiple_of(base + first, 16), size)
        if part is None:
            return wholes[w].at[lines]
        width = shards[w].shape[1] // 2
        return wholes[w].at[lines, pl.ds(part * width, width)]

    def across_copy(w, i):
        first, size = rows(w, (own_q, diag_q)[i], at.k)
        base = at.x * shards[w].shape[0]
        return remote(
            shards[w].at[pl.ds(first, size)],
            wholes[w].at[pl.ds(pl.multiple_of(base + first, 16), size)],
            s.wx,
            2 * (w - 1) + i,
            at.across,
        )

    def piece_copy(w, quarter, sems, index, device, part=None, core=None):
        piece = far(w, quarter, at.k if core is None else core, part)
        if sems is s.wx:
            slot = 2 * (w - 1) + index
        elif sems is s.wc:
            slot = 12 if index == 4 else 4 * (w - 1) + index
        else:
            slot = 3 if index else w - 1
        return remote(piece, piece, sems, slot, device)

    def relay_own(w):
        piece_copy(w, own_q, s.wx, 0, at.across).wait_recv()
        start(piece_copy(w, own_q, s.wy, 0, at.beside))
        start(piece_copy(w, own_q, s.wz, 0, at.pair))
        start(piece_copy(w, own_q, s.wc, 0, at.sister))

    def relay_rest(w):
        if direct[w]:
            piece_copy(w, diag_q, s.wx, 1, at.across).wait_recv()
            start(piece_copy(w, diag_q, s.wc, 1, at.sister))
        piece_copy(w, beside_q, s.wy, 0, at.beside).wait_recv()
        if not direct[w]:
            start(piece_copy(w, beside_q, s.wz, 1, at.pair, part=1))
        start(piece_copy(w, beside_q, s.wc, 2, at.sister))
        piece_copy(w, pair_q, s.wz, 0, at.pair).wait_recv()
        if not direct[w]:
            start(piece_copy(w, pair_q, s.wy, 1, at.beside, part=0))
        start(piece_copy(w, pair_q, s.wc, 3, at.sister))

    def relay_diagonal(w):
        piece_copy(w, diag_q, s.wy, 1, at.beside, part=0).wait_recv()
        start(piece_copy(w, diag_q, s.wc, 1, at.sister, part=0))
        piece_copy(w, diag_q, s.wz, 1, at.pair, part=1).wait_recv()
        start(piece_copy(w, diag_q, s.wc, 4, at.sister, part=1))

    def sister_arrivals(w):
        other = 1 - at.k
        piece_copy(w, own_q, s.wc, 0, at.sister, core=other).wait_recv()
        piece_copy(w, beside_q, s.wc, 2, at.sister, core=other).wait_recv()
        piece_copy(w, pair_q, s.wc, 3, at.sister, core=other).wait_recv()
        if direct[w]:
            piece_copy(w, diag_q, s.wc, 1, at.sister, core=other).wait_recv()
        else:
            piece_copy(w, diag_q, s.wc, 1, at.sister, part=0, core=other).wait_recv()
            piece_copy(w, diag_q, s.wc, 4, at.sister, part=1, core=other).wait_recv()

    near_tokens = pl.ds(0, BLOCK)
    far_tokens = pl.ds(BLOCK, BLOCK)
    bias_copy = remote(b.bias_own, b.bias2.at[at.x], s.ex, 0, at.across)
    tok_copy = remote(b.tokens.at[0], b.tok2.at[far_tokens], s.ex, 1, at.across)
    dout_copy = remote(b.d_out.at[0], b.dout_far, s.ex, 2, at.across)
    def q_piece(ref, first_row, size, j, side):
        return ref.at[
            pl.ds(pl.multiple_of(first_row, 16), size),
            pl.ds(pl.multiple_of(j * MODEL + side * HALF, 128), HALF),
        ]

    def q_rows(core, parity):
        return (core * 2 + parity) * QUARTER

    far_base = (1 - at.x) * HALF
    near_base = at.x * HALF

    def q_across(j):
        line = q_rows(at.k, at.parity)
        return remote(
            q_piece(b.w_qkv, line, QUARTER, j, at.y),
            q_piece(b.wq, near_base + line, QUARTER, j, at.y),
            s.qx,
            j,
            at.across,
        )

    def q_move(core, parity, j, sems, index, device):
        piece = q_piece(b.wq, far_base + q_rows(core, parity), QUARTER, j, at.y)
        return remote(piece, piece, sems, index, device)

    def tok_block(i, sem, device):
        piece = b.tok_plane.at[block_rows(0, i)]
        return remote(piece, piece, s.tp, sem, device)

    own_copies = []
    for w in range(4):
        size = shards[w].shape[0]
        own_copies.append(
            pltpu.make_async_copy(
                shards[w],
                wholes[w].at[pl.ds(pl.multiple_of(at.x * size, 16), size)],
                s.local[0].at[w],
            )
        )
    for j in range(3):
        start(q_across(j))
    start(bias_copy)
    start(tok_block(at.r, 0, at.beside))
    start(tok_block(at.r, 1, at.sister))
    own_copies[0].start()
    for d in (1, 2, 3):
        mine = b.ids.at[1, at.r]
        start(remote(mine, mine, s.a2a, (0, d - 1), at.in_plane(at.peer(d))))

    near_rows = pl.multiple_of(at.x * HALF, HALF)
    far_rows = pl.multiple_of((1 - at.x) * HALF, HALF)
    b.tok2[near_tokens, :] = b.tokens[0]
    for j in range(3):
        q_move(at.k, at.parity, j, s.qx, j, at.across).wait_recv()
        start(q_move(at.k, at.parity, j, s.qz, j, at.pair))
        start(q_move(at.k, at.parity, j, s.qc, (0, j), at.sister))
    start(across_copy(2, 0))
    for i in range(2):
        start(across_copy(1, i))
    start(across_copy(3, 0))
    start(across_copy(2, 1))
    start(tok_copy)
    for w in (1, 2, 3):
        own_copies[w].start()
    tok_block(at.peer(2), 0, at.beside).wait_recv()
    start(tok_block(at.peer(2), 2, at.sister))
    for j in range(3):
        q_move(at.k, 1 - at.parity, j, s.qz, j, at.pair).wait_recv()
        start(q_move(at.k, 1 - at.parity, j, s.qc, (1, j), at.sister))
    tok_block(at.peer(1), 1, at.sister).wait_recv()
    tok_block(at.peer(3), 2, at.sister).wait_recv()
    own_copies[0].wait()
    window = [
        pl.ds(pl.multiple_of(j * MODEL + at.y * HALF + at.k * 128, 128), 256) for j in range(3)
    ]
    for j in range(3):
        b.acc[:, j * 256 : (j + 1) * 256] = jnp.dot(
            b.tok_plane[:, pl.ds(near_rows, HALF)],
            b.wq[pl.ds(near_rows, HALF), window[j]],
            preferred_element_type=F32,
        )
    remote(b.bias_own, b.bias2.at[1 - at.x], s.ex, 0, at.across).wait_recv()
    halves = (b.bias2[0].astype(F32), b.bias2[1].astype(F32))
    bias = jnp.concatenate(halves, axis=1)

    def group_bias(row):
        line = bias[row : row + 1, 0:LANES]
        for g in range(1, GROUP):
            line = jnp.where(at.r == g, bias[row : row + 1, g * LANES : (g + 1) * LANES], line)
        return line

    for j in range(3):
        q_move(1 - at.k, at.parity, j, s.qc, (0, j), at.sister).wait_recv()
        q_move(1 - at.k, 1 - at.parity, j, s.qc, (1, j), at.sister).wait_recv()
    made = []
    for j in range(3):
        part = b.acc[:, j * 256 : (j + 1) * 256] + jnp.dot(
            b.tok_plane[:, pl.ds(far_rows, HALF)],
            b.wq[pl.ds(far_rows, HALF), window[j]],
            preferred_element_type=F32,
        )
        made.append(jnp.where(at.k == 0, part[:, 0:LANES], part[:, HEAD_DIM:256]))
    b.kv[pl.ds(PLANE, PLANE), :] = jnp.concatenate(
        [made[1], made[2] + group_bias(1)], axis=1
    ).astype(BF16)

    def both_ways(up, down, act):
        @pl.when(at.has_up)
        def _():
            act(up)

        @pl.when(at.has_down)
        def _():
            act(down)

    def go(copy):
        copy.start()

    middle = b.kv.at[pl.ds(PLANE, PLANE)]
    up_kv = remote(middle, b.kv.at[pl.ds(0, PLANE)], s.halo_f, (0, 0), at.up)
    down_kv = remote(middle, b.kv.at[pl.ds(2 * PLANE, PLANE)], s.halo_f, (1, 0), at.down)
    up_ids = remote(b.ids.at[1], b.ids.at[0], s.halo_f, (0, 1), at.up)
    down_ids = remote(b.ids.at[1], b.ids.at[2], s.halo_f, (1, 1), at.down)

    def from_peer(piece, kind, d):
        remote(piece, piece, s.a2a, (kind, d - 1), at.in_plane(at.peer(d))).wait_recv()

    both_ways(up_kv, down_kv, go)
    b.qp[...] = jnp.concatenate(
        [made[0] + group_bias(0), jnp.zeros((PLANE, HEAD_DIM), F32)], axis=1
    ).astype(BF16)
    for d in (1, 2, 3):
        from_peer(b.ids.at[1, at.peer(d)], 0, d)
    both_ways(up_ids, down_ids, go)

    q_ids = jnp.concatenate([b.ids[1, j][0:1, :] for j in range(GROUP)], axis=1)
    peaks = b.peaks

    def key_ids(i):
        for j in range(GROUP):
            b.k_ids[(i * GROUP + j) * BLOCK : (i * GROUP + j + 1) * BLOCK, :] = column_of(
                b.ids[i, j][0:1, :]
            )

    def attend(i):
        key_ids(i)
        span = pl.ds(i * PLANE, PLANE)
        same = b.k_ids[span, 0:1] == q_ids
        for h in range(GROUP_HEADS):
            q = b.qp[...] * SCALE
            q = jnp.where(lane_head((PLANE, 256), 0) == h, q, jnp.zeros_like(q))
            score = lax.dot_general(b.kv[span, 0:256], q, NT, preferred_element_type=F32)
            score = jnp.where(same, score, NEGATIVE)
            peak = jnp.max(score, axis=0, keepdims=True)
            if i != 1:
                old = peaks[h][0:1, :]
                peak = jnp.maximum(peak, old)
                factor = jnp.exp(old - peak)
            weight = jnp.exp(score - peak)
            summed = jnp.sum(weight, axis=0, keepdims=True)
            first_lane, line = ((128, HEAD_DIM), (256, 0), (256, HEAD_DIM))[h]
            out = lax.dot_general(
                b.kv[span, first_lane : first_lane + 128],
                weight.astype(BF16),
                TN,
                preferred_element_type=F32,
            )[line : line + HEAD_DIM, :]
            if i != 1:
                out = out + b.out_t[h] * factor
                summed = summed + peaks[GROUP_HEADS + h][0:1, :] * factor
            b.out_t[h] = out
            peaks[h] = jnp.broadcast_to(peak, (8, PLANE))
            peaks[GROUP_HEADS + h] = jnp.broadcast_to(summed, (8, PLANE))

    relay_own(2)
    attend(1)
    relay_own(1)

    @pl.when(at.has_down)
    def _():
        came = b.kv.at[pl.ds(0, PLANE)]
        remote(came, came, s.halo_f, (0, 0), at.down).wait_recv()
        remote(b.ids.at[0], b.ids.at[0], s.halo_f, (0, 1), at.down).wait_recv()

    attend(0)

    @pl.when(at.has_up)
    def _():
        came = b.kv.at[pl.ds(2 * PLANE, PLANE)]
        remote(came, came, s.halo_f, (1, 0), at.up).wait_recv()
        remote(b.ids.at[2], b.ids.at[2], s.halo_f, (1, 1), at.up).wait_recv()

    attend(2)
    outs = [jnp.zeros((HEAD_DIM, PLANE), F32)]
    for h in range(GROUP_HEADS):
        summed = peaks[GROUP_HEADS + h][0:1, :]
        out = b.out_t[h] / summed
        b.out_t[h] = out
        b.stats[h] = peaks[h] + jnp.log(peaks[GROUP_HEADS + h])
        outs.append(out)
    attended = jnp.concatenate(outs, axis=0).T.astype(BF16)
    for i in range(GROUP):
        b.asend[i] = attended[i * BLOCK : (i + 1) * BLOCK, :]

    for d in (1, 2, 3):
        i = at.peer(d)
        start(remote(b.asend.at[i], b.arecv.at[at.r], s.a2a, (1, d - 1), at.in_plane(i)))
    b.arecv[at.r] = b.asend[at.r]
    relay_own(3)
    relay_rest(1)
    relay_rest(2)
    for d in (1, 2, 3):
        from_peer(b.arecv.at[at.peer(d)], 1, d)
    b.att2[near_tokens, :] = jnp.concatenate(
        [b.arecv[g].astype(F32)[:, HEAD_DIM : HEAD_DIM + LANES] for g in range(GROUP)], axis=1
    ).astype(BF16)
    att_copy = remote(b.att2.at[near_tokens], b.att2.at[far_tokens], s.ex, 3, at.across)
    start(att_copy)
    start(dout_copy)
    for w in (1, 2):
        own_copies[w].wait()
        sister_arrivals(w)

    def normalise(hidden):
        center = hidden - jnp.mean(hidden, -1, keepdims=True)
        inverse = lax.rsqrt(jnp.mean(center * center, -1, keepdims=True) + EPSILON)
        return center * inverse, inverse

    def norm_back(upstream, unit, inverse, gain):
        scaled = upstream * gain
        return inverse * (
            scaled
            - jnp.mean(scaled, -1, keepdims=True)
            - unit * jnp.mean(scaled * unit, -1, keepdims=True)
        )

    def column_sum(value):
        return jnp.sum(value, axis=0, keepdims=True)

    def dense_forward(side):
        lines = (near_tokens, far_tokens)[side]
        first = (
            b.tok2[lines, :].astype(F32)
            + jnp.dot(b.att2[lines, :], b.wo[...], preferred_element_type=F32)
            + bias[2:3]
        )
        unit, inverse = normalise(first)
        b.unit_one[lines, :] = unit
        normed = unit * bias[3:4] + bias[4:5]
        b.norm_low[lines, :] = normed.astype(BF16)
        b.second[lines, :] = normed + bias[9:10]
        for c in range(4):
            if side == 1 and c == 2:
                relay_diagonal(3)
            cols = slice(c * MODEL, (c + 1) * MODEL)
            part = halves[c // 2]
            i = 5 + 2 * (c % 2)
            line = jnp.concatenate([part[i : i + 1], part[i + 1 : i + 2]], axis=1)
            inner = line + jnp.dot(
                b.norm_low[lines, :], b.wi[:, cols], preferred_element_type=F32
            )
            gate = 0.5 * (1.0 + lax.erf(inner * ROOT_HALF))
            b.act[lines, cols] = (inner * gate).astype(BF16)
            b.slope[pl.ds(c * BOTH + side * BLOCK, BLOCK), :] = (
                gate + inner * jnp.exp(-0.5 * inner * inner) * INV_ROOT_TAU
            )
        return inverse

    near_inverse = dense_forward(0)
    relay_rest(3)
    tok_copy.wait_recv()
    att_copy.wait_recv()
    inverse_one = jnp.concatenate([near_inverse, dense_forward(1)], axis=0)
    own_copies[3].wait()
    sister_arrivals(3)
    b.second[...] += jnp.dot(b.act[...], b.wb[...], preferred_element_type=F32)
    unit_two, inverse_two = normalise(b.second[...])
    b.result[...] = (unit_two[:BLOCK] * bias[10:11] + bias[11:12]).astype(BF16)
    dout_copy.wait_recv()
    upstream = jnp.concatenate([b.d_out[0], b.dout_far[...]], axis=0).astype(F32)
    b.small[...] = jnp.zeros_like(b.small)
    b.small[10:11, :] = column_sum(upstream * unit_two)
    b.small[11:12, :] = column_sum(upstream)
    d_second = norm_back(upstream, unit_two, inverse_two, bias[10:11])
    b.small[9:10, :] = column_sum(d_second)
    b.d_second[...] = d_second.astype(BF16)
    b.second[...] = d_second

    chunks = [chunk_of(rows, planes) for rows in SET_ROWS]
    owners = [rows // chunk for rows, chunk in zip(SET_ROWS, chunks)]

    def of(name, group):
        return getattr(b, f"{name}{group}")

    def tile(group, t):
        if group == 0:
            lanes = pl.multiple_of(at.x * (TILES * HALF) + t * HALF, 128)
            left, right = b.act[:, pl.ds(lanes, HALF)], b.d_second[...]
        else:
            left = b.norm_low[:, pl.ds(near_rows, HALF)]
            right = b.d_inner[:, pl.ds(pl.multiple_of(t * MODEL, 128), MODEL)]
        return lax.dot_general(left, right, TN, preferred_element_type=F32)

    def out_quarter(t):
        return b.out_tile[pl.ds(pl.multiple_of(t * QUARTER, 16), QUARTER), :]

    def chunk_rows(group, j, size=None):
        return pl.ds(pl.multiple_of(j * chunks[group], 16), size or chunks[group])

    def trimmed(group, j, act):
        size, last = chunks[group], owners[group] - 1
        used = HALF + QUARTER - last * size
        if group != 1 or not 0 < used < size:
            act(size)
            return

        @pl.when(j == last)
        def _():
            act(used)

        @pl.when(j != last)
        def _():
            act(size)

    def own_chunk(group, j):
        if group == 2:
            return b.q_sum.at[chunk_rows(2, j)]
        first_row = OWN_ROWS[group] + j * chunks[group]
        return b.slope.at[pl.ds(pl.multiple_of(first_row, 16), chunks[group])]

    def core_copy(group, i):
        return remote(
            of("core_send", group).at[i],
            of("core_recv", group).at[i],
            s.core,
            group * 2 + i,
            at.sister,
        )

    def y_copy(group, j, size):
        lines = chunk_rows(group, j, size)
        return remote(
            of("y_send", group).at[lines],
            of("y_recv", group).at[lines],
            s.ys,
            (group, j),
            at.beside,
        )

    def up_copy(group, j, size):
        lines = chunk_rows(group, j, size)
        return remote(
            of("z_send", group).at[lines],
            of("up_recv", group).at[lines],
            s.up,
            (group, j),
            at.up,
        )

    def down_copy(group, j, size):
        lines = chunk_rows(group, j, size)
        return remote(
            of("z_send", group).at[lines],
            of("down_recv", group).at[lines],
            s.down,
            (group, j),
            at.down,
        )

    middle_step = planes // 2 + 1
    early, late = (1, middle_step), (middle_step, planes + 1)
    whole_way = (1, planes + 1)

    def each_owner(group, act, span):
        def one(d, carry):
            j = jnp.where(at.p < planes // 2, planes - d, d - 1)

            @pl.when(j < owners[group])
            def _():
                act(j)

            return carry

        lax.fori_loop(*span, one, 0)

    def make(group):
        base = OWN_ROWS[group]
        for i, t in enumerate((at.peer(3), at.peer(1))):
            of("core_send", group)[i, 0:HALF, :] = tile(group, t).astype(BF16)
            if group == 1:
                of("core_send", group)[i, HALF : HALF + QUARTER, :] = out_quarter(t).astype(BF16)
            start(core_copy(group, i))
        b.slope[base : base + HALF, :] = tile(group, at.r)
        if group == 1:
            b.slope[base + HALF : base + HALF + QUARTER, :] = out_quarter(at.r)

    def go_trimmed(group, span):
        def act(j):
            trimmed(group, j, lambda size: y_copy(group, j, size).start())

        each_owner(group, act, span)

    def exchange(group):
        base = OWN_ROWS[group]
        passing = tile(group, at.peer(2))
        core_copy(group, 0).wait_recv()
        come = of("core_recv", group)
        of("y_send", group)[0:HALF, :] = (passing + come[0, 0:HALF, :].astype(F32)).astype(BF16)
        if group == 1:
            lines = slice(HALF, HALF + QUARTER)
            b.y_send1[HALF + QUARTER :, :] = jnp.zeros((BLOCK - QUARTER, MODEL), BF16)
            of("y_send", group)[lines, :] = (
                out_quarter(at.peer(2)) + come[0, lines, :].astype(F32)
            ).astype(BF16)
        go_trimmed(group, (1, 2) if group == 0 else early)
        core_copy(group, 1).wait_recv()
        used = SET_ROWS[0] if group == 0 else HALF + QUARTER
        b.slope[base : base + used, :] += come[1, 0:used, :].astype(F32)

    def scatter(group, span):
        def act(j):
            mine = own_chunk(group, j)
            if group == 2:
                x_copy(j).wait_recv()
                came = b.x_recv[chunk_rows(2, j), :]
            else:
                trimmed(group, j, lambda size: y_copy(group, j, size).wait_recv())
                came = of("y_recv", group)[chunk_rows(group, j), :]
            total = mine[...] + came.astype(F32)
            mine[...] = total

            @pl.when(jnp.logical_and(at.p == 0, j > 0))
            def _():
                of("z_send", group)[chunk_rows(group, j), :] = total.astype(BF16)
                trimmed(group, j, lambda size: up_copy(group, j, size).start())

            @pl.when(jnp.logical_and(at.p == planes - 1, j < planes - 1))
            def _():
                of("z_send", group)[chunk_rows(group, j), :] = total.astype(BF16)
                trimmed(group, j, lambda size: down_copy(group, j, size).start())

        each_owner(group, act, span)

    def add_arrived(group, j, name, sems, device):
        def wait(size):
            came = of(name, group).at[chunk_rows(group, j, size)]
            remote(came, came, sems, (group, j), device).wait_recv()

        trimmed(group, j, wait)
        return of(name, group)[chunk_rows(group, j), :].astype(F32)

    def relay_sums(group, h):
        @pl.when(at.p == h)
        def _():
            def one(i, carry):
                j = owners[group] - 1 - i
                total = own_chunk(group, j)[...] + add_arrived(
                    group, j, "up_recv", s.up, at.down
                )
                of("z_send", group)[chunk_rows(group, j), :] = total.astype(BF16)
                trimmed(group, j, lambda size: up_copy(group, j, size).start())
                return carry

            lax.fori_loop(0, owners[group] - 1 - at.p, one, 0)

        @pl.when(at.p == planes - 1 - h)
        def _():
            def one(j, carry):
                total = own_chunk(group, j)[...] + add_arrived(
                    group, j, "down_recv", s.down, at.up
                )
                of("z_send", group)[chunk_rows(group, j), :] = total.astype(BF16)
                trimmed(group, j, lambda size: down_copy(group, j, size).start())
                return carry

            lax.fori_loop(0, jnp.minimum(at.p, owners[group]), one, 0)

    def x_copy(j):
        lines = chunk_rows(2, j)
        return remote(b.x_send.at[lines], b.x_recv.at[lines], s.xs, j, at.across)

    def more_sums(group):
        def one(h, carry):
            relay_sums(group, h)
            return carry

        lax.fori_loop(3, planes - 1, one, 0)

    def place(group, t, j, size=None):
        first_row = t * SET_ROWS[group] + j * chunks[group]
        lines = pl.ds(pl.multiple_of(first_row, 16), size or chunks[group])
        return of("sums", group).at[lines]

    def gather_copy(group, t, j, sems, device, source=None, size=None):
        piece = place(group, t, j, size)
        if source is None:
            source = piece
        elif size is not None:
            source = source.at[pl.ds(0, size)]
        return remote(source, piece, sems, (group, j), device)

    def linked(group, t, j, sems, device, source=None):
        def copy(size):
            return gather_copy(group, t, j, sems, device, source, size)

        return types.SimpleNamespace(
            start=lambda: trimmed(group, j, lambda size: copy(size).start()),
            wait_recv=lambda: trimmed(group, j, lambda size: copy(size).wait_recv()),
            wait_send=lambda: trimmed(group, j, lambda size: copy(size).wait_send()),
        )

    def spread(group, j, source=None):
        @pl.when(jnp.logical_and(j <= at.p, at.has_up))
        def _():
            linked(group, at.r, j, s.gu, at.up, source).start()

        @pl.when(jnp.logical_and(j >= at.p, at.has_down))
        def _():
            linked(group, at.r, j, s.gd, at.down, source).start()

        linked(group, at.r, j, s.gy, at.beside, source).start()
        gather_copy(group, at.r, j, s.gc, at.sister, source).start()

    def settle_copy(group):
        return pltpu.make_async_copy(
            of("final", group), place(group, at.r, at.p), s.local[1].at[group]
        )

    def settle(group):
        @pl.when(at.p < owners[group])
        def _():
            mine = own_chunk(group, at.p)

            @pl.when(at.has_down)
            def _():
                mine[...] += add_arrived(group, at.p, "up_recv", s.up, at.down)

            @pl.when(at.has_up)
            def _():
                mine[...] += add_arrived(group, at.p, "down_recv", s.down, at.up)

            total = mine[...]
            of("final", group)[...] = total.astype(BF16)
            spread(group, at.p, of("final", group))
            settle_copy(group).start()

    def around(group, d, act):
        @pl.when(jnp.logical_and(at.p - d >= 0, at.p - d < owners[group]))
        def _():
            act(at.p - d, s.gu, at.down)

        @pl.when(jnp.logical_and(d > 0, at.p + d < owners[group]))
        def _():
            act(at.p + d, s.gd, at.up)

    def come_in(group, d):
        def act(j, sems, device):
            linked(group, at.r, j, sems, device).wait_recv()
            spread(group, j)

        around(group, d, act)

    def hand_over(group, d):
        def act(j, sems, device):
            linked(group, at.peer(2), j, s.gy, at.beside).wait_recv()
            gather_copy(group, at.peer(2), j, s.gf, at.sister).start()

        around(group, d, act)

    def more_gathers():
        def one(d, carry):
            for group in range(3):
                come_in(group, d)
                hand_over(group, d)
            return carry

        lax.fori_loop(4, planes, one, 0)

    make(0)
    for c in range(4):
        if c == 2:
            exchange(0)
        cols = slice(c * MODEL, (c + 1) * MODEL)
        d_inner = (
            lax.dot_general(b.d_second[...], b.wb[cols, :], NT, preferred_element_type=F32)
            * b.slope[c * BOTH : (c + 1) * BOTH, :]
        )
        b.small[5 + c : 6 + c, :] = column_sum(d_inner)
        low = d_inner.astype(BF16)
        b.d_inner[:, cols] = low
        b.second[...] += lax.dot_general(low, b.wi[:, cols], NT, preferred_element_type=F32)
    d_normed = b.second[...]
    unit_one = b.unit_one[...]
    b.small[3:4, :] = column_sum(d_normed * unit_one)
    b.small[4:5, :] = column_sum(d_normed)
    d_first = norm_back(d_normed, unit_one, inverse_one, bias[3:4])
    b.small[2:3, :] = column_sum(d_first)
    d_first_low = d_first.astype(BF16)
    b.d_first[...] = d_first_low
    b.d_tokens[...] = d_first[:BLOCK]
    d_attn = lax.dot_general(d_first_low[:BLOCK], b.wo[...], NT, preferred_element_type=F32)
    for g in range(GROUP):
        b.dsend[g] = jnp.concatenate(
            [jnp.zeros((BLOCK, HEAD_DIM), F32), d_attn[:, g * LANES : (g + 1) * LANES]], axis=1
        ).astype(BF16)
    for d in (1, 2, 3):
        g = at.peer(d)
        start(
            remote(
                b.dsend.at[g], b.do.at[block_rows(0, at.r)], s.a2a, (2, d - 1), at.in_plane(g)
            )
        )
    go_trimmed(0, (2, planes + 1))
    b.do[block_rows(0, at.r), :] = b.dsend[at.r]

    b.out_tile[...] = lax.dot_general(
        b.att2[:, pl.ds(near_rows, HALF)], b.d_first[...], TN, preferred_element_type=F32
    )
    make(1)
    scatter(0, (1, 2))

    b.grads[...] = jnp.zeros_like(b.grads)
    b.dq[...] = jnp.zeros_like(b.dq)
    for d in (1, 2, 3):
        from_peer(b.do.at[block_rows(0, at.peer(d))], 2, d)
    do_t = b.do[...].astype(F32).T
    for h in range(GROUP_HEADS):
        lines = slice(HEAD_DIM * (h + 1), HEAD_DIM * (h + 2))
        b.stats[GROUP_HEADS + h] = jnp.broadcast_to(
            column_sum(do_t[lines, :] * b.out_t[h]), (8, PLANE)
        )

    def visit(h, i):
        span = pl.ds(i * PLANE, PLANE)
        pick_q = lane_head((PLANE, 256), 0) == h
        q = b.qp[...]
        q = jnp.where(pick_q, q, jnp.zeros_like(q))
        dout = b.do[...]
        dout = jnp.where(lane_head((PLANE, 256), 1) == h, dout, jnp.zeros_like(dout))
        keys = b.kv[span, 0:256]
        score = lax.dot_general(keys, q * SCALE, NT, preferred_element_type=F32)
        same = b.k_ids[span, 0:1] == q_ids
        prob = jnp.where(same, jnp.exp(score - b.stats[h][0:1, :]), 0.0)
        d_prob = lax.dot_general(b.kv[span, 128:384], dout, NT, preferred_element_type=F32)
        d_score = (prob * (d_prob - b.stats[GROUP_HEADS + h][0:1, :]) * SCALE).astype(BF16)
        b.grads[span, 0:256] += jnp.dot(d_score, q, preferred_element_type=F32)
        b.grads[span, 128:384] += jnp.dot(
            prob.astype(BF16), dout, preferred_element_type=F32
        )
        b.dq[...] += jnp.where(
            pick_q, lax.dot_general(d_score, keys, TN, preferred_element_type=F32), 0.0
        )

    def visit_plane(i):
        def one(h, carry):
            visit(h, i)
            return carry

        lax.fori_loop(0, GROUP_HEADS, one, 0)

    down_grads = remote(b.halo_send.at[0], b.halo.at[1], s.halo_b, 0, at.down)
    up_grads = remote(b.halo_send.at[1], b.halo.at[0], s.halo_b, 1, at.up)
    visit_plane(0)
    b.halo_send[0] = b.grads[pl.ds(0, PLANE), :].astype(BF16)

    @pl.when(at.has_down)
    def _():
        down_grads.start()

    scatter(0, (2, 3))
    exchange(1)
    visit_plane(2)
    b.halo_send[1] = b.grads[pl.ds(2 * PLANE, PLANE), :].astype(BF16)

    @pl.when(at.has_up)
    def _():
        up_grads.start()

    go_trimmed(1, late)
    scatter(0, (3, planes + 1))
    relay_sums(0, 1)
    visit_plane(1)
    b.d_group[:, 0:256] = b.dq[...].astype(BF16)

    @pl.when(at.has_up)
    def _():
        remote(b.halo.at[1], b.halo.at[1], s.halo_b, 0, at.up).wait_recv()
        b.grads[pl.ds(PLANE, PLANE), :] += b.halo[1].astype(F32)

    relay_sums(0, 2)
    scatter(1, early)

    @pl.when(at.has_down)
    def _():
        remote(b.halo.at[0], b.halo.at[0], s.halo_b, 1, at.down).wait_recv()
        b.grads[pl.ds(PLANE, PLANE), :] += b.halo[0].astype(F32)

    b.d_group[:, 256:640] = b.grads[pl.ds(PLANE, PLANE), :].astype(BF16)

    b.line_send[...] = jnp.broadcast_to(column_sum(b.d_group[...].astype(F32)), (8, 640))
    line_copy = remote(b.line_send, b.line_recv, s.ex, 4, at.across)
    start(line_copy)
    b.x_send[...] = lax.dot_general(
        b.tok_plane[:, pl.ds(far_rows, HALF)], b.d_group[...], TN, preferred_element_type=F32
    ).astype(BF16)
    each_owner(2, lambda j: x_copy(j).start(), whole_way)
    b.q_sum[...] = lax.dot_general(
        b.tok_plane[:, pl.ds(near_rows, HALF)], b.d_group[...], TN, preferred_element_type=F32
    )

    partners = [at.sister, at.beside]
    span = 1
    while span < planes:
        partners.append((at.c + GROUP * span * (1 - 2 * ((at.p // span) % 2)), at.x))
        span *= 2

    def small_copy(i):
        return remote(b.small, b.small_recv.at[i], s.sm, i, partners[i])

    def small_finish(i):
        small_copy(i).wait()
        b.small[...] += b.small_recv[i]

    def sums_sent(group):
        def one(j, carry):
            if group == 2:
                x_copy(j).wait_send()
            else:
                trimmed(group, j, lambda size: y_copy(group, j, size).wait_send())

            @pl.when(at.p < j)
            def _():
                trimmed(group, j, lambda size: up_copy(group, j, size).wait_send())

            @pl.when(at.p > j)
            def _():
                trimmed(group, j, lambda size: down_copy(group, j, size).wait_send())

            return carry

        lax.fori_loop(0, owners[group], one, 0)

        @pl.when(at.p < owners[group])
        def _():
            settle_copy(group).wait()

    def gathers_done(group):
        def one(j, carry):
            gather_copy(group, at.peer(1), j, s.gc, at.sister).wait_recv()
            gather_copy(group, at.peer(3), j, s.gf, at.sister).wait_recv()
            linked(group, at.r, j, s.gy, at.beside).wait_send()
            gather_copy(group, at.r, j, s.gc, at.sister).wait_send()
            gather_copy(group, at.peer(2), j, s.gf, at.sister).wait_send()

            @pl.when(jnp.logical_and(j <= at.p, at.has_up))
            def _():
                linked(group, at.r, j, s.gu, at.up).wait_send()

            @pl.when(jnp.logical_and(j >= at.p, at.has_down))
            def _():
                linked(group, at.r, j, s.gd, at.down).wait_send()

            return carry

        lax.fori_loop(0, owners[group], one, 0)

    def finish(copy):
        copy.wait_send()

    more_sums(0)
    settle(0)
    relay_sums(1, 1)
    line_copy.wait_recv()
    line = b.line_send[...] + b.line_recv[...]
    mine = lax.broadcasted_iota(jnp.int32, (8, 640), 0) == at.r
    b.small[16:24, 0:640] = jnp.where(mine, line, 0.0)
    small_copy(0).start()
    scatter(2, early)
    small_finish(0)
    small_copy(1).start()
    scatter(1, late)

    spare = 2 * BOTH
    gap = jnp.zeros((PLANE, HEAD_DIM), F32)
    for j, first_lane in enumerate((0, 256, 448)):
        piece = b.d_group[...].astype(F32)[:, first_lane : first_lane + LANES]
        wide = jnp.where(
            at.k == 0,
            jnp.concatenate([piece, gap], axis=1),
            jnp.concatenate([gap, piece], axis=1),
        ).astype(BF16)
        part = lax.dot_general(wide, b.wq[:, window[j]], NT, preferred_element_type=F32)
        if j == 0:
            b.slope[spare : spare + PLANE, :] = part
        else:
            b.slope[spare : spare + PLANE, :] += part

    def dt_block(i):
        return b.slope[block_rows(spare, i), :]

    def dt_copy(i):
        device = at.beside if i == 2 else at.sister
        return remote(b.dt_send.at[i], b.dt_recv.at[i], s.dt, i, device)

    for i, block in enumerate((at.peer(3), at.peer(1))):
        b.dt_send[i] = dt_block(block).astype(BF16)
        start(dt_copy(i))

    come_in(0, 1)
    relay_sums(1, 2)
    relay_sums(2, 1)
    hand_over(0, 0)
    scatter(2, late)
    relay_sums(2, 2)
    dt_copy(0).wait_recv()
    b.dt_send[2] = (dt_block(at.peer(2)) + b.dt_recv[0].astype(F32)).astype(BF16)
    start(dt_copy(2))
    more_sums(1)
    settle(1)
    come_in(0, 2)
    more_sums(2)
    settle(2)
    small_finish(1)
    small_copy(2).start()
    hand_over(0, 1)
    come_in(1, 1)
    come_in(0, 3)
    come_in(2, 1)
    for copy in sent:
        copy.wait_send()
    both_ways(up_kv, down_kv, finish)
    both_ways(up_ids, down_ids, finish)
    both_ways(up_grads, down_grads, finish)
    for group in range(3):
        sums_sent(group)
    hand_over(0, 2)
    dt_copy(1).wait_recv()
    dt_copy(2).wait_recv()
    b.d_tokens[...] += (
        dt_block(at.r) + b.dt_recv[1].astype(F32) + b.dt_recv[2].astype(F32)
    )
    come_in(1, 2)
    come_in(2, 2)
    small_finish(2)
    small_copy(3).start()
    hand_over(0, 3)
    hand_over(1, 0)
    come_in(1, 3)
    come_in(2, 3)
    hand_over(2, 0)
    hand_over(1, 1)
    if planes <= GROUP:
        gathers_done(0)
    hand_over(2, 1)
    hand_over(1, 2)
    small_finish(3)
    hand_over(2, 2)
    hand_over(1, 3)
    if planes <= GROUP:
        gathers_done(1)
    hand_over(2, 3)
    more_gathers()
    for i in range(4, len(partners)):
        small_copy(i).start()
        small_finish(i)

    if planes > GROUP:
        gathers_done(0)
        gathers_done(1)
    gathers_done(2)


def layer_call(planes, args):
    buffers, semaphores = scratch_plan(planes)
    hbm = pl.BlockSpec(memory_space=pltpu.HBM)
    vmem = pl.BlockSpec(memory_space=pltpu.VMEM)
    weights = ("w_qkv", "w_out", "w_in", "w_back")
    scratch = [pltpu.VMEM(shape, kind) for shape, kind in buffers.values()]
    for shape in semaphores.values():
        scratch += [pltpu.SemaphoreType.DMA(shape)] * 2
    return pl.pallas_call(
        functools.partial(layer_kernel, planes, list(buffers), list(semaphores)),
        out_shape=[
            jax.ShapeDtypeStruct((BLOCK, MODEL), BF16),
            jax.ShapeDtypeStruct((BLOCK, MODEL), F32),
        ]
        + [
            jax.ShapeDtypeStruct((TILES * rows, width), BF16)
            for rows, width in zip(SET_ROWS, SET_WIDTH)
        ]
        + [jax.ShapeDtypeStruct((24, MODEL), F32)],
        in_specs=[hbm if name in weights else vmem for name in ARGS],
        out_specs=[vmem, vmem, hbm, hbm, hbm, vmem],
        scratch_shapes=scratch,
        compiler_params=pltpu.CompilerParams(
            collective_id=0, has_side_effects=True, vmem_limit_bytes=60 * 2**20
        ),
        name="layer",
    )(*args)


def unpack_kernel(result_in, tokens_in, sums0, sums1, sums2, small, *refs):
    result, d_tokens, w_qkv, bq, bv, w_out, bo, g1, o1, w_in, bi, w_back, bb, g2, o2 = refs[:15]
    in0, in1, in2, out_q, out_o, out_i, out_b, come, go = refs[15:]
    loads = []
    for g, (sums, held) in enumerate(((sums0, in0), (sums1, in1), (sums2, in2))):
        for t in range(TILES):
            lines = pl.ds(t * SET_ROWS[g], SET_ROWS[g])
            loads.append(
                pltpu.make_async_copy(sums.at[lines], held.at[t], come.at[g * TILES + t])
            )
    for load in loads:
        load.start()
    stores = [
        pltpu.make_async_copy(result_in, result, go.at[14]),
        pltpu.make_async_copy(tokens_in, d_tokens, go.at[15]),
    ]
    for store in stores:
        store.start()

    def put(source, target, i):
        store = pltpu.make_async_copy(source, target, go.at[i])
        store.start()
        stores.append(store)

    x = lax.axis_index("wsh")
    half = small[0:16, pl.ds(pl.multiple_of(x * HALF, 128), HALF)]
    for ref, row in zip((bo, g1, o1, bb, g2, o2), (2, 3, 4, 9, 10, 11)):
        ref[...] = half[row, :]
    whole = jnp.where(x == 0, small[5:7, :], small[7:9, :])
    bi[pl.ds(0, MODEL)] = whole[0, :]
    bi[pl.ds(MODEL, MODEL)] = whole[1, :]
    for ref, first in ((bq, 0), (bv, 448)):
        row = jnp.concatenate(
            [small[16 + g : 17 + g, first : first + LANES] for g in range(GROUP)], axis=1
        )
        ref[...] = jnp.where(x == 0, row[:, :HALF], row[:, HALF:])[0, :]

    for t in range(TILES):
        loads[t].wait()
        lines = pl.ds(t * HALF, HALF)
        out_b[lines, :] = in0[t].astype(F32)
        put(out_b.at[lines], w_back.at[lines], t)
    for t in range(TILES):
        loads[TILES + t].wait()
        out_i[t] = in1[t, 0:HALF, :].astype(F32)
        put(out_i.at[t], w_in.at[:, pl.ds(t * MODEL, MODEL)], 4 + t)
        lines = pl.ds(t * QUARTER, QUARTER)
        out_o[lines, :] = in1[t, HALF : HALF + QUARTER, :].astype(F32)
        put(out_o.at[lines], w_out.at[lines], 8 + t)
    for pair in range(2):
        loads[2 * TILES + 2 * pair].wait()
        loads[2 * TILES + 2 * pair + 1].wait()
        for j, first in enumerate((0, 256, 448)):
            out_q[:, j * MODEL + pair * HALF : j * MODEL + (pair + 1) * HALF] = (
                jnp.concatenate(
                    [
                        in2[2 * pair + i].astype(F32)[:, first : first + LANES]
                        for i in range(2)
                    ],
                    axis=1,
                )
            )
    put(out_q, w_qkv, 12)
    for store in stores:
        store.wait()


def unpack_call(*arrays):
    shape = jax.ShapeDtypeStruct
    vmem = pl.BlockSpec(memory_space=pltpu.VMEM)
    hbm = pl.BlockSpec(memory_space=pltpu.HBM)
    vector = (shape((HALF,), F32), vmem)
    outs = [
        (shape((BLOCK, MODEL), BF16), hbm),
        (shape((BLOCK, MODEL), F32), hbm),
        (shape((HALF, 3 * MODEL), F32), hbm),
        vector,
        vector,
        (shape((HALF, MODEL), F32), hbm),
        vector,
        vector,
        vector,
        (shape((HALF, FF), F32), hbm),
        (shape((FF // 2,), F32), vmem),
        (shape((FF // 2, MODEL), F32), hbm),
        vector,
        vector,
        vector,
    ]
    return pl.pallas_call(
        unpack_kernel,
        out_shape=[o[0] for o in outs],
        in_specs=[vmem, vmem, hbm, hbm, hbm, vmem],
        out_specs=[o[1] for o in outs],
        scratch_shapes=[
            pltpu.VMEM((TILES, rows, width), BF16)
            for rows, width in zip(SET_ROWS, SET_WIDTH)
        ]
        + [
            pltpu.VMEM((HALF, 3 * MODEL), F32),
            pltpu.VMEM((HALF, MODEL), F32),
            pltpu.VMEM((TILES, HALF, MODEL), F32),
            pltpu.VMEM((FF // 2, MODEL), F32),
            pltpu.SemaphoreType.DMA((3 * TILES,)),
            pltpu.SemaphoreType.DMA((16,)),
        ],
        compiler_params=pltpu.CompilerParams(vmem_limit_bytes=60 * 2**20),
        name="unpack",
    )(*arrays)


def body(*args):
    planes = lax.axis_size("ctx") // GROUP
    result, d_tokens, *rest = unpack_call(*layer_call(planes, args))
    return (result[None], d_tokens[None], *rest)


def solution(mesh):
    token_spec = P("wsh", "ctx", None)
    matrix, vector = P("wsh", None), P("wsh")
    in_specs = (
        token_spec,
        P("wsh", "ctx"),
        matrix,
        vector,
        vector,
        matrix,
        vector,
        vector,
        vector,
        matrix,
        vector,
        matrix,
        vector,
        vector,
        vector,
        token_spec,
    )
    out_specs = (
        token_spec,
        token_spec,
        matrix,
        vector,
        vector,
        matrix,
        vector,
        vector,
        vector,
        matrix,
        vector,
        matrix,
        vector,
        vector,
        vector,
    )
    return jax.shard_map(body, mesh=mesh, in_specs=in_specs, out_specs=out_specs, check_vma=False)
```

```python
import functools
import types

import jax
import jax.numpy as jnp
from jax import lax
from jax.experimental import pallas as pl
from jax.experimental.pallas import tpu as pltpu
from jax.sharding import PartitionSpec as P

HEAD_DIM = 64
GROUP = 4
GROUP_HEADS = 3
BLOCK = 128
PLANE = GROUP * BLOCK
MODEL = 768
FF = 3072
HALF = MODEL // 2
LANES = GROUP_HEADS * HEAD_DIM
TILES = 4
OWN_ROWS = (4 * 2 * BLOCK, 0)
BOTH = 2 * BLOCK
EPSILON = 1e-05
NEGATIVE = -1e30
ROOT_HALF = 0.7071067811865476
INV_ROOT_TAU = 0.3989422804014327
SCALE = HEAD_DIM**-0.5
MESH = pl.DeviceIdType.MESH
F32 = jnp.float32
BF16 = jnp.bfloat16
NT = (((1,), (1,)), ((), ()))
TN = (((0,), (0,)), ((), ()))


class Place:
    def __init__(self, planes):
        self.n = planes
        self.c = lax.axis_index("ctx")
        self.x = lax.axis_index("wsh")
        self.p = self.c // GROUP
        self.r = self.c % GROUP
        self.y = self.r // 2
        self.k = self.r % 2
        self.parity = self.p % 2
        self.sister = (self.c + 1 - 2 * self.k, self.x)
        self.beside = (self.c + 2 - 4 * self.y, self.x)
        self.across = (self.c, 1 - self.x)
        self.pair = (self.c + GROUP * (1 - 2 * self.parity), self.x)
        self.up = (self.c + GROUP, self.x)
        self.down = (self.c - GROUP, self.x)
        self.has_up = self.p < planes - 1
        self.has_down = self.p > 0

    def peer(self, d):
        if d == 1:
            return self.y * 2 + (1 - self.k)
        if d == 2:
            return (1 - self.y) * 2 + self.k
        return (1 - self.y) * 2 + (1 - self.k)

    def in_plane(self, position):
        return (self.p * GROUP + position, self.x)

    def plane(self, p):
        return (p * GROUP + self.r, self.x)


def signal(sem, device):
    pl.semaphore_signal(sem, inc=1, device_id=device, device_id_type=MESH)


def greet(at):
    barrier = pltpu.get_barrier_semaphore()
    for d in (1, 2, 3):
        signal(barrier, at.in_plane(at.peer(d)))
    signal(barrier, at.across)

    def other_plane(d, carry):
        signal(barrier, at.plane((at.p + d) % at.n))
        return carry

    lax.fori_loop(1, at.n, other_plane, 0)
    pl.semaphore_wait(barrier, 4 + at.n - 1)


def remote(src, dst, sems, index, device, recv_index=None):
    send, recv = sems
    return pltpu.make_async_remote_copy(
        src_ref=src,
        dst_ref=dst,
        send_sem=send.at[index],
        recv_sem=recv.at[index if recv_index is None else recv_index],
        device_id=device,
        device_id_type=MESH,
    )


def lane_head(shape, first):
    return lax.broadcasted_iota(jnp.int32, shape, 1) // HEAD_DIM - first


def column_of(row):
    return jnp.broadcast_to(row, (BLOCK, BLOCK)).T


def chunk_of(rows, planes):
    chunk = -(-(-(-rows // planes)) // 16) * 16
    while rows % chunk:
        chunk += 16
    return chunk


SET_ROWS = (HALF, 512, HALF)
SET_WIDTH = (MODEL, MODEL, 640)
QUARTER = HALF // GROUP


def scratch_plan(planes):
    steps = planes.bit_length() - 1
    buffers = dict(
        wq=((MODEL, 3 * MODEL), BF16),
        wo=((MODEL, MODEL), BF16),
        wi=((MODEL, FF), BF16),
        wb=((FF, MODEL), BF16),
        bias_own=((16, HALF), BF16),
        bias2=((2, 16, HALF), BF16),
        dout_far=((BLOCK, MODEL), BF16),
        ids=((3, GROUP, 8, BLOCK), F32),
        acc=((PLANE, 3 * 256), F32),
        qp=((PLANE, 256), BF16),
        kv=((3 * PLANE, 2 * LANES), BF16),
        out_t=((GROUP_HEADS, HEAD_DIM, PLANE), F32),
        peaks=((2 * GROUP_HEADS, 8, PLANE), F32),
        asend=((GROUP, BLOCK, 256), BF16),
        arecv=((GROUP, BLOCK, 256), BF16),
        tok_plane=((PLANE, MODEL), BF16),
        tok2=((BOTH, MODEL), BF16),
        att2=((BOTH, MODEL), BF16),
        unit_one=((BOTH, MODEL), F32),
        norm_low=((BOTH, MODEL), BF16),
        act=((BOTH, FF), BF16),
        d_inner=((BOTH, FF), BF16),
        d_second=((BOTH, MODEL), BF16),
        d_first=((BOTH, MODEL), BF16),
        second=((BOTH, MODEL), F32),
        slope=((4 * BOTH + HALF, MODEL), F32),
        out_tile=((HALF, MODEL), F32),
        dsend=((GROUP, BLOCK, 256), BF16),
        do=((PLANE, 256), BF16),
        grads=((3 * PLANE, 2 * LANES), F32),
        dq=((PLANE, 256), F32),
        k_ids=((3 * PLANE, BLOCK), F32),
        stats=((2 * GROUP_HEADS, 8, PLANE), F32),
        halo_send=((2, PLANE, 2 * LANES), BF16),
        halo=((2, PLANE, 2 * LANES), BF16),
        d_group=((PLANE, 640), BF16),
        dt_send=((3, BLOCK, MODEL), BF16),
        dt_recv=((3, BLOCK, MODEL), BF16),
        q_sum=((HALF, 640), F32),
        x_send=((HALF, 640), BF16),
        x_recv=((HALF, 640), BF16),
        small_recv=((2 + steps, 24, MODEL), F32),
        line_send=((8, 640), F32),
        line_recv=((8, 640), F32),
    )
    for g, (rows, width) in enumerate(zip(SET_ROWS, SET_WIDTH)):
        chunk = chunk_of(rows, planes)
        if g < 2:
            buffers[f"core_send{g}"] = ((2, rows, width), BF16)
            buffers[f"core_recv{g}"] = ((2, rows, width), BF16)
            buffers[f"y_send{g}"] = ((rows, width), BF16)
            buffers[f"y_recv{g}"] = ((rows, width), BF16)
        buffers[f"z_send{g}"] = ((rows, width), BF16)
        buffers[f"up_recv{g}"] = ((rows, width), BF16)
        buffers[f"down_recv{g}"] = ((rows, width), BF16)
        buffers[f"final{g}"] = ((chunk, width), BF16)
    semaphores = dict(
        local=(4,),
        qx=(3,),
        qz=(3,),
        qc=(2, 3),
        dt=(3,),
        wx=(5,),
        wy=(4,),
        wz=(4,),
        wc=(13,),
        ex=(5,),
        tp=(3,),
        a2a=(3, 3),
        halo_f=(2, 2),
        halo_b=(2,),
        core=(4,),
        xs=(planes,),
        ys=(2, planes),
        up=(3, planes),
        down=(3, planes),
        gu=(3, planes),
        gd=(3, planes),
        gy=(3, planes),
        gc=(3, planes),
        gf=(3, planes),
        sm=(2 + steps,),
    )
    return buffers, semaphores


ARGS = ["tokens", "doc_ids", "w_qkv", "b_query", "b_value", "w_out", "b_out", "ln1_gain"]
ARGS += ["ln1_bias", "w_in", "b_in", "w_back", "b_back", "ln2_gain", "ln2_bias", "d_out"]
RESULTS = ["result", "d_tokens", "sums0", "sums1", "sums2", "small"]


def layer_kernel(planes, names, sem_names, *refs):
    split = len(ARGS) + len(RESULTS) + len(names)
    b = types.SimpleNamespace(**dict(zip(ARGS + RESULTS + names, refs[:split])))
    pairs = refs[split:]
    s = types.SimpleNamespace(
        **{n: (pairs[2 * i], pairs[2 * i + 1]) for i, n in enumerate(sem_names)}
    )
    at = Place(planes)
    sent = []

    def start(copy):
        copy.start()
        sent.append(copy)

    def block_rows(first, i):
        return pl.ds(pl.multiple_of(first + i * BLOCK, BLOCK), BLOCK)

    b.ids[1, at.r] = jnp.broadcast_to(b.doc_ids[...].astype(F32), (8, BLOCK))
    b.tok_plane[block_rows(0, at.r), :] = b.tokens[0]

    @pl.when(jnp.logical_not(at.has_down))
    def _():
        b.kv[pl.ds(0, PLANE), :] = jnp.zeros((PLANE, 2 * LANES), BF16)
        b.ids[0] = jnp.full((GROUP, 8, BLOCK), -1.0, F32)

    @pl.when(jnp.logical_not(at.has_up))
    def _():
        b.kv[pl.ds(2 * PLANE, PLANE), :] = jnp.zeros((PLANE, 2 * LANES), BF16)
        b.ids[2] = jnp.full((GROUP, 8, BLOCK), -1.0, F32)

    vectors = [b.b_query, b.b_value, b.b_out, b.ln1_gain, b.ln1_bias]
    lines = [v[...].astype(F32).reshape(1, HALF) for v in vectors]
    lines += [
        b.b_in[pl.ds(i * HALF, HALF)].astype(F32).reshape(1, HALF) for i in range(4)
    ]
    lines += [
        v[...].astype(F32).reshape(1, HALF) for v in (b.b_back, b.ln2_gain, b.ln2_bias)
    ]
    lines.append(jnp.zeros((4, HALF), F32))
    packed_bias = jnp.concatenate(lines, axis=0).astype(BF16)
    b.bias_own[...] = packed_bias
    b.bias2[at.x] = packed_bias
    greet(at)

    shards = (b.w_qkv, b.w_out, b.w_in, b.w_back)
    wholes = (b.wq, b.wo, b.wi, b.wb)
    direct = (True, True, True, False)
    own_q = at.y * 2 + at.parity
    diag_q = (1 - at.y) * 2 + (1 - at.parity)
    beside_q = (1 - at.y) * 2 + at.parity
    pair_q = at.y * 2 + (1 - at.parity)

    def rows(w, quarter, core):
        eighth = shards[w].shape[0] // 8
        return pl.multiple_of((quarter * 2 + core) * eighth, 16), eighth

    def far(w, quarter, core, part=None):
        first, size = rows(w, quarter, core)
        base = (1 - at.x) * shards[w].shape[0]
        lines = pl.ds(pl.multiple_of(base + first, 16), size)
        if part is None:
            return wholes[w].at[lines]
        width = shards[w].shape[1] // 2
        return wholes[w].at[lines, pl.ds(part * width, width)]

    def across_copy(w, i):
        first, size = rows(w, (own_q, diag_q)[i], at.k)
        base = at.x * shards[w].shape[0]
        return remote(
            shards[w].at[pl.ds(first, size)],
            wholes[w].at[pl.ds(pl.multiple_of(base + first, 16), size)],
            s.wx,
            2 * (w - 1) + i,
            at.across,
        )

    def piece_copy(w, quarter, sems, index, device, part=None, core=None):
        piece = far(w, quarter, at.k if core is None else core, part)
        if sems is s.wx:
            slot = 2 * (w - 1) + index
        elif sems is s.wc:
            slot = 12 if index == 4 else 4 * (w - 1) + index
        else:
            slot = 3 if index else w - 1
        return remote(piece, piece, sems, slot, device)

    def relay_own(w):
        piece_copy(w, own_q, s.wx, 0, at.across).wait_recv()
        start(piece_copy(w, own_q, s.wy, 0, at.beside))
        start(piece_copy(w, own_q, s.wz, 0, at.pair))
        start(piece_copy(w, own_q, s.wc, 0, at.sister))

    def relay_rest(w):
        if direct[w]:
            piece_copy(w, diag_q, s.wx, 1, at.across).wait_recv()
            start(piece_copy(w, diag_q, s.wc, 1, at.sister))
        piece_copy(w, beside_q, s.wy, 0, at.beside).wait_recv()
        if not direct[w]:
            start(piece_copy(w, beside_q, s.wz, 1, at.pair, part=1))
        start(piece_copy(w, beside_q, s.wc, 2, at.sister))
        piece_copy(w, pair_q, s.wz, 0, at.pair).wait_recv()
        if not direct[w]:
            start(piece_copy(w, pair_q, s.wy, 1, at.beside, part=0))
        start(piece_copy(w, pair_q, s.wc, 3, at.sister))

    def relay_diagonal(w):
        piece_copy(w, diag_q, s.wy, 1, at.beside, part=0).wait_recv()
        start(piece_copy(w, diag_q, s.wc, 1, at.sister, part=0))
        piece_copy(w, diag_q, s.wz, 1, at.pair, part=1).wait_recv()
        start(piece_copy(w, diag_q, s.wc, 4, at.sister, part=1))

    def sister_arrivals(w):
        other = 1 - at.k
        piece_copy(w, own_q, s.wc, 0, at.sister, core=other).wait_recv()
        piece_copy(w, beside_q, s.wc, 2, at.sister, core=other).wait_recv()
        piece_copy(w, pair_q, s.wc, 3, at.sister, core=other).wait_recv()
        if direct[w]:
            piece_copy(w, diag_q, s.wc, 1, at.sister, core=other).wait_recv()
        else:
            piece_copy(w, diag_q, s.wc, 1, at.sister, part=0, core=other).wait_recv()
            piece_copy(w, diag_q, s.wc, 4, at.sister, part=1, core=other).wait_recv()

    near_tokens = pl.ds(0, BLOCK)
    far_tokens = pl.ds(BLOCK, BLOCK)
    bias_copy = remote(b.bias_own, b.bias2.at[at.x], s.ex, 0, at.across)
    tok_copy = remote(b.tokens.at[0], b.tok2.at[far_tokens], s.ex, 1, at.across)
    dout_copy = remote(b.d_out.at[0], b.dout_far, s.ex, 2, at.across)
    def q_piece(ref, first_row, size, j, side):
        return ref.at[
            pl.ds(pl.multiple_of(first_row, 16), size),
            pl.ds(pl.multiple_of(j * MODEL + side * HALF, 128), HALF),
        ]

    def q_rows(core, parity):
        return (core * 2 + parity) * QUARTER

    far_base = (1 - at.x) * HALF
    near_base = at.x * HALF

    def q_across(j):
        line = q_rows(at.k, at.parity)
        return remote(
            q_piece(b.w_qkv, line, QUARTER, j, at.y),
            q_piece(b.wq, near_base + line, QUARTER, j, at.y),
            s.qx,
            j,
            at.across,
        )

    def q_move(core, parity, j, sems, index, device):
        piece = q_piece(b.wq, far_base + q_rows(core, parity), QUARTER, j, at.y)
        return remote(piece, piece, sems, index, device)

    def tok_block(i, sem, device):
        piece = b.tok_plane.at[block_rows(0, i)]
        return remote(piece, piece, s.tp, sem, device)

    own_copies = []
    for w in range(4):
        size = shards[w].shape[0]
        own_copies.append(
            pltpu.make_async_copy(
                shards[w],
                wholes[w].at[pl.ds(pl.multiple_of(at.x * size, 16), size)],
                s.local[0].at[w],
            )
        )
    for j in range(3):
        start(q_across(j))
    start(bias_copy)
    start(tok_block(at.r, 0, at.beside))
    start(tok_block(at.r, 1, at.sister))
    own_copies[0].start()
    for d in (1, 2, 3):
        mine = b.ids.at[1, at.r]
        start(remote(mine, mine, s.a2a, (0, d - 1), at.in_plane(at.peer(d))))

    near_rows = pl.multiple_of(at.x * HALF, HALF)
    far_rows = pl.multiple_of((1 - at.x) * HALF, HALF)
    b.tok2[near_tokens, :] = b.tokens[0]
    for j in range(3):
        q_move(at.k, at.parity, j, s.qx, j, at.across).wait_recv()
        start(q_move(at.k, at.parity, j, s.qz, j, at.pair))
        start(q_move(at.k, at.parity, j, s.qc, (0, j), at.sister))
    start(across_copy(2, 0))
    for i in range(2):
        start(across_copy(1, i))
    start(across_copy(3, 0))
    start(across_copy(2, 1))
    start(tok_copy)
    for w in (1, 2, 3):
        own_copies[w].start()
    tok_block(at.peer(2), 0, at.beside).wait_recv()
    start(tok_block(at.peer(2), 2, at.sister))
    for j in range(3):
        q_move(at.k, 1 - at.parity, j, s.qz, j, at.pair).wait_recv()
        start(q_move(at.k, 1 - at.parity, j, s.qc, (1, j), at.sister))
    tok_block(at.peer(1), 1, at.sister).wait_recv()
    tok_block(at.peer(3), 2, at.sister).wait_recv()
    own_copies[0].wait()
    window = [
        pl.ds(pl.multiple_of(j * MODEL + at.y * HALF + at.k * 128, 128), 256) for j in range(3)
    ]
    for j in range(3):
        b.acc[:, j * 256 : (j + 1) * 256] = jnp.dot(
            b.tok_plane[:, pl.ds(near_rows, HALF)],
            b.wq[pl.ds(near_rows, HALF), window[j]],
            preferred_element_type=F32,
        )
    remote(b.bias_own, b.bias2.at[1 - at.x], s.ex, 0, at.across).wait_recv()
    halves = (b.bias2[0].astype(F32), b.bias2[1].astype(F32))
    bias = jnp.concatenate(halves, axis=1)

    def group_bias(row):
        line = bias[row : row + 1, 0:LANES]
        for g in range(1, GROUP):
            line = jnp.where(at.r == g, bias[row : row + 1, g * LANES : (g + 1) * LANES], line)
        return line

    for j in range(3):
        q_move(1 - at.k, at.parity, j, s.qc, (0, j), at.sister).wait_recv()
        q_move(1 - at.k, 1 - at.parity, j, s.qc, (1, j), at.sister).wait_recv()
    made = []
    for j in range(3):
        part = b.acc[:, j * 256 : (j + 1) * 256] + jnp.dot(
            b.tok_plane[:, pl.ds(far_rows, HALF)],
            b.wq[pl.ds(far_rows, HALF), window[j]],
            preferred_element_type=F32,
        )
        made.append(jnp.where(at.k == 0, part[:, 0:LANES], part[:, HEAD_DIM:256]))
    b.kv[pl.ds(PLANE, PLANE), :] = jnp.concatenate(
        [made[1], made[2] + group_bias(1)], axis=1
    ).astype(BF16)

    def both_ways(up, down, act):
        @pl.when(at.has_up)
        def _():
            act(up)

        @pl.when(at.has_down)
        def _():
            act(down)

    def go(copy):
        copy.start()

    middle = b.kv.at[pl.ds(PLANE, PLANE)]
    up_kv = remote(middle, b.kv.at[pl.ds(0, PLANE)], s.halo_f, (0, 0), at.up)
    down_kv = remote(middle, b.kv.at[pl.ds(2 * PLANE, PLANE)], s.halo_f, (1, 0), at.down)
    up_ids = remote(b.ids.at[1], b.ids.at[0], s.halo_f, (0, 1), at.up)
    down_ids = remote(b.ids.at[1], b.ids.at[2], s.halo_f, (1, 1), at.down)

    def from_peer(piece, kind, d):
        remote(piece, piece, s.a2a, (kind, d - 1), at.in_plane(at.peer(d))).wait_recv()

    both_ways(up_kv, down_kv, go)
    b.qp[...] = jnp.concatenate(
        [made[0] + group_bias(0), jnp.zeros((PLANE, HEAD_DIM), F32)], axis=1
    ).astype(BF16)
    for d in (1, 2, 3):
        from_peer(b.ids.at[1, at.peer(d)], 0, d)
    both_ways(up_ids, down_ids, go)

    q_ids = jnp.concatenate([b.ids[1, j][0:1, :] for j in range(GROUP)], axis=1)
    peaks = b.peaks

    def key_ids(i):
        for j in range(GROUP):
            b.k_ids[(i * GROUP + j) * BLOCK : (i * GROUP + j + 1) * BLOCK, :] = column_of(
                b.ids[i, j][0:1, :]
            )

    def attend(i):
        key_ids(i)
        span = pl.ds(i * PLANE, PLANE)
        same = b.k_ids[span, 0:1] == q_ids
        for h in range(GROUP_HEADS):
            q = b.qp[...] * SCALE
            q = jnp.where(lane_head((PLANE, 256), 0) == h, q, jnp.zeros_like(q))
            score = lax.dot_general(b.kv[span, 0:256], q, NT, preferred_element_type=F32)
            score = jnp.where(same, score, NEGATIVE)
            peak = jnp.max(score, axis=0, keepdims=True)
            if i != 1:
                old = peaks[h][0:1, :]
                peak = jnp.maximum(peak, old)
                factor = jnp.exp(old - peak)
            weight = jnp.exp(score - peak)
            summed = jnp.sum(weight, axis=0, keepdims=True)
            first_lane, line = ((128, HEAD_DIM), (256, 0), (256, HEAD_DIM))[h]
            out = lax.dot_general(
                b.kv[span, first_lane : first_lane + 128],
                weight.astype(BF16),
                TN,
                preferred_element_type=F32,
            )[line : line + HEAD_DIM, :]
            if i != 1:
                out = out + b.out_t[h] * factor
                summed = summed + peaks[GROUP_HEADS + h][0:1, :] * factor
            b.out_t[h] = out
            peaks[h] = jnp.broadcast_to(peak, (8, PLANE))
            peaks[GROUP_HEADS + h] = jnp.broadcast_to(summed, (8, PLANE))

    relay_own(2)
    attend(1)
    relay_own(1)

    @pl.when(at.has_down)
    def _():
        came = b.kv.at[pl.ds(0, PLANE)]
        remote(came, came, s.halo_f, (0, 0), at.down).wait_recv()
        remote(b.ids.at[0], b.ids.at[0], s.halo_f, (0, 1), at.down).wait_recv()

    attend(0)

    @pl.when(at.has_up)
    def _():
        came = b.kv.at[pl.ds(2 * PLANE, PLANE)]
        remote(came, came, s.halo_f, (1, 0), at.up).wait_recv()
        remote(b.ids.at[2], b.ids.at[2], s.halo_f, (1, 1), at.up).wait_recv()

    attend(2)
    outs = [jnp.zeros((HEAD_DIM, PLANE), F32)]
    for h in range(GROUP_HEADS):
        summed = peaks[GROUP_HEADS + h][0:1, :]
        out = b.out_t[h] / summed
        b.out_t[h] = out
        b.stats[h] = peaks[h] + jnp.log(peaks[GROUP_HEADS + h])
        outs.append(out)
    attended = jnp.concatenate(outs, axis=0).T.astype(BF16)
    for i in range(GROUP):
        b.asend[i] = attended[i * BLOCK : (i + 1) * BLOCK, :]

    for d in (1, 2, 3):
        i = at.peer(d)
        start(remote(b.asend.at[i], b.arecv.at[at.r], s.a2a, (1, d - 1), at.in_plane(i)))
    b.arecv[at.r] = b.asend[at.r]
    relay_own(3)
    relay_rest(1)
    relay_rest(2)
    for d in (1, 2, 3):
        from_peer(b.arecv.at[at.peer(d)], 1, d)
    b.att2[near_tokens, :] = jnp.concatenate(
        [b.arecv[g].astype(F32)[:, HEAD_DIM : HEAD_DIM + LANES] for g in range(GROUP)], axis=1
    ).astype(BF16)
    att_copy = remote(b.att2.at[near_tokens], b.att2.at[far_tokens], s.ex, 3, at.across)
    start(att_copy)
    start(dout_copy)
    for w in (1, 2):
        own_copies[w].wait()
        sister_arrivals(w)

    def normalise(hidden):
        center = hidden - jnp.mean(hidden, -1, keepdims=True)
        inverse = lax.rsqrt(jnp.mean(center * center, -1, keepdims=True) + EPSILON)
        return center * inverse, inverse

    def norm_back(upstream, unit, inverse, gain):
        scaled = upstream * gain
        return inverse * (
            scaled
            - jnp.mean(scaled, -1, keepdims=True)
            - unit * jnp.mean(scaled * unit, -1, keepdims=True)
        )

    def column_sum(value):
        return jnp.sum(value, axis=0, keepdims=True)

    def dense_forward(side):
        lines = (near_tokens, far_tokens)[side]
        first = (
            b.tok2[lines, :].astype(F32)
            + jnp.dot(b.att2[lines, :], b.wo[...], preferred_element_type=F32)
            + bias[2:3]
        )
        unit, inverse = normalise(first)
        b.unit_one[lines, :] = unit
        normed = unit * bias[3:4] + bias[4:5]
        b.norm_low[lines, :] = normed.astype(BF16)
        b.second[lines, :] = normed + bias[9:10]
        for c in range(4):
            if side == 1 and c == 2:
                relay_diagonal(3)
            cols = slice(c * MODEL, (c + 1) * MODEL)
            part = halves[c // 2]
            i = 5 + 2 * (c % 2)
            line = jnp.concatenate([part[i : i + 1], part[i + 1 : i + 2]], axis=1)
            inner = line + jnp.dot(
                b.norm_low[lines, :], b.wi[:, cols], preferred_element_type=F32
            )
            gate = 0.5 * (1.0 + lax.erf(inner * ROOT_HALF))
            b.act[lines, cols] = (inner * gate).astype(BF16)
            b.slope[pl.ds(c * BOTH + side * BLOCK, BLOCK), :] = (
                gate + inner * jnp.exp(-0.5 * inner * inner) * INV_ROOT_TAU
            )
        return inverse

    near_inverse = dense_forward(0)
    relay_rest(3)
    tok_copy.wait_recv()
    att_copy.wait_recv()
    inverse_one = jnp.concatenate([near_inverse, dense_forward(1)], axis=0)
    own_copies[3].wait()
    sister_arrivals(3)
    b.second[...] += jnp.dot(b.act[...], b.wb[...], preferred_element_type=F32)
    unit_two, inverse_two = normalise(b.second[...])
    b.result[...] = (unit_two[:BLOCK] * bias[10:11] + bias[11:12]).astype(BF16)
    dout_copy.wait_recv()
    upstream = jnp.concatenate([b.d_out[0], b.dout_far[...]], axis=0).astype(F32)
    b.small[...] = jnp.zeros_like(b.small)
    b.small[10:11, :] = column_sum(upstream * unit_two)
    b.small[11:12, :] = column_sum(upstream)
    d_second = norm_back(upstream, unit_two, inverse_two, bias[10:11])
    b.small[9:10, :] = column_sum(d_second)
    b.d_second[...] = d_second.astype(BF16)
    b.second[...] = d_second

    chunks = [chunk_of(rows, planes) for rows in SET_ROWS]
    owners = [rows // chunk for rows, chunk in zip(SET_ROWS, chunks)]

    def of(name, group):
        return getattr(b, f"{name}{group}")

    def tile(group, t):
        if group == 0:
            lanes = pl.multiple_of(at.x * (TILES * HALF) + t * HALF, 128)
            left, right = b.act[:, pl.ds(lanes, HALF)], b.d_second[...]
        else:
            left = b.norm_low[:, pl.ds(near_rows, HALF)]
            right = b.d_inner[:, pl.ds(pl.multiple_of(t * MODEL, 128), MODEL)]
        return lax.dot_general(left, right, TN, preferred_element_type=F32)

    def out_quarter(t):
        return b.out_tile[pl.ds(pl.multiple_of(t * QUARTER, 16), QUARTER), :]

    def chunk_rows(group, j, size=None):
        return pl.ds(pl.multiple_of(j * chunks[group], 16), size or chunks[group])

    def trimmed(group, j, act):
        size, last = chunks[group], owners[group] - 1
        used = HALF + QUARTER - last * size
        if group != 1 or not 0 < used < size:
            act(size)
            return

        @pl.when(j == last)
        def _():
            act(used)

        @pl.when(j != last)
        def _():
            act(size)

    def own_chunk(group, j):
        if group == 2:
            return b.q_sum.at[chunk_rows(2, j)]
        first_row = OWN_ROWS[group] + j * chunks[group]
        return b.slope.at[pl.ds(pl.multiple_of(first_row, 16), chunks[group])]

    def core_copy(group, i):
        return remote(
            of("core_send", group).at[i],
            of("core_recv", group).at[i],
            s.core,
            group * 2 + i,
            at.sister,
        )

    def y_copy(group, j, size):
        lines = chunk_rows(group, j, size)
        return remote(
            of("y_send", group).at[lines],
            of("y_recv", group).at[lines],
            s.ys,
            (group, j),
            at.beside,
        )

    def up_copy(group, j, size):
        lines = chunk_rows(group, j, size)
        return remote(
            of("z_send", group).at[lines],
            of("up_recv", group).at[lines],
            s.up,
            (group, j),
            at.up,
        )

    def down_copy(group, j, size):
        lines = chunk_rows(group, j, size)
        return remote(
            of("z_send", group).at[lines],
            of("down_recv", group).at[lines],
            s.down,
            (group, j),
            at.down,
        )

    middle_step = planes // 2 + 1
    early, late = (1, middle_step), (middle_step, planes + 1)
    whole_way = (1, planes + 1)

    def each_owner(group, act, span):
        def one(d, carry):
            j = jnp.where(at.p < planes // 2, planes - d, d - 1)

            @pl.when(j < owners[group])
            def _():
                act(j)

            return carry

        lax.fori_loop(*span, one, 0)

    def make(group):
        base = OWN_ROWS[group]
        for i, t in enumerate((at.peer(3), at.peer(1))):
            of("core_send", group)[i, 0:HALF, :] = tile(group, t).astype(BF16)
            if group == 1:
                of("core_send", group)[i, HALF : HALF + QUARTER, :] = out_quarter(t).astype(BF16)
            start(core_copy(group, i))
        b.slope[base : base + HALF, :] = tile(group, at.r)
        if group == 1:
            b.slope[base + HALF : base + HALF + QUARTER, :] = out_quarter(at.r)

    def go_over_y(group, span):
        def act(j):
            trimmed(group, j, lambda size: y_copy(group, j, size).start())

        each_owner(group, act, span)

    def exchange(group):
        base = OWN_ROWS[group]
        passing = tile(group, at.peer(2))
        core_copy(group, 0).wait_recv()
        come = of("core_recv", group)
        of("y_send", group)[0:HALF, :] = (passing + come[0, 0:HALF, :].astype(F32)).astype(BF16)
        if group == 1:
            lines = slice(HALF, HALF + QUARTER)
            b.y_send1[HALF + QUARTER :, :] = jnp.zeros((BLOCK - QUARTER, MODEL), BF16)
            of("y_send", group)[lines, :] = (
                out_quarter(at.peer(2)) + come[0, lines, :].astype(F32)
            ).astype(BF16)
        go_over_y(group, (1, 2) if group == 0 else early)
        core_copy(group, 1).wait_recv()
        used = SET_ROWS[0] if group == 0 else HALF + QUARTER
        b.slope[base : base + used, :] += come[1, 0:used, :].astype(F32)

    def scatter(group, span):
        def act(j):
            mine = own_chunk(group, j)
            if group == 2:
                x_copy(j).wait_recv()
                came = b.x_recv[chunk_rows(2, j), :]
            else:
                trimmed(group, j, lambda size: y_copy(group, j, size).wait_recv())
                came = of("y_recv", group)[chunk_rows(group, j), :]
            total = mine[...] + came.astype(F32)
            mine[...] = total

            @pl.when(jnp.logical_and(at.p == 0, j > 0))
            def _():
                of("z_send", group)[chunk_rows(group, j), :] = total.astype(BF16)
                trimmed(group, j, lambda size: up_copy(group, j, size).start())

            @pl.when(jnp.logical_and(at.p == planes - 1, j < planes - 1))
            def _():
                of("z_send", group)[chunk_rows(group, j), :] = total.astype(BF16)
                trimmed(group, j, lambda size: down_copy(group, j, size).start())

        each_owner(group, act, span)

    def add_arrived(group, j, name, sems, device):
        def wait(size):
            came = of(name, group).at[chunk_rows(group, j, size)]
            remote(came, came, sems, (group, j), device).wait_recv()

        trimmed(group, j, wait)
        return of(name, group)[chunk_rows(group, j), :].astype(F32)

    def relay_sums(group, h):
        @pl.when(at.p == h)
        def _():
            def one(i, carry):
                j = owners[group] - 1 - i
                total = own_chunk(group, j)[...] + add_arrived(
                    group, j, "up_recv", s.up, at.down
                )
                of("z_send", group)[chunk_rows(group, j), :] = total.astype(BF16)
                trimmed(group, j, lambda size: up_copy(group, j, size).start())
                return carry

            lax.fori_loop(0, owners[group] - 1 - at.p, one, 0)

        @pl.when(at.p == planes - 1 - h)
        def _():
            def one(j, carry):
                total = own_chunk(group, j)[...] + add_arrived(
                    group, j, "down_recv", s.down, at.up
                )
                of("z_send", group)[chunk_rows(group, j), :] = total.astype(BF16)
                trimmed(group, j, lambda size: down_copy(group, j, size).start())
                return carry

            lax.fori_loop(0, jnp.minimum(at.p, owners[group]), one, 0)

    def x_copy(j):
        lines = chunk_rows(2, j)
        return remote(b.x_send.at[lines], b.x_recv.at[lines], s.xs, j, at.across)

    def more_sums(group):
        def one(h, carry):
            relay_sums(group, h)
            return carry

        lax.fori_loop(3, planes - 1, one, 0)

    def place(group, t, j, size=None):
        first_row = t * SET_ROWS[group] + j * chunks[group]
        lines = pl.ds(pl.multiple_of(first_row, 16), size or chunks[group])
        return of("sums", group).at[lines]

    def gather_copy(group, t, j, sems, device, source=None, size=None):
        piece = place(group, t, j, size)
        if source is None:
            source = piece
        elif size is not None:
            source = source.at[pl.ds(0, size)]
        return remote(source, piece, sems, (group, j), device)

    def linked(group, t, j, sems, device, source=None):
        def copy(size):
            return gather_copy(group, t, j, sems, device, source, size)

        return types.SimpleNamespace(
            start=lambda: trimmed(group, j, lambda size: copy(size).start()),
            wait_recv=lambda: trimmed(group, j, lambda size: copy(size).wait_recv()),
            wait_send=lambda: trimmed(group, j, lambda size: copy(size).wait_send()),
        )

    def spread(group, j, source=None):
        @pl.when(jnp.logical_and(j <= at.p, at.has_up))
        def _():
            linked(group, at.r, j, s.gu, at.up, source).start()

        @pl.when(jnp.logical_and(j >= at.p, at.has_down))
        def _():
            linked(group, at.r, j, s.gd, at.down, source).start()

        linked(group, at.r, j, s.gy, at.beside, source).start()
        gather_copy(group, at.r, j, s.gc, at.sister, source).start()

    def settle_copy(group):
        return pltpu.make_async_copy(
            of("final", group), place(group, at.r, at.p), s.local[1].at[group]
        )

    def settle(group):
        @pl.when(at.p < owners[group])
        def _():
            mine = own_chunk(group, at.p)

            @pl.when(at.has_down)
            def _():
                mine[...] += add_arrived(group, at.p, "up_recv", s.up, at.down)

            @pl.when(at.has_up)
            def _():
                mine[...] += add_arrived(group, at.p, "down_recv", s.down, at.up)

            total = mine[...]
            of("final", group)[...] = total.astype(BF16)
            spread(group, at.p, of("final", group))
            settle_copy(group).start()

    def around(group, d, act):
        @pl.when(jnp.logical_and(at.p - d >= 0, at.p - d < owners[group]))
        def _():
            act(at.p - d, s.gu, at.down)

        @pl.when(jnp.logical_and(d > 0, at.p + d < owners[group]))
        def _():
            act(at.p + d, s.gd, at.up)

    def come_in(group, d):
        def act(j, sems, device):
            linked(group, at.r, j, sems, device).wait_recv()
            spread(group, j)

        around(group, d, act)

    def hand_over(group, d):
        def act(j, sems, device):
            linked(group, at.peer(2), j, s.gy, at.beside).wait_recv()
            gather_copy(group, at.peer(2), j, s.gf, at.sister).start()

        around(group, d, act)

    def more_gathers():
        def one(d, carry):
            for group in range(3):
                come_in(group, d)
                hand_over(group, d)
            return carry

        lax.fori_loop(4, planes, one, 0)

    make(0)
    for c in range(4):
        if c == 2:
            exchange(0)
        cols = slice(c * MODEL, (c + 1) * MODEL)
        d_inner = (
            lax.dot_general(b.d_second[...], b.wb[cols, :], NT, preferred_element_type=F32)
            * b.slope[c * BOTH : (c + 1) * BOTH, :]
        )
        b.small[5 + c : 6 + c, :] = column_sum(d_inner)
        low = d_inner.astype(BF16)
        b.d_inner[:, cols] = low
        b.second[...] += lax.dot_general(low, b.wi[:, cols], NT, preferred_element_type=F32)
    d_normed = b.second[...]
    unit_one = b.unit_one[...]
    b.small[3:4, :] = column_sum(d_normed * unit_one)
    b.small[4:5, :] = column_sum(d_normed)
    d_first = norm_back(d_normed, unit_one, inverse_one, bias[3:4])
    b.small[2:3, :] = column_sum(d_first)
    d_first_low = d_first.astype(BF16)
    b.d_first[...] = d_first_low
    b.d_tokens[...] = d_first[:BLOCK]
    d_attn = lax.dot_general(d_first_low[:BLOCK], b.wo[...], NT, preferred_element_type=F32)
    for g in range(GROUP):
        b.dsend[g] = jnp.concatenate(
            [jnp.zeros((BLOCK, HEAD_DIM), F32), d_attn[:, g * LANES : (g + 1) * LANES]], axis=1
        ).astype(BF16)
    for d in (1, 2, 3):
        g = at.peer(d)
        start(
            remote(
                b.dsend.at[g], b.do.at[block_rows(0, at.r)], s.a2a, (2, d - 1), at.in_plane(g)
            )
        )
    go_over_y(0, (2, planes + 1))
    b.do[block_rows(0, at.r), :] = b.dsend[at.r]

    b.out_tile[...] = lax.dot_general(
        b.att2[:, pl.ds(near_rows, HALF)], b.d_first[...], TN, preferred_element_type=F32
    )
    make(1)
    scatter(0, (1, 2))

    b.grads[...] = jnp.zeros_like(b.grads)
    b.dq[...] = jnp.zeros_like(b.dq)
    for d in (1, 2, 3):
        from_peer(b.do.at[block_rows(0, at.peer(d))], 2, d)
    do_t = b.do[...].astype(F32).T
    for h in range(GROUP_HEADS):
        lines = slice(HEAD_DIM * (h + 1), HEAD_DIM * (h + 2))
        b.stats[GROUP_HEADS + h] = jnp.broadcast_to(
            column_sum(do_t[lines, :] * b.out_t[h]), (8, PLANE)
        )

    def visit(h, i):
        span = pl.ds(i * PLANE, PLANE)
        pick_q = lane_head((PLANE, 256), 0) == h
        q = b.qp[...]
        q = jnp.where(pick_q, q, jnp.zeros_like(q))
        dout = b.do[...]
        dout = jnp.where(lane_head((PLANE, 256), 1) == h, dout, jnp.zeros_like(dout))
        keys = b.kv[span, 0:256]
        score = lax.dot_general(keys, q * SCALE, NT, preferred_element_type=F32)
        same = b.k_ids[span, 0:1] == q_ids
        prob = jnp.where(same, jnp.exp(score - b.stats[h][0:1, :]), 0.0)
        d_prob = lax.dot_general(b.kv[span, 128:384], dout, NT, preferred_element_type=F32)
        d_score = (prob * (d_prob - b.stats[GROUP_HEADS + h][0:1, :]) * SCALE).astype(BF16)
        b.grads[span, 0:256] += jnp.dot(d_score, q, preferred_element_type=F32)
        b.grads[span, 128:384] += jnp.dot(
            prob.astype(BF16), dout, preferred_element_type=F32
        )
        b.dq[...] += jnp.where(
            pick_q, lax.dot_general(d_score, keys, TN, preferred_element_type=F32), 0.0
        )

    def visit_plane(i):
        def one(h, carry):
            visit(h, i)
            return carry

        lax.fori_loop(0, GROUP_HEADS, one, 0)

    down_grads = remote(b.halo_send.at[0], b.halo.at[1], s.halo_b, 0, at.down)
    up_grads = remote(b.halo_send.at[1], b.halo.at[0], s.halo_b, 1, at.up)
    visit_plane(0)
    b.halo_send[0] = b.grads[pl.ds(0, PLANE), :].astype(BF16)

    @pl.when(at.has_down)
    def _():
        down_grads.start()

    scatter(0, (2, 3))
    exchange(1)
    visit_plane(2)
    b.halo_send[1] = b.grads[pl.ds(2 * PLANE, PLANE), :].astype(BF16)

    @pl.when(at.has_up)
    def _():
        up_grads.start()

    go_over_y(1, late)
    scatter(0, (3, planes + 1))
    relay_sums(0, 1)
    visit_plane(1)
    b.d_group[:, 0:256] = b.dq[...].astype(BF16)

    @pl.when(at.has_up)
    def _():
        remote(b.halo.at[1], b.halo.at[1], s.halo_b, 0, at.up).wait_recv()
        b.grads[pl.ds(PLANE, PLANE), :] += b.halo[1].astype(F32)

    relay_sums(0, 2)
    scatter(1, early)

    @pl.when(at.has_down)
    def _():
        remote(b.halo.at[0], b.halo.at[0], s.halo_b, 1, at.down).wait_recv()
        b.grads[pl.ds(PLANE, PLANE), :] += b.halo[0].astype(F32)

    b.d_group[:, 256:640] = b.grads[pl.ds(PLANE, PLANE), :].astype(BF16)

    b.line_send[...] = jnp.broadcast_to(column_sum(b.d_group[...].astype(F32)), (8, 640))
    line_copy = remote(b.line_send, b.line_recv, s.ex, 4, at.across)
    start(line_copy)
    b.x_send[...] = lax.dot_general(
        b.tok_plane[:, pl.ds(far_rows, HALF)], b.d_group[...], TN, preferred_element_type=F32
    ).astype(BF16)
    each_owner(2, lambda j: x_copy(j).start(), whole_way)
    b.q_sum[...] = lax.dot_general(
        b.tok_plane[:, pl.ds(near_rows, HALF)], b.d_group[...], TN, preferred_element_type=F32
    )

    partners = [at.sister, at.beside]
    span = 1
    while span < planes:
        partners.append((at.c + GROUP * span * (1 - 2 * ((at.p // span) % 2)), at.x))
        span *= 2

    def small_copy(i):
        return remote(b.small, b.small_recv.at[i], s.sm, i, partners[i])

    def small_finish(i):
        small_copy(i).wait()
        b.small[...] += b.small_recv[i]

    def sums_sent(group):
        def one(j, carry):
            if group == 2:
                x_copy(j).wait_send()
            else:
                trimmed(group, j, lambda size: y_copy(group, j, size).wait_send())

            @pl.when(at.p < j)
            def _():
                trimmed(group, j, lambda size: up_copy(group, j, size).wait_send())

            @pl.when(at.p > j)
            def _():
                trimmed(group, j, lambda size: down_copy(group, j, size).wait_send())

            return carry

        lax.fori_loop(0, owners[group], one, 0)

        @pl.when(at.p < owners[group])
        def _():
            settle_copy(group).wait()

    def gathers_done(group):
        def one(j, carry):
            gather_copy(group, at.peer(1), j, s.gc, at.sister).wait_recv()
            gather_copy(group, at.peer(3), j, s.gf, at.sister).wait_recv()
            linked(group, at.r, j, s.gy, at.beside).wait_send()
            gather_copy(group, at.r, j, s.gc, at.sister).wait_send()
            gather_copy(group, at.peer(2), j, s.gf, at.sister).wait_send()

            @pl.when(jnp.logical_and(j <= at.p, at.has_up))
            def _():
                linked(group, at.r, j, s.gu, at.up).wait_send()

            @pl.when(jnp.logical_and(j >= at.p, at.has_down))
            def _():
                linked(group, at.r, j, s.gd, at.down).wait_send()

            return carry

        lax.fori_loop(0, owners[group], one, 0)

    def finish(copy):
        copy.wait_send()

    more_sums(0)
    settle(0)
    relay_sums(1, 1)
    line_copy.wait_recv()
    line = b.line_send[...] + b.line_recv[...]
    mine = lax.broadcasted_iota(jnp.int32, (8, 640), 0) == at.r
    b.small[16:24, 0:640] = jnp.where(mine, line, 0.0)
    small_copy(0).start()
    scatter(2, early)
    small_finish(0)
    small_copy(1).start()

    spare = 2 * BOTH
    gap = jnp.zeros((PLANE, HEAD_DIM), F32)
    for j, first_lane in enumerate((0, 256, 448)):
        piece = b.d_group[...].astype(F32)[:, first_lane : first_lane + LANES]
        wide = jnp.where(
            at.k == 0,
            jnp.concatenate([piece, gap], axis=1),
            jnp.concatenate([gap, piece], axis=1),
        ).astype(BF16)
        part = lax.dot_general(wide, b.wq[:, window[j]], NT, preferred_element_type=F32)
        if j == 0:
            b.slope[spare : spare + PLANE, :] = part
        else:
            b.slope[spare : spare + PLANE, :] += part

    def dt_block(i):
        return b.slope[block_rows(spare, i), :]

    def dt_copy(i):
        device = at.beside if i == 2 else at.sister
        return remote(b.dt_send.at[i], b.dt_recv.at[i], s.dt, i, device)

    for i, block in enumerate((at.peer(3), at.peer(1))):
        b.dt_send[i] = dt_block(block).astype(BF16)
        start(dt_copy(i))

    scatter(1, late)
    come_in(0, 1)
    relay_sums(1, 2)
    relay_sums(2, 1)
    hand_over(0, 0)
    scatter(2, late)
    relay_sums(2, 2)
    dt_copy(0).wait_recv()
    b.dt_send[2] = (dt_block(at.peer(2)) + b.dt_recv[0].astype(F32)).astype(BF16)
    start(dt_copy(2))
    more_sums(1)
    settle(1)
    come_in(0, 2)
    more_sums(2)
    settle(2)
    small_finish(1)
    small_copy(2).start()
    hand_over(0, 1)
    come_in(1, 1)
    come_in(0, 3)
    come_in(2, 1)
    for copy in sent:
        copy.wait_send()
    both_ways(up_kv, down_kv, finish)
    both_ways(up_ids, down_ids, finish)
    both_ways(up_grads, down_grads, finish)
    for group in range(3):
        sums_sent(group)
    hand_over(0, 2)
    dt_copy(1).wait_recv()
    dt_copy(2).wait_recv()
    b.d_tokens[...] += (
        dt_block(at.r) + b.dt_recv[1].astype(F32) + b.dt_recv[2].astype(F32)
    )
    come_in(1, 2)
    come_in(2, 2)
    small_finish(2)
    small_copy(3).start()
    hand_over(0, 3)
    hand_over(1, 0)
    come_in(1, 3)
    come_in(2, 3)
    hand_over(2, 0)
    hand_over(1, 1)
    if planes <= GROUP:
        gathers_done(0)
    hand_over(2, 1)
    hand_over(1, 2)
    small_finish(3)
    hand_over(2, 2)
    hand_over(1, 3)
    if planes <= GROUP:
        gathers_done(1)
    hand_over(2, 3)
    more_gathers()
    for i in range(4, len(partners)):
        small_copy(i).start()
        small_finish(i)

    if planes > GROUP:
        gathers_done(0)
        gathers_done(1)
    gathers_done(2)


def layer_call(planes, args):
    buffers, semaphores = scratch_plan(planes)
    hbm = pl.BlockSpec(memory_space=pltpu.HBM)
    vmem = pl.BlockSpec(memory_space=pltpu.VMEM)
    weights = ("w_qkv", "w_out", "w_in", "w_back")
    scratch = [pltpu.VMEM(shape, kind) for shape, kind in buffers.values()]
    for shape in semaphores.values():
        scratch += [pltpu.SemaphoreType.DMA(shape)] * 2
    return pl.pallas_call(
        functools.partial(layer_kernel, planes, list(buffers), list(semaphores)),
        out_shape=[
            jax.ShapeDtypeStruct((BLOCK, MODEL), BF16),
            jax.ShapeDtypeStruct((BLOCK, MODEL), F32),
        ]
        + [
            jax.ShapeDtypeStruct((TILES * rows, width), BF16)
            for rows, width in zip(SET_ROWS, SET_WIDTH)
        ]
        + [jax.ShapeDtypeStruct((24, MODEL), F32)],
        in_specs=[hbm if name in weights else vmem for name in ARGS],
        out_specs=[vmem, vmem, hbm, hbm, hbm, vmem],
        scratch_shapes=scratch,
        compiler_params=pltpu.CompilerParams(
            collective_id=0, has_side_effects=True, vmem_limit_bytes=60 * 2**20
        ),
        name="layer",
    )(*args)


def unpack_kernel(result_in, tokens_in, sums0, sums1, sums2, small, *refs):
    result, d_tokens, w_qkv, bq, bv, w_out, bo, g1, o1, w_in, bi, w_back, bb, g2, o2 = refs[:15]
    in0, in1, in2, out_q, out_o, out_i, out_b, come, go = refs[15:]
    loads = []
    for g, (sums, held) in enumerate(((sums0, in0), (sums1, in1), (sums2, in2))):
        for t in range(TILES):
            lines = pl.ds(t * SET_ROWS[g], SET_ROWS[g])
            loads.append(
                pltpu.make_async_copy(sums.at[lines], held.at[t], come.at[g * TILES + t])
            )
    for load in loads:
        load.start()
    stores = [
        pltpu.make_async_copy(result_in, result, go.at[14]),
        pltpu.make_async_copy(tokens_in, d_tokens, go.at[15]),
    ]
    for store in stores:
        store.start()

    def put(source, target, i):
        store = pltpu.make_async_copy(source, target, go.at[i])
        store.start()
        stores.append(store)

    x = lax.axis_index("wsh")
    half = small[0:16, pl.ds(pl.multiple_of(x * HALF, 128), HALF)]
    for ref, row in zip((bo, g1, o1, bb, g2, o2), (2, 3, 4, 9, 10, 11)):
        ref[...] = half[row, :]
    whole = jnp.where(x == 0, small[5:7, :], small[7:9, :])
    bi[pl.ds(0, MODEL)] = whole[0, :]
    bi[pl.ds(MODEL, MODEL)] = whole[1, :]
    for ref, first in ((bq, 0), (bv, 448)):
        row = jnp.concatenate(
            [small[16 + g : 17 + g, first : first + LANES] for g in range(GROUP)], axis=1
        )
        ref[...] = jnp.where(x == 0, row[:, :HALF], row[:, HALF:])[0, :]

    for t in range(TILES):
        loads[t].wait()
        lines = pl.ds(t * HALF, HALF)
        out_b[lines, :] = in0[t].astype(F32)
        put(out_b.at[lines], w_back.at[lines], t)
    for t in range(TILES):
        loads[TILES + t].wait()
        out_i[t] = in1[t, 0:HALF, :].astype(F32)
        put(out_i.at[t], w_in.at[:, pl.ds(t * MODEL, MODEL)], 4 + t)
        lines = pl.ds(t * QUARTER, QUARTER)
        out_o[lines, :] = in1[t, HALF : HALF + QUARTER, :].astype(F32)
        put(out_o.at[lines], w_out.at[lines], 8 + t)
    for pair in range(2):
        loads[2 * TILES + 2 * pair].wait()
        loads[2 * TILES + 2 * pair + 1].wait()
        for j, first in enumerate((0, 256, 448)):
            out_q[:, j * MODEL + pair * HALF : j * MODEL + (pair + 1) * HALF] = (
                jnp.concatenate(
                    [
                        in2[2 * pair + i].astype(F32)[:, first : first + LANES]
                        for i in range(2)
                    ],
                    axis=1,
                )
            )
    put(out_q, w_qkv, 12)
    for store in stores:
        store.wait()


def unpack_call(*arrays):
    shape = jax.ShapeDtypeStruct
    vmem = pl.BlockSpec(memory_space=pltpu.VMEM)
    hbm = pl.BlockSpec(memory_space=pltpu.HBM)
    vector = (shape((HALF,), F32), vmem)
    outs = [
        (shape((BLOCK, MODEL), BF16), hbm),
        (shape((BLOCK, MODEL), F32), hbm),
        (shape((HALF, 3 * MODEL), F32), hbm),
        vector,
        vector,
        (shape((HALF, MODEL), F32), hbm),
        vector,
        vector,
        vector,
        (shape((HALF, FF), F32), hbm),
        (shape((FF // 2,), F32), vmem),
        (shape((FF // 2, MODEL), F32), hbm),
        vector,
        vector,
        vector,
    ]
    return pl.pallas_call(
        unpack_kernel,
        out_shape=[o[0] for o in outs],
        in_specs=[vmem, vmem, hbm, hbm, hbm, vmem],
        out_specs=[o[1] for o in outs],
        scratch_shapes=[
            pltpu.VMEM((TILES, rows, width), BF16)
            for rows, width in zip(SET_ROWS, SET_WIDTH)
        ]
        + [
            pltpu.VMEM((HALF, 3 * MODEL), F32),
            pltpu.VMEM((HALF, MODEL), F32),
            pltpu.VMEM((TILES, HALF, MODEL), F32),
            pltpu.VMEM((FF // 2, MODEL), F32),
            pltpu.SemaphoreType.DMA((3 * TILES,)),
            pltpu.SemaphoreType.DMA((16,)),
        ],
        compiler_params=pltpu.CompilerParams(vmem_limit_bytes=60 * 2**20),
        name="unpack",
    )(*arrays)


def body(*args):
    planes = lax.axis_size("ctx") // GROUP
    result, d_tokens, *rest = unpack_call(*layer_call(planes, args))
    return (result[None], d_tokens[None], *rest)


def solution(mesh):
    token_spec = P("wsh", "ctx", None)
    matrix, vector = P("wsh", None), P("wsh")
    in_specs = (
        token_spec,
        P("wsh", "ctx"),
        matrix,
        vector,
        vector,
        matrix,
        vector,
        vector,
        vector,
        matrix,
        vector,
        matrix,
        vector,
        vector,
        vector,
        token_spec,
    )
    out_specs = (
        token_spec,
        token_spec,
        matrix,
        vector,
        vector,
        matrix,
        vector,
        vector,
        vector,
        matrix,
        vector,
        matrix,
        vector,
        vector,
        vector,
    )
    return jax.shard_map(body, mesh=mesh, in_specs=in_specs, out_specs=out_specs, check_vma=False)
```
